32 devices in a mesh: dp: 2 (over x), expert: 16 (over z, y, core).
Axes of the slice: x: 2, y: 2, z: 4, core: 2. Of those that a mesh axis runs over, the one named last changes fastest.
Arguments:
- cache_lat: bfloat16 [1536, 64, 512], P(('dp', 'expert')), may hold values from -6 to 6
- cache_rope: bfloat16 [1536, 4096], P(('dp', 'expert')), may hold values from -6 to 6
- page_scale: bfloat16 [1536], P(('dp', 'expert')), may hold values from 0.5 to 2
- move_list: int32 [32, 2, 4], P(('dp', 'expert')), may hold values from 0 to 47
- page_table: int32 [64, 32], P(('dp', 'expert')), may hold values from 0 to 55, as said below
- lengths: int32 [64], P(('dp', 'expert')), may hold values from 193 to 2048, as said below
- q_lat: bfloat16 [64, 2, 32, 512], P(('dp', 'expert')), may hold values from -72 to 72
- q_rope: bfloat16 [64, 2, 32, 64], P(('dp', 'expert')), may hold values from -12 to 12
- new_lat: bfloat16 [64, 2, 512], P(('dp', 'expert')), may hold values from -6 to 6
- new_rope: bfloat16 [64, 2, 64], P(('dp', 'expert')), may hold values from -6 to 6
- w_uv: bfloat16 [32, 512, 128], P('expert'), may hold values from -6 to 6
- w_out: bfloat16 [4096, 3584], P('expert'), may hold values from -0.09375 to 0.09375
- residual: bfloat16 [128, 3584], P(('dp', 'expert')), may hold values from -400 to 400
- norm_gain: float32 [3584], replicated, may hold values from 0.1 to 1.9
- w_router: bfloat16 [3584, 16], replicated, may hold values from -0.09375 to 0.09375
- routes: int32 [128, 8], P(('dp', 'expert')), may hold values from 0 to 15, all different within a row; in each aligned block of 4 rows (0 to 3, 4 to 7, ...) at most 4 rows name the same one
- w_gate: bfloat16 [16, 3584, 2048], P('expert', None, 'dp'), may hold values from -0.09375 to 0.09375
- w_up: bfloat16 [16, 3584, 2048], P('expert', None, 'dp'), may hold values from -0.09375 to 0.09375
- w_down: bfloat16 [16, 2048, 3584], P('expert', 'dp'), may hold values from -0.125 to 0.125
Outputs:
- attn_out: bfloat16 [128, 3584], P(('dp', 'expert'))
- moe_out: bfloat16 [128, 3584], P(('dp', 'expert'))
The draws below stay inside these ranges and needn't reach their ends.
Inputs may be any that keep to these rules, and one draw needn't show every extreme that they name: `lengths`: cached tokens of a rollout besides its 2 new ones; some rollout holds 2048. `page_table`: a rollout names no page index twice. `routes`: among the rows of one device no expert is named more than 4 times; some expert is named exactly 4 times.
All inputs are finite; a program needn't handle non-finite values.
Results may differ from the reference program's by a relative error of at most 0.03.
Values may be sent and summed in bfloat16 or wider, within the bound.
No kernel may reach another device: no remote copies, remote signals or barrier semaphores. Data moves between devices by JAX's collectives and lax.ppermute only.
A program may use at most 128 MiB of HBM per device.

```python
import math
import jax
import jax.numpy as jnp
import numpy as np
from jax import lax

D = 3584
FF = 2048
LAT = 512
ROPE = 64
VDIM = 128
TOP = 8
NEXT = 2
PAGE = 64
R_DEV = 2
MAXP = 32
MOVES = 4
SLOTS = 48
HEADS = 32
EXPERTS = 16
CAP = 4
ROLLOUTS = 64
TOKENS = 128
POOL = 1536
VIEW = 56
N_DP = 2
N_EXPERT = 16


def shared_latent(key):
    latent_base = jnp.clip(jax.random.normal(key, (ROLLOUTS, NEXT, LAT), jnp.float32), -6.0, 6.0)
    return latent_base


def shared_rope(key):
    return jnp.clip(jax.random.normal(jax.random.fold_in(key, 63), (ROLLOUTS, NEXT, ROPE), jnp.float32), -6.0, 6.0)


def table_and_lengths(key):
    keys = jax.random.split(jax.random.fold_in(key, 40), 6)
    moved_total = N_DP * MOVES
    index_ids = jnp.arange(VIEW, dtype=jnp.int32)
    position = jnp.arange(ROLLOUTS, dtype=jnp.int32) % R_DEV
    is_moved = index_ids >= SLOTS
    owned = ((index_ids - SLOTS) % R_DEV)[None, :] == position[:, None]
    priority = jnp.where(is_moved[None, :] & owned, 0, 1).astype(jnp.int32)
    noise = jax.random.randint(keys[0], (ROLLOUTS, VIEW), 0, 4096).astype(jnp.int32)
    score = (priority * 4096 + noise) * VIEW + index_ids[None, :]
    order = jnp.argsort(score, axis=-1, stable=True)[:, :MAXP].astype(jnp.int32)
    extra = (position < moved_total % R_DEV).astype(jnp.int32)
    owned_count = jnp.minimum(moved_total // R_DEV + extra, MAXP)
    floor_len = jnp.maximum(1, (owned_count - 1) * PAGE + 1)
    longest = MAXP * PAGE
    span = longest - floor_len + 1
    first_draw = jax.random.randint(keys[1], (ROLLOUTS,), 0, 1 << 20) % span
    second_draw = jax.random.randint(keys[2], (ROLLOUTS,), 0, 1 << 20) % span
    third_draw = jax.random.randint(keys[3], (ROLLOUTS,), 0, 1 << 20) % span
    short_len = floor_len + jnp.minimum(jnp.minimum(first_draw, second_draw), third_draw)
    tail_flag = jax.random.randint(keys[4], (ROLLOUTS,), 0, 16) == 0
    forced = jax.random.randint(keys[5], (), 0, ROLLOUTS)
    tail_flag = tail_flag | (jnp.arange(ROLLOUTS, dtype=jnp.int32) == forced)
    lengths_out = jnp.where(tail_flag, longest, short_len).astype(jnp.int32)
    return (order, lengths_out)


def draw_page_table(key, part):
    order, lengths_out = table_and_lengths(key)
    return order


def draw_lengths(key, part):
    order, lengths_out = table_and_lengths(key)
    return lengths_out


def draw_new_lat(key, part):
    latent_base = shared_latent(key)
    return latent_base.astype(jnp.bfloat16)


def draw_q_lat(key, part):
    key = jax.random.fold_in(key, 2)
    values = jnp.clip(jax.random.normal(key, (ROLLOUTS, NEXT, HEADS, LAT), jnp.float32), -6.0, 6.0)
    return values.astype(jnp.bfloat16)


def draw_q_rope(key, part):
    key = jax.random.fold_in(key, 6)
    values = jnp.clip(jax.random.normal(key, (ROLLOUTS, NEXT, HEADS, ROPE), jnp.float32), -6.0, 6.0)
    return values.astype(jnp.bfloat16)


def draw_new_rope(key, part):
    rope_base = shared_rope(key)
    values = rope_base
    return values.astype(jnp.bfloat16)


def draw_residual(key, part):
    key = jax.random.fold_in(key, 7)
    keys = jax.random.split(key, 3)
    row_scale = jnp.exp(jax.random.uniform(keys[0], (TOKENS, 1), jnp.float32) * 2.302585)
    column_scale = jnp.exp(jax.random.uniform(keys[1], (1, D), jnp.float32) * 2.302585)
    values = jnp.clip(jax.random.normal(keys[2], (TOKENS, D), jnp.float32), -4.0, 4.0)
    return (values * row_scale * column_scale).astype(jnp.bfloat16)


def plant(values, key, smallest, high):
    dims = values.shape
    index_at = [jax.random.randint(jax.random.fold_in(key, axis), (), 0, dims[axis]) for axis in range(len(dims))]
    values = values.at[tuple(index_at)].set(smallest)
    longest = dims.index(max(dims))
    index_at[longest] = (index_at[longest] + 1) % dims[longest]
    return values.at[tuple(index_at)].set(high)


def steps_of(key, dims, shards, smallest, largest):
    def one(dim, parts):
        steps = jax.random.uniform(jax.random.fold_in(jax.random.fold_in(key, 6), dim), (parts,), jnp.float32, smallest / len(shards), largest / len(shards))
        return jnp.repeat(jnp.exp(steps), dims[dim] // parts).reshape((-1,) + (1,) * (len(dims) - dim - 1))

    factor_of = one(*shards[0])
    for cut in shards[1:]:
        factor_of = factor_of * one(*cut)
    return factor_of


def deal_out(key, own, number, rows, count, top, reach, lean):
    sequence = jax.random.permutation(key, count)
    heavy_load, ordinary = portions_of(count, rows * top, reach, lean, True), portions_of(count, rows * top, reach, lean, False)
    places = jnp.arange(count)

    def named(tallies, offset_by):
        used = int((tallies > 0).sum())
        fixed = max(1, used // 4)
        moved = fixed + (places - fixed + offset_by * (used - fixed)) % max(1, count - fixed)
        return jnp.zeros((count,), jnp.int32).at[sequence[jnp.where(places < fixed, places, moved)]].set(jnp.asarray(tallies, jnp.int32))

    tallies = jnp.where(number % 4 == 0, named(heavy_load, number // 4), named(ordinary, number - number // 4 - 1))
    mixed = jax.random.permutation(jax.random.fold_in(own, 3), count)
    donor, receiver = mixed[0:count // 2 * 2:2], mixed[1:count // 2 * 2:2]
    slack = jnp.minimum(tallies[donor] - 1, reach - tallies[receiver]) // 2
    slack = jnp.where((donor == sequence[0]) | (receiver == sequence[0]) | (tallies[receiver] == 0), 0, jnp.maximum(slack, 0))
    moved = jax.random.randint(jax.random.fold_in(own, 4), (count // 2,), 0, 1 << 20) % (slack + 1)
    tallies = tallies.at[donor].add(-moved).at[receiver].add(moved)
    labels = jnp.searchsorted(jnp.cumsum(tallies), jnp.arange(rows * top), side="right").astype(jnp.int32)
    grid = labels.reshape(top, rows).T
    grid = grid[jax.random.permutation(jax.random.fold_in(own, 1), rows)]
    offset_by = jax.random.randint(jax.random.fold_in(own, 2), (rows, 1), 0, top)
    return jnp.take_along_axis(grid, (jnp.arange(top)[None, :] + offset_by) % top, axis=1)


def portions_of(number_of, total, limit, slope, full):
    portions = [(1 << 20) // math.isqrt(standing ** slope) + 1 for standing in range(1, number_of + 1)]
    largest = limit if full else min(limit, max(-(-total // number_of), total * portions[0] // sum(portions)))
    least = 1 if total - largest >= number_of - 1 else 0
    holding, spare = [largest] + [least] * (number_of - 1), total - largest - least * (number_of - 1)
    while spare > 0:
        free = [i for i in range(1, number_of) if holding[i] < largest] or [i for i in range(1, number_of) if holding[i] < limit]
        mass, left = sum([portions[i] for i in free]), spare
        for i in free:
            addition = min(limit - holding[i], max(1, left * portions[i] // mass), spare)
            holding[i] = holding[i] + addition
            spare = spare - addition
    return np.array(holding)


def centred(own_key, extent, spread, reach, shards=(), held_as=jnp.bfloat16):
    loudness = steps_of(own_key, extent, shards, -0.22, 0.18) if shards else 1.0
    array = jax.random.normal(own_key, extent, jnp.float32) * spread * loudness
    return jnp.minimum(jnp.maximum(array, -reach), reach).astype(held_as)


def setup_inputs(seed: int = 0) -> dict:
    streams_of = jax.random.split(jax.random.key(seed), 20)
    cache_lat = centred(streams_of[0], (POOL, PAGE, LAT), 1.0, 6.0, ((0, 32),))
    cache_rope = centred(streams_of[1], (POOL, PAGE * ROPE), 1.0, 6.0, ((0, 32),))
    page_scale = jnp.clip(jnp.exp(math.log(2.0) - 1.3862944 * jax.random.uniform(streams_of[2], (POOL,), jnp.float32) ** steps_of(streams_of[2], (POOL,), ((0, 32),), -0.2, 0.2)), 0.5, 2.0).astype(jnp.bfloat16)
    move_list = plant(jax.random.randint(streams_of[3], (N_DP * N_EXPERT, N_DP, MOVES), 0, SLOTS), jax.random.fold_in(streams_of[3], 1), 0, SLOTS - 1).astype(jnp.int32)
    page_table = draw_page_table(jax.random.fold_in(streams_of[19], 71), 0)
    lengths = draw_lengths(jax.random.fold_in(streams_of[19], 71), 0)
    q_lat = draw_q_lat(jax.random.fold_in(streams_of[19], 71), 0)
    q_rope = draw_q_rope(jax.random.fold_in(streams_of[19], 71), 0)
    new_lat = draw_new_lat(jax.random.fold_in(streams_of[19], 71), 0)
    new_rope = draw_new_rope(jax.random.fold_in(streams_of[19], 71), 0)
    w_uv = centred(streams_of[10], (HEADS, LAT, VDIM), 1.0, 6.0, ((0, 16),))
    w_out = centred(streams_of[11], (HEADS * VDIM, D), (HEADS * VDIM) ** -0.5, 0.09375, ((0, 16),))
    residual = draw_residual(jax.random.fold_in(streams_of[19], 71), 0)
    norm_gain = jnp.clip(1.0 + 0.18 * jax.random.normal(streams_of[13], (D,), jnp.float32), 0.1, 1.9)
    w_router = centred(streams_of[14], (D, EXPERTS), D ** -0.5, 0.09375)
    routes_keys = jax.random.split(jax.random.fold_in(streams_of[15], 1), TOKENS // (NEXT * R_DEV))
    routes_turns = jax.random.permutation(jax.random.fold_in(streams_of[15], 3), TOKENS // (NEXT * R_DEV))
    routes = jax.vmap(lambda own, number: deal_out(jax.random.fold_in(streams_of[15], 2), own, number, NEXT * R_DEV, EXPERTS, TOP, CAP, 2))(routes_keys, routes_turns).reshape((TOKENS, TOP))
    w_gate = centred(streams_of[16], (EXPERTS, D, FF), D ** -0.5, 0.09375, ((0, 16), (2, 2)))
    w_up = centred(streams_of[17], (EXPERTS, D, FF), D ** -0.5, 0.09375, ((0, 16), (2, 2)))
    w_down = centred(streams_of[18], (EXPERTS, FF, D), FF ** -0.5, 0.125, ((0, 16), (1, 2)))
    return {"cache_lat": cache_lat, "cache_rope": cache_rope, "page_scale": page_scale, "move_list": move_list, "page_table": page_table, "lengths": lengths, "q_lat": q_lat, "q_rope": q_rope, "new_lat": new_lat, "new_rope": new_rope, "w_uv": w_uv, "w_out": w_out, "residual": residual, "norm_gain": norm_gain, "w_router": w_router, "routes": routes, "w_gate": w_gate, "w_up": w_up, "w_down": w_down}


SCORE_SCALE = 0.07216878364870322
ROUTE_SCALE = 2.5
NORM_EPS = 1e-06

def pool_rows(move_list, page_table):
    owner = jnp.arange(ROLLOUTS, dtype=jnp.int32) // R_DEV
    row_group = owner // N_EXPERT
    column = owner % N_EXPERT
    shifted = jnp.maximum(page_table - SLOTS, 0).astype(jnp.int32)
    source = shifted // MOVES * N_EXPERT + column[:, None]
    picked = move_list[source, row_group[:, None], shifted % MOVES]
    remote = source * SLOTS + picked
    local = owner[:, None] * SLOTS + page_table
    return jnp.where(page_table < SLOTS, local, remote).astype(jnp.int32)

def reference(cache_lat, cache_rope, page_scale, move_list, page_table, lengths, q_lat, q_rope, new_lat, new_rope, w_uv, w_out, residual, norm_gain, w_router, routes, w_gate, w_up, w_down):
    page_rows = pool_rows(move_list, page_table)
    cached = MAXP * PAGE
    highest = lax.Precision.HIGHEST

    def attend(item):
        rows_here, length, query_lat, query_rope, fresh_lat, fresh_rope = item
        keys_lat = cache_lat[rows_here].astype(jnp.float32).reshape(cached, LAT)
        keys_rope = cache_rope[rows_here].astype(jnp.float32).reshape(cached, ROPE)
        token_scale = jnp.repeat(page_scale[rows_here].astype(jnp.float32), PAGE)
        qlf = query_lat.astype(jnp.float32)
        qrf = query_rope.astype(jnp.float32)
        old_scores = jnp.einsum('phl,tl->pht', qlf, keys_lat, precision=highest)
        old_scores = old_scores + jnp.einsum('phk,tk->pht', qrf, keys_rope, precision=highest)
        old_scores = old_scores * (token_scale * SCORE_SCALE)
        live = jnp.arange(cached, dtype=jnp.int32) < length
        old_scores = jnp.where(live[None, None, :], old_scores, -jnp.inf)
        fresh_lat_f = fresh_lat.astype(jnp.float32)
        new_scores = jnp.einsum('phl,ul->phu', qlf, fresh_lat_f, precision=highest)
        new_scores = new_scores + jnp.einsum('phk,uk->phu', qrf, fresh_rope.astype(jnp.float32), precision=highest)
        new_scores = new_scores * SCORE_SCALE
        causal = jnp.arange(NEXT)[None, :] <= jnp.arange(NEXT)[:, None]
        new_scores = jnp.where(causal[:, None, :], new_scores, -jnp.inf)
        peak = jnp.maximum(lax.optimization_barrier(jnp.max(old_scores, -1)), lax.optimization_barrier(jnp.max(new_scores, -1)))
        old_exp = jnp.exp(old_scores - peak[..., None])
        new_exp = jnp.exp(new_scores - peak[..., None])
        total = lax.optimization_barrier(jnp.sum(old_exp, -1)) + lax.optimization_barrier(jnp.sum(new_exp, -1))
        old_weights = (old_exp / total[..., None] * token_scale).astype(jnp.bfloat16)
        new_weights = (new_exp / total[..., None]).astype(jnp.bfloat16)
        result = jnp.einsum('pht,tl->phl', old_weights.astype(jnp.float32), keys_lat, precision=highest)
        result = result + jnp.einsum('phu,ul->phl', new_weights.astype(jnp.float32), fresh_lat_f, precision=highest)
        return result.astype(jnp.bfloat16)
    latent_out = lax.map(attend, (page_rows, lengths, q_lat, q_rope, new_lat, new_rope))
    head_values = jnp.einsum('rphl,hlv->rphv', latent_out.astype(jnp.float32), w_uv.astype(jnp.float32), precision=highest).astype(jnp.bfloat16)
    flat_values = head_values.reshape(TOKENS, HEADS * VDIM)
    attn_sum = jnp.dot(flat_values, w_out, preferred_element_type=jnp.float32)
    attn_out = attn_sum.astype(jnp.bfloat16)
    hidden = (residual.astype(jnp.float32) + attn_sum).astype(jnp.bfloat16)
    hidden_f = hidden.astype(jnp.float32)
    normed = (hidden_f * lax.rsqrt(lax.optimization_barrier(jnp.mean(hidden_f * hidden_f, -1, keepdims=True)) + NORM_EPS) * norm_gain).astype(jnp.bfloat16)
    logits = jnp.dot(normed, w_router, preferred_element_type=jnp.float32)
    onehot = routes[:, :, None] == jnp.arange(EXPERTS, dtype=jnp.int32)[None, None, :]
    selected = lax.optimization_barrier(jnp.sum(jnp.where(onehot, logits[:, None, :], jnp.float32(0.0)), -1))
    sig = jax.nn.sigmoid(selected)
    gates = ROUTE_SCALE * sig / lax.optimization_barrier(jnp.sum(sig, -1, keepdims=True))
    weight_table = lax.optimization_barrier(jnp.sum(jnp.where(onehot, gates[:, :, None], jnp.float32(0.0)), 1))

    def one_expert(carry, item):
        gate_w, up_w, down_w, column_weight = item
        gate_part = jnp.dot(normed, gate_w, preferred_element_type=jnp.float32)
        up_part = jnp.dot(normed, up_w, preferred_element_type=jnp.float32)
        expert_hidden = (jax.nn.silu(gate_part) * up_part).astype(jnp.bfloat16)
        expert_rows = jnp.dot(expert_hidden, down_w, preferred_element_type=jnp.float32)
        return (carry + column_weight[:, None] * expert_rows, None)
    start_sum = jnp.zeros((TOKENS, D), jnp.float32)
    moe_sum, _ = lax.scan(one_expert, start_sum, (w_gate, w_up, w_down, weight_table.T))
    return (attn_out, moe_sum.astype(jnp.bfloat16))
```

```python
import functools

import jax
import jax.numpy as jnp
from jax import lax
from jax.experimental import pallas as pl
from jax.experimental.pallas import tpu as pltpu
from jax.sharding import Mesh, PartitionSpec as P

SCORE_SCALE = 0.07216878364870322
ROUTE_SCALE = 2.5
NORM_EPS = 1e-06
LOW = -1e30
LANES = 128
MIB = 1 << 20
BF16 = jnp.bfloat16
F32 = jnp.float32
VMEM = pl.BlockSpec(memory_space=pltpu.VMEM)
SMEM = pl.BlockSpec(memory_space=pltpu.SMEM)
ANY = pl.BlockSpec(memory_space=pl.ANY)
HBM = pl.BlockSpec(memory_space=pltpu.HBM)
DP = ("top", "low")
EXPERT = ("far", "side", "core")
ROWS = DP + EXPERT
FAR = ("low", "far")
LOAD_MIB = 28


def dot_nt(a, b):
    return lax.dot_general(a, b, (((1,), (1,)), ((), ())), preferred_element_type=F32)


def dot_tn(a, b):
    return lax.dot_general(a, b, (((0,), (0,)), ((), ())), preferred_element_type=F32)


def dot_nn(a, b):
    return jnp.dot(a, b, preferred_element_type=F32)


def call(kernel, outs, operands, in_specs=None, out_specs=None, scratch=(), vmem=16, cost=None):
    flops, moved = cost or (0, 0)
    return pl.pallas_call(
        kernel,
        out_shape=outs,
        in_specs=in_specs or [VMEM] * len(operands),
        out_specs=out_specs or [VMEM] * len(outs),
        scratch_shapes=list(scratch),
        compiler_params=pltpu.CompilerParams(vmem_limit_bytes=vmem * MIB),
        cost_estimate=pl.CostEstimate(flops=flops, bytes_accessed=moved, transcendentals=0),
    )(*operands)


def shape(dims, dtype):
    return jax.ShapeDtypeStruct(dims, dtype)


def iota(dims, axis):
    return lax.broadcasted_iota(jnp.int32, dims, axis)


def fetch(copies):
    for copy in copies:
        copy.start()
    return copies


def pick_kernel(partners, moves, move_hbm, scale_ref, lat, rope_hbm, *rest):
    lat_outs, rope_outs = rest[:partners], rest[partners : 2 * partners]
    scale_out, move, rope, wide_scale, lat_sems, sems = rest[2 * partners :]
    slots, width = rope.shape
    half = width // 2
    me = lax.axis_index(DP)
    get_move, get_rope = fetch(
        [
            pltpu.make_async_copy(move_hbm, move, sems.at[0]),
            pltpu.make_async_copy(rope_hbm, rope, sems.at[1]),
        ]
    )
    wide_scale[...] = scale_ref[...].astype(F32)
    (put_scale,) = fetch([pltpu.make_async_copy(wide_scale, scale_out, sems.at[2])])
    get_move.wait()
    copies = []
    for k in range(partners):
        for m in range(moves):
            copies.append(
                pltpu.make_async_copy(
                    lat.at[move[0, me ^ (k + 1), m]], lat_outs[k].at[m], lat_sems.at[k, m]
                )
            )
    fetch(copies)
    put_scale.wait()
    get_rope.wait()
    row = iota((2 * moves, 1), 0)
    column = iota((2 * moves, slots), 1)
    for k in range(partners):
        target = jnp.zeros((2 * moves, 1), jnp.int32)
        factor = jnp.zeros((2 * moves, 1), F32)
        for m in range(moves):
            page = move[0, me ^ (k + 1), m]
            target = jnp.where(row // 2 == m, page, target)
            factor = jnp.where(row // 2 == m, scale_out[page], factor)
        hit = column == target
        even = row % 2 == 0
        first = jnp.where(hit & even, 1.0, 0.0).astype(BF16)
        second = jnp.where(hit & (~even), 1.0, 0.0).astype(BF16)
        both = dot_nn(first, rope[:, :half]) + dot_nn(second, rope[:, half:])
        rope_outs[k][:, :half] = both.astype(BF16)
        rope_outs[k][:, half:] = jnp.broadcast_to(factor, (2 * moves, LANES)).astype(BF16)
    for copy in copies:
        copy.wait()


def spread(scores, start, count, stride, part):
    for b in range(scores.shape[0]):
        scores.at[b][pl.ds(start, count, stride=stride), :] = part[:, b * LANES : (b + 1) * LANES]


def read(scores, span):
    parts = [scores[b, span, :] for b in range(scores.shape[0])]
    return parts[0] if len(parts) == 1 else jnp.concatenate(parts, axis=1)


def write(scores, span, part):
    for b in range(scores.shape[0]):
        scores[b, span, :] = part[:, b * LANES : (b + 1) * LANES]


GROUP = 8


def local_kernel(
    sizes,
    partners,
    scale,
    table_hbm,
    lengths_hbm,
    move_hbm,
    lat_hbm,
    rope_hbm,
    q_hbm,
    turn_hbm,
    new_lat_hbm,
    new_rope_hbm,
    acc_out,
    peak_out,
    total_out,
    qrel_out,
    q2_out,
    limit_out,
    table,
    lengths,
    move,
    lat,
    rope,
    q_lat,
    q_rope,
    new_lat,
    new_rope,
    scores,
    limits,
    new_keys,
    new_turns,
    sems,
    lat_sems,
):
    heads, per_device, rollouts, following, view = sizes
    slots, page_len, latent = lat.shape
    rows = rollouts * following * heads
    rope_dim = q_rope.shape[3]
    moves = move.shape[2]
    me = lax.axis_index(DP)
    pairs = (
        (table_hbm, table),
        (lengths_hbm, lengths),
        (move_hbm, move),
        (rope_hbm, rope),
        (turn_hbm, q_rope),
        (q_hbm, q_lat),
        (new_lat_hbm, new_lat),
        (new_rope_hbm, new_rope),
    )
    small = fetch(
        [pltpu.make_async_copy(src, dst, sems.at[i]) for i, (src, dst) in enumerate(pairs)]
    )
    chunks = fetch(
        [
            pltpu.make_async_copy(
                lat_hbm.at[pl.ds(at, GROUP)], lat.at[pl.ds(at, GROUP)], lat_sems.at[at // GROUP]
            )
            for at in range(0, slots, GROUP)
        ]
    )
    place = iota((rows, rows), 0)
    rollout = (place // following) % rollouts
    token = place % following
    head = place // (following * rollouts)
    source = (rollout * following + token) * heads + head
    order = jnp.where(iota((rows, rows), 1) == source, 1.0, 0.0).astype(BF16)
    at = iota((rope_dim, 2 * rope_dim), 1)
    frm = iota((rope_dim, 2 * rope_dim), 0)
    for copy in small:
        copy.wait()
    for slot in range(rollouts * view):
        limits[slot] = 0
    for r in range(rollouts):
        for a in range(table.shape[1]):
            live = jnp.clip(lengths[r] - a * page_len, 0, page_len)
            limits[r * view + table[r, a]] = live
    q_turn = dot_nn(order, q_rope[...].reshape(rows, rope_dim)).astype(BF16)
    q2_out[:rows, :] = dot_nn(q_turn, jnp.where(at == frm, 1.0, 0.0).astype(BF16)).astype(BF16)
    q2_out[rows:, :] = dot_nn(
        q_turn, jnp.where(at == frm + rope_dim, 1.0, 0.0).astype(BF16)
    ).astype(BF16)
    qrel_out[...] = dot_nn(order, q_lat[...].reshape(rows, latent)).astype(BF16)
    twos = page_len // 2
    wide = 2 * rope_dim
    stacked = jnp.concatenate([rope[:, c * wide : (c + 1) * wide] for c in range(twos)], axis=0)
    turned = dot_nt(stacked, q2_out[...])
    for c in range(twos):
        part = turned[c * slots : (c + 1) * slots]
        spread(scores, 2 * c, slots, page_len, part[:, :rows])
        spread(scores, 2 * c + 1, slots, page_len, part[:, rows:])

    lane_rollout = (iota((1, rows), 1) // following) % rollouts
    lane_token = iota((1, rows), 1) % following
    position = iota((page_len, rows), 0)

    def limit_row(slot):
        row = jnp.full(lane_rollout.shape, limits[slot], jnp.int32)
        for r in range(1, rollouts):
            row = jnp.where(lane_rollout == r, limits[r * view + slot], row)
        return row

    for k in range(partners):
        for m in range(moves):
            limit_out[k * moves + m : k * moves + m + 1, :] = limit_row(
                slots + (me ^ (k + 1)) * moves + m
            )
    queries = qrel_out[...]
    fresh_rows = rollouts * following
    new_keys[...] = jnp.zeros(new_keys.shape, F32)
    new_turns[...] = jnp.zeros(new_turns.shape, F32)
    for r in range(rollouts):
        span = slice(r * following, (r + 1) * following)
        new_keys[span, :] = new_lat[r].astype(F32)
        new_turns[span, :rope_dim] = new_rope[r].astype(F32)
    fresh_keys = new_keys[...].astype(BF16)
    new_part = dot_nt(fresh_keys, queries) + dot_nt(
        new_turns[...].astype(BF16), q2_out[:rows, :]
    )
    new_row = iota(new_part.shape, 0)
    seen = (new_row // following == lane_rollout) & (new_row % following <= lane_token)
    new_part = jnp.where(seen & (new_row < fresh_rows), new_part * SCORE_SCALE, LOW)

    best = jnp.full((page_len, rows), LOW, F32)
    for first in range(0, slots, GROUP):
        chunks[first // GROUP].wait()
        keys = lat[first : first + GROUP].reshape(GROUP * page_len, latent)
        fresh = dot_nt(keys, queries)
        for g in range(GROUP):
            page = first + g
            span = pl.ds(page * page_len, page_len)
            part = fresh[g * page_len : (g + 1) * page_len] + read(scores, span)
            part = part * (scale[page] * SCORE_SCALE)
            write(scores, span, part)
            best = jnp.maximum(best, jnp.where(position < limit_row(page), part, LOW))
    for m in range(moves):
        page = move[0, me, m]
        part = read(scores, pl.ds(pl.multiple_of(page * page_len, page_len), page_len))
        live = position < limit_row(slots + me * moves + m)
        best = jnp.maximum(best, jnp.where(live, part, LOW))
    peak = jnp.max(best, axis=0, keepdims=True)
    peak = jnp.maximum(peak, jnp.max(new_part, axis=0, keepdims=True))

    def weigh(part, slot, factor, total):
        grown = jnp.where(position < limit_row(slot), jnp.exp(part - peak), 0.0)
        return (grown * factor).astype(BF16), total + grown

    new_exp = jnp.exp(new_part - peak)
    total = jnp.zeros((page_len, rows), F32)
    acc = dot_tn(new_exp.astype(BF16), fresh_keys)
    for first in range(0, slots, GROUP):
        weights = []
        for g in range(GROUP):
            page = first + g
            part = read(scores, pl.ds(page * page_len, page_len))
            weight, total = weigh(part, page, scale[page], total)
            weights.append(weight)
        keys = lat[first : first + GROUP].reshape(GROUP * page_len, latent)
        acc = acc + dot_tn(jnp.concatenate(weights, axis=0), keys)
    weights, keys = [], []
    for m in range(moves):
        page = move[0, me, m]
        part = read(scores, pl.ds(pl.multiple_of(page * page_len, page_len), page_len))
        weight, total = weigh(part, slots + me * moves + m, scale[page], total)
        weights.append(weight)
        keys.append(lat[page])
    acc = acc + dot_tn(jnp.concatenate(weights, axis=0), jnp.concatenate(keys, axis=0))
    acc_out[...] = acc
    peak_out[...] = jnp.broadcast_to(peak, peak_out.shape)
    whole = jnp.sum(total, axis=0, keepdims=True) + jnp.sum(new_exp, axis=0, keepdims=True)
    total_out[...] = jnp.broadcast_to(whole, total_out.shape)


def merge_kernel(partners, *refs):
    count = 2 * partners + 6
    sources, out, held = refs[:count], refs[count], refs[count + 1 : 2 * count + 1]
    scores, sems = refs[2 * count + 1 :]
    copies = fetch(
        [
            pltpu.make_async_copy(src, dst, sems.at[i])
            for i, (src, dst) in enumerate(zip(sources, held))
        ]
    )
    for copy in copies:
        copy.wait()
    got_lat, got_rope = held[:partners], held[partners : 2 * partners]
    acc_in, peak_in, total_in, qrel, q2, limit = held[2 * partners :]
    moves, page_len, latent = got_lat[0].shape
    rows = qrel.shape[0]
    wide = q2.shape[1]
    position = iota((page_len, rows), 0)
    queries = qrel[...]
    best = jnp.full((page_len, rows), LOW, F32)
    half_lanes = got_rope[0].shape[1] - LANES
    pieces = half_lanes // wide
    span = moves * page_len
    factors = []
    for k in range(partners):
        turns = got_rope[k]
        stacked = jnp.concatenate(
            [turns[:, c * wide : (c + 1) * wide].astype(F32) for c in range(pieces)], axis=0
        ).astype(BF16)
        turned = dot_nt(stacked, q2[...])
        base = k * span
        for c in range(pieces):
            part = turned[c * 2 * moves : (c + 1) * 2 * moves]
            spread(scores, base + 2 * c, 2 * moves, page_len // 2, part[:, :rows])
            spread(scores, base + 2 * c + 1, 2 * moves, page_len // 2, part[:, rows:])
        fresh = dot_nt(got_lat[k][...].reshape(span, latent), queries)
        marks = turns[:, half_lanes:].astype(F32)
        for m in range(moves):
            factor = marks[2 * m : 2 * m + 1, :1]
            factors.append(factor)
            where_at = pl.ds(base + m * page_len, page_len)
            part = fresh[m * page_len : (m + 1) * page_len] + read(scores, where_at)
            part = part * (factor * SCORE_SCALE)
            at = k * moves + m
            part = jnp.where(position < limit[at : at + 1, :], part, LOW)
            write(scores, where_at, part)
            best = jnp.maximum(best, part)
    peak_local = peak_in[:1, :]
    peak = jnp.maximum(jnp.max(best, axis=0, keepdims=True), peak_local)
    shrink = jnp.exp(peak_local - peak)
    acc = jnp.zeros((rows, latent), F32)
    grown_sum = jnp.zeros((page_len, rows), F32)
    for k in range(partners):
        weights = []
        for m in range(moves):
            part = read(scores, pl.ds(k * span + m * page_len, page_len))
            grown = jnp.exp(part - peak)
            grown_sum = grown_sum + grown
            weights.append((grown * factors[k * moves + m]).astype(BF16))
        acc = acc + dot_tn(
            jnp.concatenate(weights, axis=0), got_lat[k][...].reshape(span, latent)
        )
    total = total_in[:1, :] * shrink + jnp.sum(grown_sum, axis=0, keepdims=True)

    def upright(row):
        return jnp.transpose(jnp.broadcast_to(row, (LANES, rows)))[:, :1]

    result = (acc_in[...] * upright(shrink) + acc) / upright(total)
    out[...] = result.reshape(out.shape).astype(BF16)


def project_kernel(tokens, blocks, w_uv, w_out, away, kept):
    devices = blocks.shape[0]
    per_device = w_uv.shape[0]
    core = lax.axis_index("core")
    stacked = blocks[...].astype(F32).reshape(-1, blocks.shape[2]).astype(BF16)
    rows = stacked.shape[0]
    row_head = (iota((rows, 1), 0) // tokens) % per_device
    values = []
    for head in range(per_device):
        part = dot_nn(stacked, w_uv[head])
        values.append(jnp.where(row_head == head, part, 0.0).astype(BF16))
    values = jnp.concatenate(values, axis=1)
    half = devices // 2 * tokens
    out_row = iota((2 * half, rows), 0)
    in_row = iota((2 * half, rows), 1)
    out_device = (out_row % half) // tokens * 2 + jnp.where(out_row < half, 1 - core, core)
    same = (in_row // (tokens * per_device) == out_device) & (in_row % tokens == out_row % tokens)
    joined = dot_nn(jnp.where(same, 1.0, 0.0).astype(BF16), values).astype(BF16)
    width = w_out.shape[1]
    step = 512 if width % 512 == 0 else width
    for at in range(0, width, step):
        part = dot_nn(joined, w_out[:, at : at + step])
        away[:, at : at + step] = part[:half].astype(BF16)
        kept[:, at : at + step] = part[half:]


def split_kernel(kept, got, out):
    total = kept[...] + got[...].astype(F32)
    out[...] = total.reshape(out.shape).astype(BF16)


def norm_kernel(got, residual, gain, routes, attn_out, out):
    total = jnp.sum(got[...].astype(F32), axis=0)
    attn_out[...] = total.astype(BF16)
    hidden = (residual[...].astype(F32) + total).astype(BF16).astype(F32)
    width = hidden.shape[1]
    power = jnp.sum(hidden * hidden, axis=1, keepdims=True) / width
    normed = (hidden * lax.rsqrt(power + NORM_EPS) * gain[...].reshape(1, width)).astype(BF16)
    named = routes[...].astype(F32).astype(BF16)
    for copy in range(out.shape[0]):
        out[copy, :, :width] = normed
        out[copy, :, width:] = jnp.zeros((hidden.shape[0], LANES), BF16)
        out[copy, :, width : width + routes.shape[1]] = named


def load_kernel(count, passed, *refs):
    sources, passed_out, outs, sems = refs[:count], refs[count], refs[count + 1 : -1], refs[-1]
    split = sems.shape[1]
    copies = []
    for k, (source, out) in enumerate(zip(sources, outs)):
        step = out.shape[0] // split
        for i in range(split):
            span = pl.ds(i * step, step)
            copies.append(
                pltpu.make_async_copy(source.at[0, span], out.at[span], sems.at[k, i])
            )
    fetch(copies)
    passed_out[...] = passed[...]
    for copy in copies:
        copy.wait()


def expert_kernel(top, count, *refs):
    pieces = refs[:count]
    w_router, w_gate, w_up, w_down = refs[count : count + 4]
    kept, away, rows_ref, hidden_ref = refs[count + 4 :]
    expert = lax.axis_index(EXPERT)
    width, units = w_gate.shape
    in_step = 256 if units % 256 == 0 else units
    out_step = 512 if width % 512 == 0 else width
    piece_rows = rows_ref.shape[0] // count
    named = []
    for k, piece in enumerate(pieces):
        whole = piece[...].astype(F32).reshape(piece_rows, -1)
        rows_ref[k * piece_rows : (k + 1) * piece_rows, :] = whole[:, :width].astype(BF16)
        named.append(whole[:, width:])
    named = jnp.concatenate(named, axis=0)
    rows = rows_ref[...]
    logits = dot_nt(rows, w_router[...])
    experts = iota(logits.shape, 1)
    chosen = jnp.zeros(logits.shape, F32)
    for k in range(top):
        route = named[:, k : k + 1].astype(jnp.int32)
        chosen = chosen + jnp.where(route == experts, 1.0, 0.0)
    sig = jax.nn.sigmoid(logits) * chosen
    mine = jnp.sum(jnp.where(experts == expert, sig, 0.0), axis=1, keepdims=True)
    gates = ROUTE_SCALE * mine / jnp.sum(sig, axis=1, keepdims=True)
    for at in range(0, units, in_step):
        gate = dot_nn(rows, w_gate[:, at : at + in_step])
        up = dot_nn(rows, w_up[:, at : at + in_step])
        hidden_ref[:, at : at + in_step] = (gate / (1.0 + jnp.exp(-gate)) * up).astype(BF16)
    hidden = hidden_ref[...]
    half = rows_ref.shape[0] // 2
    for at in range(0, width, out_step):
        part = dot_nn(hidden, w_down[:, at : at + out_step]) * gates
        kept[:, at : at + out_step] = part[:half]
        away[:, at : at + out_step] = part[half:].astype(BF16)


def halve_kernel(kept, got, keep, away):
    total = kept[...] + got[...].astype(F32)
    half = total.shape[0] // 2
    keep[...] = total[:half]
    away[...] = total[half:].astype(BF16)


def sum_kernel(got, out):
    out[...] = jnp.sum(got[...].astype(F32), axis=0).astype(BF16)


def body(dp_count, expert_count, *arrays):
    (
        cache_lat,
        cache_rope,
        page_scale,
        move_list,
        page_table,
        lengths,
        q_lat,
        q_rope,
        new_lat,
        new_rope,
        w_uv,
        w_out,
        residual,
        norm_gain,
        w_router,
        routes,
        w_gate,
        w_up,
        w_down,
    ) = arrays
    total_devices = dp_count * expert_count
    top_bit = total_devices // 2
    side_bit = 2

    def swap(x, mask, mask_odd=None):
        pairs = []
        for i in range(total_devices):
            other = mask if mask_odd is None or i % 2 == 0 else mask_odd
            pairs.append((i, i ^ other))
        return lax.ppermute(x, ROWS, pairs)

    def deal(x, names):
        return lax.all_to_all(x, names, split_axis=0, concat_axis=0, tiled=True)

    slots, page_len, latent = cache_lat.shape
    moves = move_list.shape[2]
    rollouts, following, heads, rope_dim = q_rope.shape
    view = slots + dp_count * moves
    per_device = heads // expert_count
    tokens = rollouts * following
    width = residual.shape[1]
    partners = dp_count - 1
    rows = tokens * heads
    sizes = (heads, per_device, rollouts, following, view)

    picked = call(
        functools.partial(pick_kernel, partners, moves),
        [shape((moves, page_len, latent), BF16)] * partners
        + [shape((2 * moves, cache_rope.shape[1] // 2 + LANES), BF16)] * partners
        + [shape((slots,), F32)],
        (move_list, page_scale, cache_lat, cache_rope),
        in_specs=[HBM, VMEM, HBM, HBM],
        out_specs=[VMEM] * (2 * partners) + [SMEM],
        scratch=[
            pltpu.SMEM(move_list.shape, jnp.int32),
            pltpu.VMEM(cache_rope.shape, BF16),
            pltpu.VMEM((slots,), F32),
            pltpu.SemaphoreType.DMA((partners, moves)),
            pltpu.SemaphoreType.DMA((3,)),
        ],
        vmem=60,
    )
    got_lat = [swap(picked[k], (k + 1) * expert_count) for k in range(partners)]
    got_rope = [swap(picked[partners + k], (k + 1) * expert_count) for k in range(partners)]

    local = call(
        functools.partial(local_kernel, sizes, partners),
        [
            shape((rows, latent), F32),
            shape((8, rows), F32),
            shape((8, rows), F32),
            shape((rows, latent), BF16),
            shape((2 * rows, 2 * rope_dim), BF16),
            shape((-(-partners * moves // 8) * 8, rows), jnp.int32),
        ],
        (
            picked[-1],
            page_table,
            lengths,
            move_list,
            cache_lat,
            cache_rope,
            q_lat,
            q_rope,
            new_lat,
            new_rope,
        ),
        in_specs=[SMEM] + [HBM] * 9,
        scratch=[
            pltpu.SMEM(page_table.shape, jnp.int32),
            pltpu.SMEM(lengths.shape, jnp.int32),
            pltpu.SMEM(move_list.shape, jnp.int32),
            pltpu.VMEM(cache_lat.shape, BF16),
            pltpu.VMEM(cache_rope.shape, BF16),
            pltpu.VMEM(q_lat.shape, BF16),
            pltpu.VMEM(q_rope.shape, BF16),
            pltpu.VMEM(new_lat.shape, BF16),
            pltpu.VMEM(new_rope.shape, BF16),
            pltpu.VMEM((rows // LANES, slots * page_len, LANES), F32),
            pltpu.SMEM((rollouts * view,), jnp.int32),
            pltpu.VMEM((16, latent), F32),
            pltpu.VMEM((16, 2 * rope_dim), F32),
            pltpu.SemaphoreType.DMA((8,)),
            pltpu.SemaphoreType.DMA((slots // GROUP,)),
        ],
        vmem=60,
        cost=(2 * slots * page_len * rows * (2 * latent + 2 * rope_dim), 4 * MIB),
    )
    operands = (*got_lat, *got_rope, *local)
    blocks = call(
        functools.partial(merge_kernel, partners),
        [shape((expert_count, tokens * per_device, latent), BF16)],
        operands,
        in_specs=[HBM] * len(operands),
        scratch=[pltpu.VMEM(x.shape, x.dtype) for x in operands]
        + [
            pltpu.VMEM((rows // LANES, partners * moves * page_len, LANES), F32),
            pltpu.SemaphoreType.DMA((len(operands),)),
        ],
        vmem=60,
        cost=(2 * moves * page_len * rows * 2 * latent, MIB),
    )[0]
    blocks = deal(blocks, EXPERT)

    half_rows = expert_count // 2 * tokens
    away, kept = call(
        functools.partial(project_kernel, tokens),
        [shape((half_rows, width), BF16), shape((half_rows, width), F32)],
        (blocks, w_uv, w_out),
        cost=(4 * half_rows * width * w_out.shape[0], 4 * MIB),
    )
    parts = call(
        split_kernel,
        [shape((expert_count // 2, tokens, width), BF16)],
        (kept, swap(away, 1)),
    )[0]
    parts = deal(parts, ("far", "side"))
    far_count = total_devices // 8
    attn_out, own_rows = call(
        norm_kernel,
        [shape((tokens, width), BF16), shape((far_count, tokens, width + LANES), BF16)],
        (parts, residual, norm_gain, routes),
    )

    def load(passed, sources, vmem):
        return call(
            functools.partial(load_kernel, len(sources)),
            [shape(passed.shape, BF16)] + [shape(w.shape[1:], BF16) for w in sources],
            (passed, *sources),
            in_specs=[VMEM] + [HBM] * len(sources),
            scratch=[pltpu.SemaphoreType.DMA((len(sources), 8))],
            vmem=vmem,
            cost=(0, 2 * sum(w.size for w in sources)),
        )

    piece = deal(own_rows, FAR)
    pieces = [piece, swap(piece, top_bit, side_bit)]
    pieces = pieces + [swap(p, side_bit, top_bit) for p in pieces]
    side_piece, *weights = load(pieces[1], (w_gate, w_up, w_down), LOAD_MIB)
    pieces = [piece, side_piece] + pieces[2:]
    pieces = pieces + [swap(p, 1) for p in pieces]

    all_rows = total_devices * tokens
    hidden_units = w_gate.shape[2]
    half = all_rows // 2
    kept, away = call(
        functools.partial(expert_kernel, routes.shape[1], len(pieces)),
        [shape((half, width), F32), shape((half, width), BF16)],
        (*pieces, w_router.T, *weights),
        scratch=[
            pltpu.VMEM((all_rows, width), BF16),
            pltpu.VMEM((all_rows, hidden_units), BF16),
        ],
        vmem=16 if all_rows <= 256 else 56,
        cost=(6 * all_rows * width * hidden_units, 6 * width * hidden_units),
    )

    got = swap(away, 1)
    kept, away = call(
        halve_kernel,
        [shape((half // 2, width), F32), shape((half // 2, width), BF16)],
        (kept, got),
    )
    got = swap(away, side_bit, top_bit)
    kept, away = call(
        halve_kernel,
        [shape((half // 4, width), F32), shape((half // 4, width), BF16)],
        (kept, got),
    )
    got = swap(away, top_bit, side_bit)
    parts = call(split_kernel, [shape((far_count, tokens, width), BF16)], (kept, got))[0]
    moe_out = call(sum_kernel, [shape((tokens, width), BF16)], (deal(parts, FAR),))[0]
    return (attn_out, moe_out)


def solution(mesh):
    dp_count, expert_count = mesh.shape["dp"], mesh.shape["expert"]
    finer = Mesh(mesh.devices.reshape(2, dp_count // 2, expert_count // 4, 2, 2), ROWS)
    return jax.shard_map(
        functools.partial(body, dp_count, expert_count),
        mesh=finer,
        in_specs=(
            P(ROWS, None, None),
            P(ROWS, None),
            P(ROWS),
            P(ROWS, None, None),
            P(ROWS, None),
            P(ROWS),
            P(ROWS, None, None, None),
            P(ROWS, None, None, None),
            P(ROWS, None, None),
            P(ROWS, None, None),
            P(EXPERT, None, None),
            P(EXPERT, None),
            P(ROWS, None),
            P(),
            P(),
            P(ROWS, None),
            P(EXPERT, None, DP),
            P(EXPERT, None, DP),
            P(EXPERT, DP, None),
        ),
        out_specs=(P(ROWS, None), P(ROWS, None)),
        check_vma=False,
    )
```

```python
import functools

import jax
import jax.numpy as jnp
from jax import lax
from jax.experimental import pallas as pl
from jax.experimental.pallas import tpu as pltpu
from jax.sharding import Mesh, PartitionSpec as P

SCORE_SCALE = 0.07216878364870322
ROUTE_SCALE = 2.5
NORM_EPS = 1e-06
LOW = -1e30
LANES = 128
MIB = 1 << 20
BF16 = jnp.bfloat16
F32 = jnp.float32
VMEM = pl.BlockSpec(memory_space=pltpu.VMEM)
SMEM = pl.BlockSpec(memory_space=pltpu.SMEM)
ANY = pl.BlockSpec(memory_space=pl.ANY)
HBM = pl.BlockSpec(memory_space=pltpu.HBM)
DP = ("top", "low")
EXPERT = ("far", "side", "core")
ROWS = DP + EXPERT
FAR = ("low", "far")
LOAD_MIB = 36
EXPERT_MIB = 36


def dot_nt(a, b):
    return lax.dot_general(a, b, (((1,), (1,)), ((), ())), preferred_element_type=F32)


def dot_tn(a, b):
    return lax.dot_general(a, b, (((0,), (0,)), ((), ())), preferred_element_type=F32)


def dot_nn(a, b):
    return jnp.dot(a, b, preferred_element_type=F32)


def call(kernel, outs, operands, in_specs=None, out_specs=None, scratch=(), vmem=16, cost=None):
    flops, moved = cost or (0, 0)
    return pl.pallas_call(
        kernel,
        out_shape=outs,
        in_specs=in_specs or [VMEM] * len(operands),
        out_specs=out_specs or [VMEM] * len(outs),
        scratch_shapes=list(scratch),
        compiler_params=pltpu.CompilerParams(vmem_limit_bytes=vmem * MIB),
        cost_estimate=pl.CostEstimate(flops=flops, bytes_accessed=moved, transcendentals=0),
    )(*operands)


def shape(dims, dtype):
    return jax.ShapeDtypeStruct(dims, dtype)


def iota(dims, axis):
    return lax.broadcasted_iota(jnp.int32, dims, axis)


def fetch(copies):
    for copy in copies:
        copy.start()
    return copies


def pick_kernel(partners, moves, move_hbm, scale_hbm, lat, rope_hbm, *rest):
    lat_outs, rope_outs = rest[:partners], rest[partners : 2 * partners]
    scale_out, move, rope, scale_ref, wide_scale, lat_sems, sems = rest[2 * partners :]
    slots, width = rope.shape
    half = width // 2
    me = lax.axis_index(DP)
    get_move, get_scale, get_rope = fetch(
        [
            pltpu.make_async_copy(move_hbm, move, sems.at[0]),
            pltpu.make_async_copy(scale_hbm, scale_ref, sems.at[1]),
            pltpu.make_async_copy(rope_hbm, rope, sems.at[2]),
        ]
    )
    get_move.wait()
    copies = []
    for k in range(partners):
        for m in range(moves):
            copies.append(
                pltpu.make_async_copy(
                    lat.at[move[0, me ^ (k + 1), m]], lat_outs[k].at[m], lat_sems.at[k, m]
                )
            )
    fetch(copies)
    get_scale.wait()
    wide_scale[...] = scale_ref[...].astype(F32)
    (put_scale,) = fetch([pltpu.make_async_copy(wide_scale, scale_out, sems.at[3])])
    put_scale.wait()
    get_rope.wait()
    row = iota((2 * moves, 1), 0)
    column = iota((2 * moves, slots), 1)
    for k in range(partners):
        target = jnp.zeros((2 * moves, 1), jnp.int32)
        factor = jnp.zeros((2 * moves, 1), F32)
        for m in range(moves):
            page = move[0, me ^ (k + 1), m]
            target = jnp.where(row // 2 == m, page, target)
            factor = jnp.where(row // 2 == m, scale_out[page], factor)
        hit = column == target
        even = row % 2 == 0
        first = jnp.where(hit & even, 1.0, 0.0).astype(BF16)
        second = jnp.where(hit & (~even), 1.0, 0.0).astype(BF16)
        both = dot_nn(first, rope[:, :half]) + dot_nn(second, rope[:, half:])
        rope_outs[k][:, :half] = both.astype(BF16)
        rope_outs[k][:, half:] = jnp.broadcast_to(factor, (2 * moves, LANES)).astype(BF16)
    for copy in copies:
        copy.wait()


def spread(scores, start, count, stride, part):
    for b in range(scores.shape[0]):
        scores.at[b][pl.ds(start, count, stride=stride), :] = part[:, b * LANES : (b + 1) * LANES]


def read(scores, span):
    parts = [scores[b, span, :] for b in range(scores.shape[0])]
    return parts[0] if len(parts) == 1 else jnp.concatenate(parts, axis=1)


def write(scores, span, part):
    for b in range(scores.shape[0]):
        scores[b, span, :] = part[:, b * LANES : (b + 1) * LANES]


GROUP = 8


def local_kernel(
    sizes,
    partners,
    scale_hbm,
    table_hbm,
    lengths_hbm,
    move_hbm,
    lat_hbm,
    rope_hbm,
    q_hbm,
    turn_hbm,
    new_lat_hbm,
    new_rope_hbm,
    out,
    scale,
    qrel_out,
    q2_out,
    table,
    lengths,
    move,
    lat,
    rope,
    q_lat,
    q_rope,
    new_lat,
    new_rope,
    scores,
    limits,
    new_keys,
    new_turns,
    sems,
    lat_sems,
):
    heads, per_device, rollouts, following, view = sizes
    slots, page_len, latent = lat.shape
    rows = rollouts * following * heads
    rope_dim = q_rope.shape[3]
    moves = move.shape[2]
    me = lax.axis_index(DP)
    pairs = (
        (table_hbm, table),
        (lengths_hbm, lengths),
        (move_hbm, move),
        (scale_hbm, scale),
        (rope_hbm, rope),
        (turn_hbm, q_rope),
        (q_hbm, q_lat),
        (new_lat_hbm, new_lat),
        (new_rope_hbm, new_rope),
    )
    small = fetch(
        [pltpu.make_async_copy(src, dst, sems.at[i]) for i, (src, dst) in enumerate(pairs)]
    )
    chunks = fetch(
        [
            pltpu.make_async_copy(
                lat_hbm.at[pl.ds(at, GROUP)], lat.at[pl.ds(at, GROUP)], lat_sems.at[at // GROUP]
            )
            for at in range(0, slots, GROUP)
        ]
    )
    place = iota((rows, rows), 0)
    rollout = (place // following) % rollouts
    token = place % following
    head = place // (following * rollouts)
    source = (rollout * following + token) * heads + head
    order = jnp.where(iota((rows, rows), 1) == source, 1.0, 0.0).astype(BF16)
    at = iota((rope_dim, 2 * rope_dim), 1)
    frm = iota((rope_dim, 2 * rope_dim), 0)
    for copy in small:
        copy.wait()
    for slot in range(rollouts * view):
        limits[slot] = 0
    for r in range(rollouts):
        for a in range(table.shape[1]):
            live = jnp.clip(lengths[r] - a * page_len, 0, page_len)
            limits[r * view + table[r, a]] = live
    q_turn = dot_nn(order, q_rope[...].reshape(rows, rope_dim)).astype(BF16)
    q2_out[:rows, :] = dot_nn(q_turn, jnp.where(at == frm, 1.0, 0.0).astype(BF16)).astype(BF16)
    q2_out[rows:, :] = dot_nn(
        q_turn, jnp.where(at == frm + rope_dim, 1.0, 0.0).astype(BF16)
    ).astype(BF16)
    qrel_out[...] = dot_nn(order, q_lat[...].reshape(rows, latent)).astype(BF16)
    twos = page_len // 2
    wide = 2 * rope_dim
    stacked = jnp.concatenate([rope[:, c * wide : (c + 1) * wide] for c in range(twos)], axis=0)
    turned = dot_nt(stacked, q2_out[...])
    for c in range(twos):
        part = turned[c * slots : (c + 1) * slots]
        spread(scores, 2 * c, slots, page_len, part[:, :rows])
        spread(scores, 2 * c + 1, slots, page_len, part[:, rows:])

    lane_rollout = (iota((1, rows), 1) // following) % rollouts
    lane_token = iota((1, rows), 1) % following
    position = iota((page_len, rows), 0)

    def limit_row(slot):
        row = jnp.full(lane_rollout.shape, limits[slot], jnp.int32)
        for r in range(1, rollouts):
            row = jnp.where(lane_rollout == r, limits[r * view + slot], row)
        return row

    for k in range(partners):
        for m in range(moves):
            at = 2 * rows + 2 + k * moves + m
            limit = limit_row(slots + (me ^ (k + 1)) * moves + m)
            out[at : at + 1, :rows] = limit.astype(F32)
    queries = qrel_out[...]
    fresh_rows = rollouts * following
    new_keys[...] = jnp.zeros(new_keys.shape, F32)
    new_turns[...] = jnp.zeros(new_turns.shape, F32)
    for r in range(rollouts):
        span = slice(r * following, (r + 1) * following)
        new_keys[span, :] = new_lat[r].astype(F32)
        new_turns[span, :rope_dim] = new_rope[r].astype(F32)
    fresh_keys = new_keys[...].astype(BF16)
    new_part = dot_nt(fresh_keys, queries) + dot_nt(
        new_turns[...].astype(BF16), q2_out[:rows, :]
    )
    new_row = iota(new_part.shape, 0)
    seen = (new_row // following == lane_rollout) & (new_row % following <= lane_token)
    new_part = jnp.where(seen & (new_row < fresh_rows), new_part * SCORE_SCALE, LOW)

    best = jnp.full((page_len, rows), LOW, F32)
    for first in range(0, slots, GROUP):
        chunks[first // GROUP].wait()
        keys = lat[first : first + GROUP].reshape(GROUP * page_len, latent)
        fresh = dot_nt(keys, queries)
        for g in range(GROUP):
            page = first + g
            span = pl.ds(page * page_len, page_len)
            part = fresh[g * page_len : (g + 1) * page_len] + read(scores, span)
            part = part * (scale[page] * SCORE_SCALE)
            write(scores, span, part)
            best = jnp.maximum(best, jnp.where(position < limit_row(page), part, LOW))
    for m in range(moves):
        page = move[0, me, m]
        part = read(scores, pl.ds(pl.multiple_of(page * page_len, page_len), page_len))
        live = position < limit_row(slots + me * moves + m)
        best = jnp.maximum(best, jnp.where(live, part, LOW))
    peak = jnp.max(best, axis=0, keepdims=True)
    peak = jnp.maximum(peak, jnp.max(new_part, axis=0, keepdims=True))

    def weigh(part, slot, factor, total):
        grown = jnp.where(position < limit_row(slot), jnp.exp(part - peak), 0.0)
        return (grown * factor).astype(BF16), total + grown

    new_exp = jnp.exp(new_part - peak)
    total = jnp.zeros((page_len, rows), F32)
    acc = dot_tn(new_exp.astype(BF16), fresh_keys)
    for first in range(0, slots, GROUP):
        weights = []
        for g in range(GROUP):
            page = first + g
            part = read(scores, pl.ds(page * page_len, page_len))
            weight, total = weigh(part, page, scale[page], total)
            weights.append(weight)
        keys = lat[first : first + GROUP].reshape(GROUP * page_len, latent)
        acc = acc + dot_tn(jnp.concatenate(weights, axis=0), keys)
    weights, keys = [], []
    for m in range(moves):
        page = move[0, me, m]
        part = read(scores, pl.ds(pl.multiple_of(page * page_len, page_len), page_len))
        weight, total = weigh(part, slots + me * moves + m, scale[page], total)
        weights.append(weight)
        keys.append(lat[page])
    acc = acc + dot_tn(jnp.concatenate(weights, axis=0), jnp.concatenate(keys, axis=0))
    whole = jnp.sum(total, axis=0, keepdims=True) + jnp.sum(new_exp, axis=0, keepdims=True)
    out[:rows, :latent] = acc
    out[rows : 2 * rows, :latent] = qrel_out[...].astype(F32)
    out[2 * rows : 2 * rows + 1, :rows] = peak
    out[2 * rows + 1 : 2 * rows + 2, :rows] = whole
    out[: 2 * rows, latent:] = q2_out[...].astype(F32)


def merge_kernel(partners, *refs):
    got_lat, got_rope = refs[:partners], refs[partners : 2 * partners]
    local, out, scores = refs[2 * partners :]
    moves, page_len, latent = got_lat[0].shape
    rows = out.shape[0] * out.shape[1]
    qrel = local[rows : 2 * rows, :latent].astype(BF16)
    q2 = local[: 2 * rows, latent:].astype(BF16)
    wide = q2.shape[1]
    position = iota((page_len, rows), 0).astype(F32)
    best = jnp.full((page_len, rows), LOW, F32)
    half_lanes = got_rope[0].shape[1] - LANES
    pieces = half_lanes // wide
    span = moves * page_len
    factors = []
    for k in range(partners):
        turns = got_rope[k]
        stacked = jnp.concatenate(
            [turns[:, c * wide : (c + 1) * wide].astype(F32) for c in range(pieces)], axis=0
        ).astype(BF16)
        turned = dot_nt(stacked, q2)
        base = k * span
        for c in range(pieces):
            part = turned[c * 2 * moves : (c + 1) * 2 * moves]
            spread(scores, base + 2 * c, 2 * moves, page_len // 2, part[:, :rows])
            spread(scores, base + 2 * c + 1, 2 * moves, page_len // 2, part[:, rows:])
        fresh = dot_nt(got_lat[k][...].reshape(span, latent), qrel)
        marks = turns[:, half_lanes:].astype(F32)
        for m in range(moves):
            factor = marks[2 * m : 2 * m + 1, :1]
            factors.append(factor)
            where_at = pl.ds(base + m * page_len, page_len)
            part = fresh[m * page_len : (m + 1) * page_len] + read(scores, where_at)
            part = part * (factor * SCORE_SCALE)
            at = 2 * rows + 2 + k * moves + m
            part = jnp.where(position < local[at : at + 1, :rows], part, LOW)
            write(scores, where_at, part)
            best = jnp.maximum(best, part)
    peak_local = local[2 * rows : 2 * rows + 1, :rows]
    peak = jnp.maximum(jnp.max(best, axis=0, keepdims=True), peak_local)
    shrink = jnp.exp(peak_local - peak)
    acc = jnp.zeros((rows, latent), F32)
    grown_sum = jnp.zeros((page_len, rows), F32)
    for k in range(partners):
        weights = []
        for m in range(moves):
            part = read(scores, pl.ds(k * span + m * page_len, page_len))
            grown = jnp.exp(part - peak)
            grown_sum = grown_sum + grown
            weights.append((grown * factors[k * moves + m]).astype(BF16))
        acc = acc + dot_tn(
            jnp.concatenate(weights, axis=0), got_lat[k][...].reshape(span, latent)
        )
    total = local[2 * rows + 1 : 2 * rows + 2, :rows] * shrink + jnp.sum(grown_sum, axis=0, keepdims=True)

    def upright(row):
        return jnp.transpose(jnp.broadcast_to(row, (LANES, rows)))[:, :1]

    result = (local[:rows, :latent] * upright(shrink) + acc) / upright(total)
    out[...] = result.reshape(out.shape).astype(BF16)


def project_kernel(tokens, blocks, w_uv, w_out, away, kept):
    devices = blocks.shape[0]
    per_device = w_uv.shape[0]
    core = lax.axis_index("core")
    stacked = blocks[...].astype(F32).reshape(-1, blocks.shape[2]).astype(BF16)
    rows = stacked.shape[0]
    row_head = (iota((rows, 1), 0) // tokens) % per_device
    values = []
    for head in range(per_device):
        part = dot_nn(stacked, w_uv[head])
        values.append(jnp.where(row_head == head, part, 0.0).astype(BF16))
    values = jnp.concatenate(values, axis=1)
    half = devices // 2 * tokens
    out_row = iota((2 * half, rows), 0)
    in_row = iota((2 * half, rows), 1)
    out_device = (out_row % half) // tokens * 2 + jnp.where(out_row < half, 1 - core, core)
    same = (in_row // (tokens * per_device) == out_device) & (in_row % tokens == out_row % tokens)
    joined = dot_nn(jnp.where(same, 1.0, 0.0).astype(BF16), values).astype(BF16)
    width = w_out.shape[1]
    step = 512 if width % 512 == 0 else width
    for at in range(0, width, step):
        part = dot_nn(joined, w_out[:, at : at + step])
        away[:, at : at + step] = part[:half].astype(BF16)
        kept[:, at : at + step] = part[half:]


def split_kernel(kept, got, out):
    total = kept[...] + got[...].astype(F32)
    out[...] = total.reshape(out.shape).astype(BF16)


def norm_kernel(got, residual, gain, routes, attn_out, out):
    total = jnp.sum(got[...].astype(F32), axis=0)
    attn_out[...] = total.astype(BF16)
    hidden = (residual[...].astype(F32) + total).astype(BF16).astype(F32)
    width = hidden.shape[1]
    power = jnp.sum(hidden * hidden, axis=1, keepdims=True) / width
    normed = (hidden * lax.rsqrt(power + NORM_EPS) * gain[...].reshape(1, width)).astype(BF16)
    named = routes[...].astype(F32).astype(BF16)
    for copy in range(out.shape[0]):
        out[copy, :, :width] = normed
        out[copy, :, width:] = jnp.zeros((hidden.shape[0], LANES), BF16)
        out[copy, :, width : width + routes.shape[1]] = named


def stack_kernel(*refs):
    for k, ref in enumerate(refs[:-1]):
        refs[-1][k] = ref[0]


def parts_kernel(kept, got, *outs):
    total = kept[...] + got[...].astype(F32)
    rows = outs[0].shape[0]
    for k, out in enumerate(outs):
        out[...] = total[k * rows : (k + 1) * rows].astype(out.dtype)


def add_kernel(*refs):
    total = refs[0][...]
    for ref in refs[1:-1]:
        total = total + ref[...].astype(F32)
    refs[-1][...] = total.astype(BF16)


def load_kernel(count, passed, *refs):
    sources, passed_out, outs, sems = refs[:count], refs[count], refs[count + 1 : -1], refs[-1]
    split = sems.shape[1]
    copies = []
    for k, (source, out) in enumerate(zip(sources, outs)):
        step = out.shape[0] // split
        for i in range(split):
            span = pl.ds(i * step, step)
            copies.append(
                pltpu.make_async_copy(source.at[0, span], out.at[span], sems.at[k, i])
            )
    fetch(copies)
    passed_out[...] = passed[...]
    for copy in copies:
        copy.wait()


def expert_kernel(top, count, *refs):
    pieces = refs[:count]
    w_router, w_gate, w_up, down_hbm = refs[count : count + 4]
    kept, away, rows_ref, hidden_ref, w_down, sems = refs[count + 4 :]
    expert = lax.axis_index(EXPERT)
    width, units = w_gate.shape
    in_step = 256 if units % 256 == 0 else units
    out_step = 512 if width % 512 == 0 else width
    down_copies = fetch(
        [
            pltpu.make_async_copy(
                down_hbm.at[0, :, pl.ds(at, out_step)], w_down.at[:, pl.ds(at, out_step)], sems.at[i]
            )
            for i, at in enumerate(range(0, width, out_step))
        ]
    )
    piece_rows = rows_ref.shape[0] // count
    named = []
    for k, piece in enumerate(pieces):
        whole = piece[...].astype(F32).reshape(piece_rows, -1)
        rows_ref[k * piece_rows : (k + 1) * piece_rows, :] = whole[:, :width].astype(BF16)
        named.append(whole[:, width:])
    named = jnp.concatenate(named, axis=0)
    rows = rows_ref[...]
    logits = dot_nt(rows, w_router[...])
    experts = iota(logits.shape, 1)
    chosen = jnp.zeros(logits.shape, F32)
    for k in range(top):
        route = named[:, k : k + 1].astype(jnp.int32)
        chosen = chosen + jnp.where(route == experts, 1.0, 0.0)
    sig = jax.nn.sigmoid(logits) * chosen
    mine = jnp.sum(jnp.where(experts == expert, sig, 0.0), axis=1, keepdims=True)
    gates = ROUTE_SCALE * mine / jnp.sum(sig, axis=1, keepdims=True)
    for at in range(0, units, in_step):
        gate = dot_nn(rows, w_gate[:, at : at + in_step])
        up = dot_nn(rows, w_up[:, at : at + in_step])
        hidden_ref[:, at : at + in_step] = (gate / (1.0 + jnp.exp(-gate)) * up).astype(BF16)
    hidden = hidden_ref[...]
    half = rows_ref.shape[0] // 2
    for i, at in enumerate(range(0, width, out_step)):
        down_copies[i].wait()
        part = dot_nn(hidden, w_down[:, at : at + out_step]) * gates
        kept[:, at : at + out_step] = part[:half]
        away[:, at : at + out_step] = part[half:].astype(BF16)


def halve_kernel(kept, got, keep, away):
    total = kept[...] + got[...].astype(F32)
    half = total.shape[0] // 2
    keep[...] = total[:half]
    away[...] = total[half:].astype(BF16)


def sum_kernel(got, out):
    out[...] = jnp.sum(got[...].astype(F32), axis=0).astype(BF16)


def body(dp_count, expert_count, *arrays):
    (
        cache_lat,
        cache_rope,
        page_scale,
        move_list,
        page_table,
        lengths,
        q_lat,
        q_rope,
        new_lat,
        new_rope,
        w_uv,
        w_out,
        residual,
        norm_gain,
        w_router,
        routes,
        w_gate,
        w_up,
        w_down,
    ) = arrays
    total_devices = dp_count * expert_count
    top_bit = total_devices // 2
    side_bit = 2

    def swap(x, mask, mask_odd=None):
        pairs = []
        for i in range(total_devices):
            other = mask if mask_odd is None or i % 2 == 0 else mask_odd
            pairs.append((i, i ^ other))
        return lax.ppermute(x, ROWS, pairs)

    def deal(x, names):
        return lax.all_to_all(x, names, split_axis=0, concat_axis=0, tiled=True)

    slots, page_len, latent = cache_lat.shape
    moves = move_list.shape[2]
    rollouts, following, heads, rope_dim = q_rope.shape
    view = slots + dp_count * moves
    per_device = heads // expert_count
    tokens = rollouts * following
    width = residual.shape[1]
    partners = dp_count - 1
    rows = tokens * heads
    sizes = (heads, per_device, rollouts, following, view)

    picked = call(
        functools.partial(pick_kernel, partners, moves),
        [shape((moves, page_len, latent), BF16)] * partners
        + [shape((2 * moves, cache_rope.shape[1] // 2 + LANES), BF16)] * partners
        + [shape((slots,), F32)],
        (move_list, page_scale, cache_lat, cache_rope),
        in_specs=[HBM] * 4,
        out_specs=[VMEM] * (2 * partners) + [SMEM],
        scratch=[
            pltpu.SMEM(move_list.shape, jnp.int32),
            pltpu.VMEM(cache_rope.shape, BF16),
            pltpu.VMEM(page_scale.shape, BF16),
            pltpu.VMEM((slots,), F32),
            pltpu.SemaphoreType.DMA((partners, moves)),
            pltpu.SemaphoreType.DMA((4,)),
        ],
        vmem=60,
    )
    got_lat = [swap(picked[k], (k + 1) * expert_count) for k in range(partners)]
    got_rope = [swap(picked[partners + k], (k + 1) * expert_count) for k in range(partners)]

    extra = -(-(2 + partners * moves) // 8) * 8
    local = call(
        functools.partial(local_kernel, sizes, partners),
        [shape((2 * rows + extra, latent + 2 * rope_dim), F32)],
        (
            picked[-1],
            page_table,
            lengths,
            move_list,
            cache_lat,
            cache_rope,
            q_lat,
            q_rope,
            new_lat,
            new_rope,
        ),
        in_specs=[HBM] * 10,
        scratch=[
            pltpu.SMEM((slots,), F32),
            pltpu.VMEM((rows, latent), BF16),
            pltpu.VMEM((2 * rows, 2 * rope_dim), BF16),
            pltpu.SMEM(page_table.shape, jnp.int32),
            pltpu.SMEM(lengths.shape, jnp.int32),
            pltpu.SMEM(move_list.shape, jnp.int32),
            pltpu.VMEM(cache_lat.shape, BF16),
            pltpu.VMEM(cache_rope.shape, BF16),
            pltpu.VMEM(q_lat.shape, BF16),
            pltpu.VMEM(q_rope.shape, BF16),
            pltpu.VMEM(new_lat.shape, BF16),
            pltpu.VMEM(new_rope.shape, BF16),
            pltpu.VMEM((rows // LANES, slots * page_len, LANES), F32),
            pltpu.SMEM((rollouts * view,), jnp.int32),
            pltpu.VMEM((16, latent), F32),
            pltpu.VMEM((16, 2 * rope_dim), F32),
            pltpu.SemaphoreType.DMA((9,)),
            pltpu.SemaphoreType.DMA((slots // GROUP,)),
        ],
        vmem=60,
        cost=(2 * slots * page_len * rows * (2 * latent + 2 * rope_dim), 4 * MIB),
    )
    blocks = call(
        functools.partial(merge_kernel, partners),
        [shape((expert_count, tokens * per_device, latent), BF16)],
        (*got_lat, *got_rope, *local),
        scratch=[pltpu.VMEM((rows // LANES, partners * moves * page_len, LANES), F32)],
        cost=(2 * moves * page_len * rows * 2 * latent, MIB),
    )[0]

    blocks = deal(blocks, EXPERT)

    half_rows = expert_count // 2 * tokens
    away, kept = call(
        functools.partial(project_kernel, tokens),
        [shape((half_rows, width), BF16), shape((half_rows, width), F32)],
        (blocks, w_uv, w_out),
        cost=(4 * half_rows * width * w_out.shape[0], 4 * MIB),
    )
    parts = call(
        split_kernel,
        [shape((expert_count // 2, tokens, width), BF16)],
        (kept, swap(away, 1)),
    )[0]
    parts = deal(parts, ("far", "side"))
    far_count = total_devices // 8
    masks = [2 * side_bit * k for k in range(far_count)]
    direct = far_count <= 4
    attn_out, own_rows = call(
        norm_kernel,
        [
            shape((tokens, width), BF16),
            shape((1 if direct else far_count, tokens, width + LANES), BF16),
        ],
        (parts, residual, norm_gain, routes),
    )

    def load(passed, sources, vmem):
        return call(
            functools.partial(load_kernel, len(sources)),
            [shape(passed.shape, BF16)] + [shape(w.shape[1:], BF16) for w in sources],
            (passed, *sources),
            in_specs=[VMEM] + [HBM] * len(sources),
            scratch=[pltpu.SemaphoreType.DMA((len(sources), 8))],
            vmem=vmem,
            cost=(0, 2 * sum(w.size for w in sources)),
        )

    if direct:
        others = [swap(own_rows, mask) for mask in masks[1:]]
        piece = call(
            stack_kernel,
            [shape((far_count, tokens, width + LANES), BF16)],
            (own_rows, *others),
        )[0]
    else:
        piece = deal(own_rows, FAR)
    pieces = [piece, swap(piece, top_bit, side_bit)]
    pieces = pieces + [swap(p, side_bit, top_bit) for p in pieces]
    side_piece, gate_here, up_here = load(pieces[1], (w_gate, w_up), LOAD_MIB)
    pieces = [piece, side_piece] + pieces[2:]
    pieces = pieces + [swap(p, 1) for p in pieces]

    all_rows = total_devices * tokens
    hidden_units = w_gate.shape[2]
    half = all_rows // 2
    kept, away = call(
        functools.partial(expert_kernel, routes.shape[1], len(pieces)),
        [shape((half, width), F32), shape((half, width), BF16)],
        (*pieces, w_router.T, gate_here, up_here, w_down),
        in_specs=[VMEM] * (len(pieces) + 3) + [HBM],
        scratch=[
            pltpu.VMEM((all_rows, width), BF16),
            pltpu.VMEM((all_rows, hidden_units), BF16),
            pltpu.VMEM(w_down.shape[1:], BF16),
            pltpu.SemaphoreType.DMA((16,)),
        ],
        vmem=EXPERT_MIB if all_rows <= 256 else 56,
        cost=(6 * all_rows * width * hidden_units, 6 * width * hidden_units),
    )

    got = swap(away, 1)
    kept, away = call(
        halve_kernel,
        [shape((half // 2, width), F32), shape((half // 2, width), BF16)],
        (kept, got),
    )
    got = swap(away, side_bit, top_bit)
    kept, away = call(
        halve_kernel,
        [shape((half // 4, width), F32), shape((half // 4, width), BF16)],
        (kept, got),
    )
    got = swap(away, top_bit, side_bit)
    moe_shape = [shape((tokens, width), BF16)]
    if direct:
        parts = call(
            parts_kernel, [shape((tokens, width), F32)] + moe_shape * (far_count - 1), (kept, got)
        )
        got = [swap(part, mask) for part, mask in zip(parts[1:], masks[1:])]
        moe_out = call(add_kernel, moe_shape, (parts[0], *got))[0]
    else:
        parts = call(split_kernel, [shape((far_count, tokens, width), BF16)], (kept, got))[0]
        moe_out = call(sum_kernel, moe_shape, (deal(parts, FAR),))[0]
    return (attn_out, moe_out)


def solution(mesh):
    dp_count, expert_count = mesh.shape["dp"], mesh.shape["expert"]
    finer = Mesh(mesh.devices.reshape(2, dp_count // 2, expert_count // 4, 2, 2), ROWS)
    return jax.shard_map(
        functools.partial(body, dp_count, expert_count),
        mesh=finer,
        in_specs=(
            P(ROWS, None, None),
            P(ROWS, None),
            P(ROWS),
            P(ROWS, None, None),
            P(ROWS, None),
            P(ROWS),
            P(ROWS, None, None, None),
            P(ROWS, None, None, None),
            P(ROWS, None, None),
            P(ROWS, None, None),
            P(EXPERT, None, None),
            P(EXPERT, None),
            P(ROWS, None),
            P(),
            P(),
            P(ROWS, None),
            P(EXPERT, None, DP),
            P(EXPERT, None, DP),
            P(EXPERT, DP, None),
        ),
        out_specs=(P(ROWS, None), P(ROWS, None)),
        check_vma=False,
    )
```

```python
import functools

import jax
import jax.numpy as jnp
from jax import lax
from jax.experimental import pallas as pl
from jax.experimental.pallas import tpu as pltpu
from jax.sharding import Mesh, PartitionSpec as P

SCORE_SCALE = 0.07216878364870322
ROUTE_SCALE = 2.5
NORM_EPS = 1e-06
LOW = -1e30
LANES = 128
MIB = 1 << 20
BF16 = jnp.bfloat16
F32 = jnp.float32
VMEM = pl.BlockSpec(memory_space=pltpu.VMEM)
SMEM = pl.BlockSpec(memory_space=pltpu.SMEM)
ANY = pl.BlockSpec(memory_space=pl.ANY)
HBM = pl.BlockSpec(memory_space=pltpu.HBM)
DP = ("top", "low")
EXPERT = ("far", "side", "core")
ROWS = DP + EXPERT
FAR = ("low", "far")
CHIP = ("far", "side")
LOAD_MIB = 36
EXPERT_MIB = 36


def dot_nt(a, b):
    return lax.dot_general(a, b, (((1,), (1,)), ((), ())), preferred_element_type=F32)


def dot_tn(a, b):
    return lax.dot_general(a, b, (((0,), (0,)), ((), ())), preferred_element_type=F32)


def dot_nn(a, b):
    return jnp.dot(a, b, preferred_element_type=F32)


def call(kernel, outs, operands, in_specs=None, out_specs=None, scratch=(), vmem=16, cost=None):
    flops, moved = cost or (0, 0)
    return pl.pallas_call(
        kernel,
        out_shape=outs,
        in_specs=in_specs or [VMEM] * len(operands),
        out_specs=out_specs or [VMEM] * len(outs),
        scratch_shapes=list(scratch),
        compiler_params=pltpu.CompilerParams(vmem_limit_bytes=vmem * MIB),
        cost_estimate=pl.CostEstimate(flops=flops, bytes_accessed=moved, transcendentals=0),
    )(*operands)


def shape(dims, dtype):
    return jax.ShapeDtypeStruct(dims, dtype)


def iota(dims, axis):
    return lax.broadcasted_iota(jnp.int32, dims, axis)


def fetch(copies):
    for copy in copies:
        copy.start()
    return copies


def pick_kernel(partners, moves, move_hbm, scale_hbm, lat, rope_hbm, *rest):
    lat_outs, rope_outs = rest[:partners], rest[partners : 2 * partners]
    scale_out, move, rope, scale_ref, wide_scale, lat_sems, sems = rest[2 * partners :]
    slots, width = rope.shape
    half = width // 2
    me = lax.axis_index(DP)
    get_move, get_scale, get_rope = fetch(
        [
            pltpu.make_async_copy(move_hbm, move, sems.at[0]),
            pltpu.make_async_copy(scale_hbm, scale_ref, sems.at[1]),
            pltpu.make_async_copy(rope_hbm, rope, sems.at[2]),
        ]
    )
    get_move.wait()
    copies = []
    for k in range(partners):
        for m in range(moves):
            copies.append(
                pltpu.make_async_copy(
                    lat.at[move[0, me ^ (k + 1), m]], lat_outs[k].at[m], lat_sems.at[k, m]
                )
            )
    fetch(copies)
    get_scale.wait()
    wide_scale[...] = scale_ref[...].astype(F32)
    (put_scale,) = fetch([pltpu.make_async_copy(wide_scale, scale_out, sems.at[3])])
    put_scale.wait()
    get_rope.wait()
    row = iota((2 * moves, 1), 0)
    column = iota((2 * moves, slots), 1)
    for k in range(partners):
        target = jnp.zeros((2 * moves, 1), jnp.int32)
        factor = jnp.zeros((2 * moves, 1), F32)
        for m in range(moves):
            page = move[0, me ^ (k + 1), m]
            target = jnp.where(row // 2 == m, page, target)
            factor = jnp.where(row // 2 == m, scale_out[page], factor)
        hit = column == target
        even = row % 2 == 0
        first = jnp.where(hit & even, 1.0, 0.0).astype(BF16)
        second = jnp.where(hit & (~even), 1.0, 0.0).astype(BF16)
        both = dot_nn(first, rope[:, :half]) + dot_nn(second, rope[:, half:])
        rope_outs[k][:, :half] = both.astype(BF16)
        rope_outs[k][:, half:] = jnp.broadcast_to(factor, (2 * moves, LANES)).astype(BF16)
    for copy in copies:
        copy.wait()


def spread(scores, start, count, stride, part):
    for b in range(scores.shape[0]):
        scores.at[b][pl.ds(start, count, stride=stride), :] = part[:, b * LANES : (b + 1) * LANES]


def read(scores, span):
    parts = [scores[b, span, :] for b in range(scores.shape[0])]
    return parts[0] if len(parts) == 1 else jnp.concatenate(parts, axis=1)


def write(scores, span, part):
    for b in range(scores.shape[0]):
        scores[b, span, :] = part[:, b * LANES : (b + 1) * LANES]


GROUP = 8


def local_kernel(
    sizes,
    partners,
    scale_hbm,
    table_hbm,
    lengths_hbm,
    move_hbm,
    lat_hbm,
    rope_hbm,
    q_hbm,
    turn_hbm,
    new_lat_hbm,
    new_rope_hbm,
    out,
    scale,
    qrel_out,
    q2_out,
    table,
    lengths,
    move,
    lat,
    rope,
    q_lat,
    q_rope,
    new_lat,
    new_rope,
    scores,
    limits,
    new_keys,
    new_turns,
    sems,
    lat_sems,
):
    heads, per_device, rollouts, following, view = sizes
    slots, page_len, latent = lat.shape
    rows = rollouts * following * heads
    rope_dim = q_rope.shape[3]
    moves = move.shape[2]
    me = lax.axis_index(DP)
    pairs = (
        (table_hbm, table),
        (lengths_hbm, lengths),
        (move_hbm, move),
        (scale_hbm, scale),
        (rope_hbm, rope),
        (turn_hbm, q_rope),
        (q_hbm, q_lat),
        (new_lat_hbm, new_lat),
        (new_rope_hbm, new_rope),
    )
    small = fetch(
        [pltpu.make_async_copy(src, dst, sems.at[i]) for i, (src, dst) in enumerate(pairs)]
    )
    chunks = fetch(
        [
            pltpu.make_async_copy(
                lat_hbm.at[pl.ds(at, GROUP)], lat.at[pl.ds(at, GROUP)], lat_sems.at[at // GROUP]
            )
            for at in range(0, slots, GROUP)
        ]
    )
    place = iota((rows, rows), 0)
    rollout = (place // following) % rollouts
    token = place % following
    head = place // (following * rollouts)
    source = (rollout * following + token) * heads + head
    order = jnp.where(iota((rows, rows), 1) == source, 1.0, 0.0).astype(BF16)
    at = iota((rope_dim, 2 * rope_dim), 1)
    frm = iota((rope_dim, 2 * rope_dim), 0)
    for copy in small:
        copy.wait()
    for slot in range(rollouts * view):
        limits[slot] = 0
    for r in range(rollouts):
        for a in range(table.shape[1]):
            live = jnp.clip(lengths[r] - a * page_len, 0, page_len)
            limits[r * view + table[r, a]] = live
    q_turn = dot_nn(order, q_rope[...].reshape(rows, rope_dim)).astype(BF16)
    q2_out[:rows, :] = dot_nn(q_turn, jnp.where(at == frm, 1.0, 0.0).astype(BF16)).astype(BF16)
    q2_out[rows:, :] = dot_nn(
        q_turn, jnp.where(at == frm + rope_dim, 1.0, 0.0).astype(BF16)
    ).astype(BF16)
    qrel_out[...] = dot_nn(order, q_lat[...].reshape(rows, latent)).astype(BF16)
    twos = page_len // 2
    wide = 2 * rope_dim
    stacked = jnp.concatenate([rope[:, c * wide : (c + 1) * wide] for c in range(twos)], axis=0)
    turned = dot_nt(stacked, q2_out[...])
    for c in range(twos):
        part = turned[c * slots : (c + 1) * slots]
        spread(scores, 2 * c, slots, page_len, part[:, :rows])
        spread(scores, 2 * c + 1, slots, page_len, part[:, rows:])

    lane_rollout = (iota((1, rows), 1) // following) % rollouts
    lane_token = iota((1, rows), 1) % following
    position = iota((page_len, rows), 0)

    def limit_row(slot):
        row = jnp.full(lane_rollout.shape, limits[slot], jnp.int32)
        for r in range(1, rollouts):
            row = jnp.where(lane_rollout == r, limits[r * view + slot], row)
        return row

    for k in range(partners):
        for m in range(moves):
            at = 2 * rows + 2 + k * moves + m
            limit = limit_row(slots + (me ^ (k + 1)) * moves + m)
            out[at : at + 1, :rows] = limit.astype(F32)
    queries = qrel_out[...]
    fresh_rows = rollouts * following
    new_keys[...] = jnp.zeros(new_keys.shape, F32)
    new_turns[...] = jnp.zeros(new_turns.shape, F32)
    for r in range(rollouts):
        span = slice(r * following, (r + 1) * following)
        new_keys[span, :] = new_lat[r].astype(F32)
        new_turns[span, :rope_dim] = new_rope[r].astype(F32)
    fresh_keys = new_keys[...].astype(BF16)
    new_part = dot_nt(fresh_keys, queries) + dot_nt(
        new_turns[...].astype(BF16), q2_out[:rows, :]
    )
    new_row = iota(new_part.shape, 0)
    seen = (new_row // following == lane_rollout) & (new_row % following <= lane_token)
    new_part = jnp.where(seen & (new_row < fresh_rows), new_part * SCORE_SCALE, LOW)

    best = jnp.full((page_len, rows), LOW, F32)
    for first in range(0, slots, GROUP):
        chunks[first // GROUP].wait()
        keys = lat[first : first + GROUP].reshape(GROUP * page_len, latent)
        fresh = dot_nt(keys, queries)
        for g in range(GROUP):
            page = first + g
            span = pl.ds(page * page_len, page_len)
            part = fresh[g * page_len : (g + 1) * page_len] + read(scores, span)
            part = part * (scale[page] * SCORE_SCALE)
            write(scores, span, part)
            best = jnp.maximum(best, jnp.where(position < limit_row(page), part, LOW))
    for m in range(moves):
        page = move[0, me, m]
        part = read(scores, pl.ds(pl.multiple_of(page * page_len, page_len), page_len))
        live = position < limit_row(slots + me * moves + m)
        best = jnp.maximum(best, jnp.where(live, part, LOW))
    peak = jnp.max(best, axis=0, keepdims=True)
    peak = jnp.maximum(peak, jnp.max(new_part, axis=0, keepdims=True))

    def weigh(part, slot, factor, total):
        grown = jnp.where(position < limit_row(slot), jnp.exp(part - peak), 0.0)
        return (grown * factor).astype(BF16), total + grown

    new_exp = jnp.exp(new_part - peak)
    total = jnp.zeros((page_len, rows), F32)
    acc = dot_tn(new_exp.astype(BF16), fresh_keys)
    for first in range(0, slots, GROUP):
        weights = []
        for g in range(GROUP):
            page = first + g
            part = read(scores, pl.ds(page * page_len, page_len))
            weight, total = weigh(part, page, scale[page], total)
            weights.append(weight)
        keys = lat[first : first + GROUP].reshape(GROUP * page_len, latent)
        acc = acc + dot_tn(jnp.concatenate(weights, axis=0), keys)
    weights, keys = [], []
    for m in range(moves):
        page = move[0, me, m]
        part = read(scores, pl.ds(pl.multiple_of(page * page_len, page_len), page_len))
        weight, total = weigh(part, slots + me * moves + m, scale[page], total)
        weights.append(weight)
        keys.append(lat[page])
    acc = acc + dot_tn(jnp.concatenate(weights, axis=0), jnp.concatenate(keys, axis=0))
    whole = jnp.sum(total, axis=0, keepdims=True) + jnp.sum(new_exp, axis=0, keepdims=True)
    out[:rows, :latent] = acc
    out[rows : 2 * rows, :latent] = qrel_out[...].astype(F32)
    out[2 * rows : 2 * rows + 1, :rows] = peak
    out[2 * rows + 1 : 2 * rows + 2, :rows] = whole
    out[: 2 * rows, latent:] = q2_out[...].astype(F32)


def merge_kernel(partners, *refs):
    got_lat, got_rope = refs[:partners], refs[partners : 2 * partners]
    local, out, scores = refs[2 * partners :]
    moves, page_len, latent = got_lat[0].shape
    rows = out.shape[0] * out.shape[1]
    qrel = local[rows : 2 * rows, :latent].astype(BF16)
    q2 = local[: 2 * rows, latent:].astype(BF16)
    wide = q2.shape[1]
    position = iota((page_len, rows), 0).astype(F32)
    best = jnp.full((page_len, rows), LOW, F32)
    half_lanes = got_rope[0].shape[1] - LANES
    pieces = half_lanes // wide
    span = moves * page_len
    factors = []
    for k in range(partners):
        turns = got_rope[k]
        stacked = jnp.concatenate(
            [turns[:, c * wide : (c + 1) * wide].astype(F32) for c in range(pieces)], axis=0
        ).astype(BF16)
        turned = dot_nt(stacked, q2)
        base = k * span
        for c in range(pieces):
            part = turned[c * 2 * moves : (c + 1) * 2 * moves]
            spread(scores, base + 2 * c, 2 * moves, page_len // 2, part[:, :rows])
            spread(scores, base + 2 * c + 1, 2 * moves, page_len // 2, part[:, rows:])
        fresh = dot_nt(got_lat[k][...].reshape(span, latent), qrel)
        marks = turns[:, half_lanes:].astype(F32)
        for m in range(moves):
            factor = marks[2 * m : 2 * m + 1, :1]
            factors.append(factor)
            where_at = pl.ds(base + m * page_len, page_len)
            part = fresh[m * page_len : (m + 1) * page_len] + read(scores, where_at)
            part = part * (factor * SCORE_SCALE)
            at = 2 * rows + 2 + k * moves + m
            part = jnp.where(position < local[at : at + 1, :rows], part, LOW)
            write(scores, where_at, part)
            best = jnp.maximum(best, part)
    peak_local = local[2 * rows : 2 * rows + 1, :rows]
    peak = jnp.maximum(jnp.max(best, axis=0, keepdims=True), peak_local)
    shrink = jnp.exp(peak_local - peak)
    acc = jnp.zeros((rows, latent), F32)
    grown_sum = jnp.zeros((page_len, rows), F32)
    for k in range(partners):
        weights = []
        for m in range(moves):
            part = read(scores, pl.ds(k * span + m * page_len, page_len))
            grown = jnp.exp(part - peak)
            grown_sum = grown_sum + grown
            weights.append((grown * factors[k * moves + m]).astype(BF16))
        acc = acc + dot_tn(
            jnp.concatenate(weights, axis=0), got_lat[k][...].reshape(span, latent)
        )
    total = local[2 * rows + 1 : 2 * rows + 2, :rows] * shrink + jnp.sum(grown_sum, axis=0, keepdims=True)

    def upright(row):
        return jnp.transpose(jnp.broadcast_to(row, (LANES, rows)))[:, :1]

    result = (local[:rows, :latent] * upright(shrink) + acc) / upright(total)
    out[...] = result.reshape(out.shape).astype(BF16)


def project_kernel(tokens, blocks, w_uv, other_uv, w_out, other_out, out):
    chips = blocks.shape[0]
    per_device = w_uv.shape[0]
    core = lax.axis_index("core")
    stacked = blocks[...].astype(F32).reshape(-1, blocks.shape[2]).astype(BF16)
    rows = stacked.shape[0]
    row_head = (iota((rows, 1), 0) // tokens) % (2 * per_device)
    values = []
    for first, uv in ((core * per_device, w_uv), ((1 - core) * per_device, other_uv)):
        for head in range(per_device):
            part = dot_nn(stacked, uv[head])
            values.append(jnp.where(row_head == first + head, part, 0.0).astype(BF16))
    values = jnp.concatenate(values, axis=1)
    out_row = iota((chips * tokens, rows), 0)
    in_row = iota((chips * tokens, rows), 1)
    same_chip = in_row // (tokens * 2 * per_device) == out_row // tokens
    same = same_chip & (in_row % tokens == out_row % tokens)
    joined = dot_nn(jnp.where(same, 1.0, 0.0).astype(BF16), values).astype(BF16)
    depth, width = w_out.shape
    step = 512 if width % 512 == 0 else width
    for at in range(0, width, step):
        part = dot_nn(joined[:, :depth], w_out[:, at : at + step])
        part = part + dot_nn(joined[:, depth:], other_out[:, at : at + step])
        out[:, :, at : at + step] = part.reshape(chips, tokens, step).astype(BF16)


def split_kernel(kept, got, out):
    total = kept[...] + got[...].astype(F32)
    out[...] = total.reshape(out.shape).astype(BF16)


def norm_kernel(got, residual, gain, routes, attn_out, out):
    total = jnp.sum(got[...].astype(F32), axis=0)
    attn_out[...] = total.astype(BF16)
    hidden = (residual[...].astype(F32) + total).astype(BF16).astype(F32)
    width = hidden.shape[1]
    power = jnp.sum(hidden * hidden, axis=1, keepdims=True) / width
    normed = (hidden * lax.rsqrt(power + NORM_EPS) * gain[...].reshape(1, width)).astype(BF16)
    named = routes[...].astype(F32).astype(BF16)
    for copy in range(out.shape[0]):
        out[copy, :, :width] = normed
        out[copy, :, width:] = jnp.zeros((hidden.shape[0], LANES), BF16)
        out[copy, :, width : width + routes.shape[1]] = named


def stack_kernel(*refs):
    for k, ref in enumerate(refs[:-1]):
        refs[-1][k] = ref[0]


def parts_kernel(kept, got, *outs):
    total = kept[...] + got[...].astype(F32)
    rows = outs[0].shape[0]
    for k, out in enumerate(outs):
        out[...] = total[k * rows : (k + 1) * rows].astype(out.dtype)


def add_kernel(*refs):
    total = refs[0][...]
    for ref in refs[1:-1]:
        total = total + ref[...].astype(F32)
    refs[-1][...] = total.astype(BF16)


def load_kernel(count, passed, *refs):
    sources, passed_out, outs, sems = refs[:count], refs[count], refs[count + 1 : -1], refs[-1]
    split = sems.shape[1]
    copies = []
    for k, (source, out) in enumerate(zip(sources, outs)):
        step = out.shape[0] // split
        for i in range(split):
            span = pl.ds(i * step, step)
            copies.append(
                pltpu.make_async_copy(source.at[0, span], out.at[span], sems.at[k, i])
            )
    fetch(copies)
    passed_out[...] = passed[...]
    for copy in copies:
        copy.wait()


def expert_kernel(top, count, *refs):
    pieces = refs[:count]
    w_router, w_gate, w_up, down_hbm = refs[count : count + 4]
    kept, away, rows_ref, hidden_ref, acc, w_down, sems = refs[count + 4 :]
    expert = lax.axis_index(EXPERT)
    width, units = w_gate.shape
    in_step = 256 if units % 256 == 0 else units
    out_step = 512 if width % 512 == 0 else width
    down_copies = fetch(
        [
            pltpu.make_async_copy(
                down_hbm.at[0, pl.ds(at, in_step)], w_down.at[pl.ds(at, in_step)], sems.at[i]
            )
            for i, at in enumerate(range(0, units, in_step))
        ]
    )
    piece_rows = rows_ref.shape[0] // count
    named = []
    for k, piece in enumerate(pieces):
        whole = piece[...].astype(F32).reshape(piece_rows, -1)
        rows_ref[k * piece_rows : (k + 1) * piece_rows, :] = whole[:, :width].astype(BF16)
        named.append(whole[:, width:])
    named = jnp.concatenate(named, axis=0)
    rows = rows_ref[...]
    logits = dot_nt(rows, w_router[...])
    experts = iota(logits.shape, 1)
    chosen = jnp.zeros(logits.shape, F32)
    for k in range(top):
        route = named[:, k : k + 1].astype(jnp.int32)
        chosen = chosen + jnp.where(route == experts, 1.0, 0.0)
    sig = jax.nn.sigmoid(logits) * chosen
    mine = jnp.sum(jnp.where(experts == expert, sig, 0.0), axis=1, keepdims=True)
    gates = ROUTE_SCALE * mine / jnp.sum(sig, axis=1, keepdims=True)
    for at in range(0, units, in_step):
        gate = dot_nn(rows, w_gate[:, at : at + in_step])
        up = dot_nn(rows, w_up[:, at : at + in_step])
        hidden_ref[:, at : at + in_step] = (gate / (1.0 + jnp.exp(-gate)) * up).astype(BF16)
    half = rows_ref.shape[0] // 2
    steps = units // in_step
    for i, down_copy in enumerate(down_copies):
        down_copy.wait()
        span = slice(i * in_step, (i + 1) * in_step)
        hidden = hidden_ref[:, span]
        for at in range(0, width, out_step):
            part = dot_nn(hidden, w_down[span, at : at + out_step])
            if i:
                part = part + acc[:, at : at + out_step]
            if i < steps - 1:
                acc[:, at : at + out_step] = part
            else:
                part = part * gates
                kept[:, at : at + out_step] = part[:half]
                away[:, at : at + out_step] = part[half:].astype(BF16)


def halve_kernel(kept, got, keep, away):
    total = kept[...] + got[...].astype(F32)
    half = total.shape[0] // 2
    keep[...] = total[:half]
    away[...] = total[half:].astype(BF16)


def sum_kernel(got, out):
    out[...] = jnp.sum(got[...].astype(F32), axis=0).astype(BF16)


def body(dp_count, expert_count, *arrays):
    (
        cache_lat,
        cache_rope,
        page_scale,
        move_list,
        page_table,
        lengths,
        q_lat,
        q_rope,
        new_lat,
        new_rope,
        w_uv,
        w_out,
        residual,
        norm_gain,
        w_router,
        routes,
        w_gate,
        w_up,
        w_down,
    ) = arrays
    total_devices = dp_count * expert_count
    top_bit = total_devices // 2
    side_bit = 2

    def swap(x, mask, mask_odd=None):
        pairs = []
        for i in range(total_devices):
            other = mask if mask_odd is None or i % 2 == 0 else mask_odd
            pairs.append((i, i ^ other))
        return lax.ppermute(x, ROWS, pairs)

    def deal(x, names):
        return lax.all_to_all(x, names, split_axis=0, concat_axis=0, tiled=True)

    slots, page_len, latent = cache_lat.shape
    moves = move_list.shape[2]
    rollouts, following, heads, rope_dim = q_rope.shape
    view = slots + dp_count * moves
    per_device = heads // expert_count
    tokens = rollouts * following
    width = residual.shape[1]
    partners = dp_count - 1
    rows = tokens * heads
    sizes = (heads, per_device, rollouts, following, view)
    chips = expert_count // 2
    other_uv, other_out = swap(w_uv, 1), swap(w_out, 1)

    picked = call(
        functools.partial(pick_kernel, partners, moves),
        [shape((moves, page_len, latent), BF16)] * partners
        + [shape((2 * moves, cache_rope.shape[1] // 2 + LANES), BF16)] * partners
        + [shape((slots,), F32)],
        (move_list, page_scale, cache_lat, cache_rope),
        in_specs=[HBM] * 4,
        out_specs=[VMEM] * (2 * partners) + [SMEM],
        scratch=[
            pltpu.SMEM(move_list.shape, jnp.int32),
            pltpu.VMEM(cache_rope.shape, BF16),
            pltpu.VMEM(page_scale.shape, BF16),
            pltpu.VMEM((slots,), F32),
            pltpu.SemaphoreType.DMA((partners, moves)),
            pltpu.SemaphoreType.DMA((4,)),
        ],
        vmem=57,
    )
    got_lat = [swap(picked[k], (k + 1) * expert_count) for k in range(partners)]
    got_rope = [swap(picked[partners + k], (k + 1) * expert_count) for k in range(partners)]

    extra = -(-(2 + partners * moves) // 8) * 8
    local = call(
        functools.partial(local_kernel, sizes, partners),
        [shape((2 * rows + extra, latent + 2 * rope_dim), F32)],
        (
            picked[-1],
            page_table,
            lengths,
            move_list,
            cache_lat,
            cache_rope,
            q_lat,
            q_rope,
            new_lat,
            new_rope,
        ),
        in_specs=[HBM] * 10,
        scratch=[
            pltpu.SMEM((slots,), F32),
            pltpu.VMEM((rows, latent), BF16),
            pltpu.VMEM((2 * rows, 2 * rope_dim), BF16),
            pltpu.SMEM(page_table.shape, jnp.int32),
            pltpu.SMEM(lengths.shape, jnp.int32),
            pltpu.SMEM(move_list.shape, jnp.int32),
            pltpu.VMEM(cache_lat.shape, BF16),
            pltpu.VMEM(cache_rope.shape, BF16),
            pltpu.VMEM(q_lat.shape, BF16),
            pltpu.VMEM(q_rope.shape, BF16),
            pltpu.VMEM(new_lat.shape, BF16),
            pltpu.VMEM(new_rope.shape, BF16),
            pltpu.VMEM((rows // LANES, slots * page_len, LANES), F32),
            pltpu.SMEM((rollouts * view,), jnp.int32),
            pltpu.VMEM((16, latent), F32),
            pltpu.VMEM((16, 2 * rope_dim), F32),
            pltpu.SemaphoreType.DMA((9,)),
            pltpu.SemaphoreType.DMA((slots // GROUP,)),
        ],
        vmem=57,
        cost=(2 * slots * page_len * rows * (2 * latent + 2 * rope_dim), 4 * MIB),
    )
    blocks = call(
        functools.partial(merge_kernel, partners),
        [shape((chips, 2 * tokens * per_device, latent), BF16)],
        (*got_lat, *got_rope, *local),
        scratch=[pltpu.VMEM((rows // LANES, partners * moves * page_len, LANES), F32)],
        cost=(2 * moves * page_len * rows * 2 * latent, MIB),
    )[0]

    blocks = deal(blocks, CHIP)

    parts = call(
        functools.partial(project_kernel, tokens),
        [shape((chips, tokens, width), BF16)],
        (blocks, w_uv, other_uv, w_out, other_out),
        cost=(4 * chips * tokens * width * w_out.shape[0], 8 * MIB),
    )[0]
    parts = deal(parts, CHIP)
    far_count = total_devices // 8
    masks = [2 * side_bit * k for k in range(far_count)]
    direct = far_count <= 4
    attn_out, own_rows = call(
        norm_kernel,
        [
            shape((tokens, width), BF16),
            shape((1 if direct else far_count, tokens, width + LANES), BF16),
        ],
        (parts, residual, norm_gain, routes),
    )

    def load(passed, sources, vmem):
        return call(
            functools.partial(load_kernel, len(sources)),
            [shape(passed.shape, BF16)] + [shape(w.shape[1:], BF16) for w in sources],
            (passed, *sources),
            in_specs=[VMEM] + [HBM] * len(sources),
            scratch=[pltpu.SemaphoreType.DMA((len(sources), 8))],
            vmem=vmem,
            cost=(0, 2 * sum(w.size for w in sources)),
        )

    if direct:
        others = [swap(own_rows, mask) for mask in masks[1:]]
        piece = call(
            stack_kernel,
            [shape((far_count, tokens, width + LANES), BF16)],
            (own_rows, *others),
        )[0]
    else:
        piece = deal(own_rows, FAR)
    pieces = [piece, swap(piece, top_bit, side_bit)]
    pieces = pieces + [swap(p, side_bit, top_bit) for p in pieces]
    side_piece, gate_here, up_here = load(pieces[1], (w_gate, w_up), LOAD_MIB)
    pieces = [piece, side_piece] + pieces[2:]
    pieces = pieces + [swap(p, 1) for p in pieces]

    all_rows = total_devices * tokens
    hidden_units = w_gate.shape[2]
    half = all_rows // 2
    kept, away = call(
        functools.partial(expert_kernel, routes.shape[1], len(pieces)),
        [shape((half, width), F32), shape((half, width), BF16)],
        (*pieces, w_router.T, gate_here, up_here, w_down),
        in_specs=[VMEM] * (len(pieces) + 3) + [HBM],
        scratch=[
            pltpu.VMEM((all_rows, width), BF16),
            pltpu.VMEM((all_rows, hidden_units), BF16),
            pltpu.VMEM((all_rows, width), F32),
            pltpu.VMEM(w_down.shape[1:], BF16),
            pltpu.SemaphoreType.DMA((16,)),
        ],
        vmem=EXPERT_MIB if all_rows <= 256 else 56,
        cost=(6 * all_rows * width * hidden_units, 6 * width * hidden_units),
    )

    got = swap(away, 1)
    kept, away = call(
        halve_kernel,
        [shape((half // 2, width), F32), shape((half // 2, width), BF16)],
        (kept, got),
    )
    got = swap(away, side_bit, top_bit)
    kept, away = call(
        halve_kernel,
        [shape((half // 4, width), F32), shape((half // 4, width), BF16)],
        (kept, got),
    )
    got = swap(away, top_bit, side_bit)
    moe_shape = [shape((tokens, width), BF16)]
    if direct:
        parts = call(
            parts_kernel, [shape((tokens, width), F32)] + moe_shape * (far_count - 1), (kept, got)
        )
        got = [swap(part, mask) for part, mask in zip(parts[1:], masks[1:])]
        moe_out = call(add_kernel, moe_shape, (parts[0], *got))[0]
    else:
        parts = call(split_kernel, [shape((far_count, tokens, width), BF16)], (kept, got))[0]
        moe_out = call(sum_kernel, moe_shape, (deal(parts, FAR),))[0]
    return (attn_out, moe_out)


def solution(mesh):
    dp_count, expert_count = mesh.shape["dp"], mesh.shape["expert"]
    finer = Mesh(mesh.devices.reshape(2, dp_count // 2, expert_count // 4, 2, 2), ROWS)
    return jax.shard_map(
        functools.partial(body, dp_count, expert_count),
        mesh=finer,
        in_specs=(
            P(ROWS, None, None),
            P(ROWS, None),
            P(ROWS),
            P(ROWS, None, None),
            P(ROWS, None),
            P(ROWS),
            P(ROWS, None, None, None),
            P(ROWS, None, None, None),
            P(ROWS, None, None),
            P(ROWS, None, None),
            P(EXPERT, None, None),
            P(EXPERT, None),
            P(ROWS, None),
            P(),
            P(),
            P(ROWS, None),
            P(EXPERT, None, DP),
            P(EXPERT, None, DP),
            P(EXPERT, DP, None),
        ),
        out_specs=(P(ROWS, None), P(ROWS, None)),
        check_vma=False,
    )
```

```python
import functools

import jax
import jax.numpy as jnp
from jax import lax
from jax.experimental import pallas as pl
from jax.experimental.pallas import tpu as pltpu
from jax.sharding import Mesh, PartitionSpec as P

SCORE_SCALE = 0.07216878364870322
ROUTE_SCALE = 2.5
NORM_EPS = 1e-06
LOW = -1e30
LANES = 128
MIB = 1 << 20
BF16 = jnp.bfloat16
F32 = jnp.float32
VMEM = pl.BlockSpec(memory_space=pltpu.VMEM)
SMEM = pl.BlockSpec(memory_space=pltpu.SMEM)
ANY = pl.BlockSpec(memory_space=pl.ANY)
HBM = pl.BlockSpec(memory_space=pltpu.HBM)
DP = ("top", "low")
EXPERT = ("far", "side", "core")
ROWS = DP + EXPERT
FAR = ("low", "far")
CHIP = ("far", "side")
LOAD_MIB = 36
EXPERT_MIB = 36


def dot_nt(a, b):
    return lax.dot_general(a, b, (((1,), (1,)), ((), ())), preferred_element_type=F32)


def dot_tn(a, b):
    return lax.dot_general(a, b, (((0,), (0,)), ((), ())), preferred_element_type=F32)


def dot_nn(a, b):
    return jnp.dot(a, b, preferred_element_type=F32)


def call(kernel, outs, operands, in_specs=None, out_specs=None, scratch=(), vmem=16, cost=None):
    flops, moved = cost or (0, 0)
    return pl.pallas_call(
        kernel,
        out_shape=outs,
        in_specs=in_specs or [VMEM] * len(operands),
        out_specs=out_specs or [VMEM] * len(outs),
        scratch_shapes=list(scratch),
        compiler_params=pltpu.CompilerParams(vmem_limit_bytes=vmem * MIB),
        cost_estimate=pl.CostEstimate(flops=flops, bytes_accessed=moved, transcendentals=0),
    )(*operands)


def shape(dims, dtype):
    return jax.ShapeDtypeStruct(dims, dtype)


def iota(dims, axis):
    return lax.broadcasted_iota(jnp.int32, dims, axis)


def fetch(copies):
    for copy in copies:
        copy.start()
    return copies


def pick_kernel(partners, moves, move_hbm, scale_hbm, lat, rope_hbm, *rest):
    lat_outs, rope_outs = rest[:partners], rest[partners : 2 * partners]
    scale_out, move, rope, scale_ref, wide_scale, lat_sems, sems = rest[2 * partners :]
    slots, width = rope.shape
    half = width // 2
    me = lax.axis_index(DP)
    get_move, get_scale, get_rope = fetch(
        [
            pltpu.make_async_copy(move_hbm, move, sems.at[0]),
            pltpu.make_async_copy(scale_hbm, scale_ref, sems.at[1]),
            pltpu.make_async_copy(rope_hbm, rope, sems.at[2]),
        ]
    )
    get_move.wait()
    copies = []
    for k in range(partners):
        for m in range(moves):
            copies.append(
                pltpu.make_async_copy(
                    lat.at[move[0, me ^ (k + 1), m]], lat_outs[k].at[m], lat_sems.at[k, m]
                )
            )
    fetch(copies)
    get_scale.wait()
    wide_scale[...] = scale_ref[...].astype(F32)
    (put_scale,) = fetch([pltpu.make_async_copy(wide_scale, scale_out, sems.at[3])])
    put_scale.wait()
    get_rope.wait()
    row = iota((2 * moves, 1), 0)
    column = iota((2 * moves, slots), 1)
    for k in range(partners):
        target = jnp.zeros((2 * moves, 1), jnp.int32)
        factor = jnp.zeros((2 * moves, 1), F32)
        for m in range(moves):
            page = move[0, me ^ (k + 1), m]
            target = jnp.where(row // 2 == m, page, target)
            factor = jnp.where(row // 2 == m, scale_out[page], factor)
        hit = column == target
        even = row % 2 == 0
        first = jnp.where(hit & even, 1.0, 0.0).astype(BF16)
        second = jnp.where(hit & (~even), 1.0, 0.0).astype(BF16)
        both = dot_nn(first, rope[:, :half]) + dot_nn(second, rope[:, half:])
        rope_outs[k][:, :half] = both.astype(BF16)
        rope_outs[k][:, half:] = jnp.broadcast_to(factor, (2 * moves, LANES)).astype(BF16)
    for copy in copies:
        copy.wait()


def spread(scores, start, count, stride, part):
    for b in range(scores.shape[0]):
        scores.at[b][pl.ds(start, count, stride=stride), :] = part[:, b * LANES : (b + 1) * LANES]


def read(scores, span):
    parts = [scores[b, span, :] for b in range(scores.shape[0])]
    return parts[0] if len(parts) == 1 else jnp.concatenate(parts, axis=1)


def write(scores, span, part):
    for b in range(scores.shape[0]):
        scores[b, span, :] = part[:, b * LANES : (b + 1) * LANES]


GROUP = 8


def local_kernel(
    sizes,
    partners,
    scale_hbm,
    table_hbm,
    lengths_hbm,
    move_hbm,
    lat_hbm,
    rope_hbm,
    q_hbm,
    turn_hbm,
    new_lat_hbm,
    new_rope_hbm,
    out,
    scale,
    qrel_out,
    q2_out,
    table,
    lengths,
    move,
    lat,
    rope,
    q_lat,
    q_rope,
    new_lat,
    new_rope,
    scores,
    limits,
    new_keys,
    new_turns,
    sems,
    lat_sems,
):
    heads, per_device, rollouts, following, view = sizes
    slots, page_len, latent = lat.shape
    rows = rollouts * following * heads
    rope_dim = q_rope.shape[3]
    moves = move.shape[2]
    me = lax.axis_index(DP)
    pairs = (
        (table_hbm, table),
        (lengths_hbm, lengths),
        (move_hbm, move),
        (scale_hbm, scale),
        (rope_hbm, rope),
        (turn_hbm, q_rope),
        (q_hbm, q_lat),
        (new_lat_hbm, new_lat),
        (new_rope_hbm, new_rope),
    )
    small = fetch(
        [pltpu.make_async_copy(src, dst, sems.at[i]) for i, (src, dst) in enumerate(pairs)]
    )
    chunks = fetch(
        [
            pltpu.make_async_copy(
                lat_hbm.at[pl.ds(at, GROUP)], lat.at[pl.ds(at, GROUP)], lat_sems.at[at // GROUP]
            )
            for at in range(0, slots, GROUP)
        ]
    )
    place = iota((rows, rows), 0)
    rollout = (place // following) % rollouts
    token = place % following
    head = place // (following * rollouts)
    source = (rollout * following + token) * heads + head
    order = jnp.where(iota((rows, rows), 1) == source, 1.0, 0.0).astype(BF16)
    at = iota((rope_dim, 2 * rope_dim), 1)
    frm = iota((rope_dim, 2 * rope_dim), 0)
    for copy in small:
        copy.wait()
    for slot in range(rollouts * view):
        limits[slot] = 0
    for r in range(rollouts):
        for a in range(table.shape[1]):
            live = jnp.clip(lengths[r] - a * page_len, 0, page_len)
            limits[r * view + table[r, a]] = live
    q_turn = dot_nn(order, q_rope[...].reshape(rows, rope_dim)).astype(BF16)
    q2_out[:rows, :] = dot_nn(q_turn, jnp.where(at == frm, 1.0, 0.0).astype(BF16)).astype(BF16)
    q2_out[rows:, :] = dot_nn(
        q_turn, jnp.where(at == frm + rope_dim, 1.0, 0.0).astype(BF16)
    ).astype(BF16)
    qrel_out[...] = dot_nn(order, q_lat[...].reshape(rows, latent)).astype(BF16)
    twos = page_len // 2
    wide = 2 * rope_dim
    stacked = jnp.concatenate([rope[:, c * wide : (c + 1) * wide] for c in range(twos)], axis=0)
    turned = dot_nt(stacked, q2_out[...])
    for c in range(twos):
        part = turned[c * slots : (c + 1) * slots]
        spread(scores, 2 * c, slots, page_len, part[:, :rows])
        spread(scores, 2 * c + 1, slots, page_len, part[:, rows:])

    lane_rollout = (iota((1, rows), 1) // following) % rollouts
    lane_token = iota((1, rows), 1) % following
    position = iota((page_len, rows), 0)

    def limit_row(slot):
        row = jnp.full(lane_rollout.shape, limits[slot], jnp.int32)
        for r in range(1, rollouts):
            row = jnp.where(lane_rollout == r, limits[r * view + slot], row)
        return row

    for k in range(partners):
        for m in range(moves):
            at = 2 * rows + 2 + k * moves + m
            limit = limit_row(slots + (me ^ (k + 1)) * moves + m)
            out[at : at + 1, :rows] = limit.astype(F32)
    queries = qrel_out[...]
    fresh_rows = rollouts * following
    new_keys[...] = jnp.zeros(new_keys.shape, F32)
    new_turns[...] = jnp.zeros(new_turns.shape, F32)
    for r in range(rollouts):
        span = slice(r * following, (r + 1) * following)
        new_keys[span, :] = new_lat[r].astype(F32)
        new_turns[span, :rope_dim] = new_rope[r].astype(F32)
    fresh_keys = new_keys[...].astype(BF16)
    new_part = dot_nt(fresh_keys, queries) + dot_nt(
        new_turns[...].astype(BF16), q2_out[:rows, :]
    )
    new_row = iota(new_part.shape, 0)
    seen = (new_row // following == lane_rollout) & (new_row % following <= lane_token)
    new_part = jnp.where(seen & (new_row < fresh_rows), new_part * SCORE_SCALE, LOW)

    best = jnp.full((page_len, rows), LOW, F32)
    for first in range(0, slots, GROUP):
        chunks[first // GROUP].wait()
        keys = lat[first : first + GROUP].reshape(GROUP * page_len, latent)
        fresh = dot_nt(keys, queries)
        for g in range(GROUP):
            page = first + g
            span = pl.ds(page * page_len, page_len)
            part = fresh[g * page_len : (g + 1) * page_len] + read(scores, span)
            part = part * (scale[page] * SCORE_SCALE)
            write(scores, span, part)
            best = jnp.maximum(best, jnp.where(position < limit_row(page), part, LOW))
    for m in range(moves):
        page = move[0, me, m]
        part = read(scores, pl.ds(pl.multiple_of(page * page_len, page_len), page_len))
        live = position < limit_row(slots + me * moves + m)
        best = jnp.maximum(best, jnp.where(live, part, LOW))
    peak = jnp.max(best, axis=0, keepdims=True)
    peak = jnp.maximum(peak, jnp.max(new_part, axis=0, keepdims=True))

    def weigh(part, slot, factor, total):
        grown = jnp.where(position < limit_row(slot), jnp.exp(part - peak), 0.0)
        return (grown * factor).astype(BF16), total + grown

    new_exp = jnp.exp(new_part - peak)
    total = jnp.zeros((page_len, rows), F32)
    acc = dot_tn(new_exp.astype(BF16), fresh_keys)
    for first in range(0, slots, GROUP):
        weights = []
        for g in range(GROUP):
            page = first + g
            part = read(scores, pl.ds(page * page_len, page_len))
            weight, total = weigh(part, page, scale[page], total)
            weights.append(weight)
        keys = lat[first : first + GROUP].reshape(GROUP * page_len, latent)
        acc = acc + dot_tn(jnp.concatenate(weights, axis=0), keys)
    weights, keys = [], []
    for m in range(moves):
        page = move[0, me, m]
        part = read(scores, pl.ds(pl.multiple_of(page * page_len, page_len), page_len))
        weight, total = weigh(part, slots + me * moves + m, scale[page], total)
        weights.append(weight)
        keys.append(lat[page])
    acc = acc + dot_tn(jnp.concatenate(weights, axis=0), jnp.concatenate(keys, axis=0))
    whole = jnp.sum(total, axis=0, keepdims=True) + jnp.sum(new_exp, axis=0, keepdims=True)
    out[:rows, :latent] = acc
    out[rows : 2 * rows, :latent] = qrel_out[...].astype(F32)
    out[2 * rows : 2 * rows + 1, :rows] = peak
    out[2 * rows + 1 : 2 * rows + 2, :rows] = whole
    out[: 2 * rows, latent:] = q2_out[...].astype(F32)


def merge_kernel(partners, *refs):
    got_lat, got_rope = refs[:partners], refs[partners : 2 * partners]
    local, out, scores = refs[2 * partners :]
    moves, page_len, latent = got_lat[0].shape
    rows = out.shape[0] * out.shape[1]
    qrel = local[rows : 2 * rows, :latent].astype(BF16)
    q2 = local[: 2 * rows, latent:].astype(BF16)
    wide = q2.shape[1]
    position = iota((page_len, rows), 0).astype(F32)
    best = jnp.full((page_len, rows), LOW, F32)
    half_lanes = got_rope[0].shape[1] - LANES
    pieces = half_lanes // wide
    span = moves * page_len
    factors = []
    for k in range(partners):
        turns = got_rope[k]
        stacked = jnp.concatenate(
            [turns[:, c * wide : (c + 1) * wide].astype(F32) for c in range(pieces)], axis=0
        ).astype(BF16)
        turned = dot_nt(stacked, q2)
        base = k * span
        for c in range(pieces):
            part = turned[c * 2 * moves : (c + 1) * 2 * moves]
            spread(scores, base + 2 * c, 2 * moves, page_len // 2, part[:, :rows])
            spread(scores, base + 2 * c + 1, 2 * moves, page_len // 2, part[:, rows:])
        fresh = dot_nt(got_lat[k][...].reshape(span, latent), qrel)
        marks = turns[:, half_lanes:].astype(F32)
        for m in range(moves):
            factor = marks[2 * m : 2 * m + 1, :1]
            factors.append(factor)
            where_at = pl.ds(base + m * page_len, page_len)
            part = fresh[m * page_len : (m + 1) * page_len] + read(scores, where_at)
            part = part * (factor * SCORE_SCALE)
            at = 2 * rows + 2 + k * moves + m
            part = jnp.where(position < local[at : at + 1, :rows], part, LOW)
            write(scores, where_at, part)
            best = jnp.maximum(best, part)
    peak_local = local[2 * rows : 2 * rows + 1, :rows]
    peak = jnp.maximum(jnp.max(best, axis=0, keepdims=True), peak_local)
    shrink = jnp.exp(peak_local - peak)
    acc = jnp.zeros((rows, latent), F32)
    grown_sum = jnp.zeros((page_len, rows), F32)
    for k in range(partners):
        weights = []
        for m in range(moves):
            part = read(scores, pl.ds(k * span + m * page_len, page_len))
            grown = jnp.exp(part - peak)
            grown_sum = grown_sum + grown
            weights.append((grown * factors[k * moves + m]).astype(BF16))
        acc = acc + dot_tn(
            jnp.concatenate(weights, axis=0), got_lat[k][...].reshape(span, latent)
        )
    total = local[2 * rows + 1 : 2 * rows + 2, :rows] * shrink + jnp.sum(grown_sum, axis=0, keepdims=True)

    def upright(row):
        return jnp.transpose(jnp.broadcast_to(row, (LANES, rows)))[:, :1]

    result = (local[:rows, :latent] * upright(shrink) + acc) / upright(total)
    out[...] = result.reshape(out.shape).astype(BF16)


def project_kernel(tokens, blocks, w_uv, other_uv, w_out, other_out, out):
    chips = blocks.shape[0]
    per_device = w_uv.shape[0]
    core = lax.axis_index("core")
    stacked = blocks[...].astype(F32).reshape(-1, blocks.shape[2]).astype(BF16)
    rows = stacked.shape[0]
    row_head = (iota((rows, 1), 0) // tokens) % (2 * per_device)
    values = []
    for first, uv in ((core * per_device, w_uv), ((1 - core) * per_device, other_uv)):
        for head in range(per_device):
            part = dot_nn(stacked, uv[head])
            values.append(jnp.where(row_head == first + head, part, 0.0).astype(BF16))
    values = jnp.concatenate(values, axis=1)
    out_row = iota((chips * tokens, rows), 0)
    in_row = iota((chips * tokens, rows), 1)
    same_chip = in_row // (tokens * 2 * per_device) == out_row // tokens
    same = same_chip & (in_row % tokens == out_row % tokens)
    joined = dot_nn(jnp.where(same, 1.0, 0.0).astype(BF16), values).astype(BF16)
    depth, width = w_out.shape
    step = 512 if width % 512 == 0 else width
    for at in range(0, width, step):
        part = dot_nn(joined[:, :depth], w_out[:, at : at + step])
        part = part + dot_nn(joined[:, depth:], other_out[:, at : at + step])
        out[:, :, at : at + step] = part.reshape(chips, tokens, step).astype(BF16)


def split_kernel(kept, got, out):
    total = kept[...] + got[...].astype(F32)
    out[...] = total.reshape(out.shape).astype(BF16)


def norm_kernel(got, residual, gain, routes, attn_out, out):
    total = jnp.sum(got[...].astype(F32), axis=0)
    attn_out[...] = total.astype(BF16)
    hidden = (residual[...].astype(F32) + total).astype(BF16).astype(F32)
    width = hidden.shape[1]
    power = jnp.sum(hidden * hidden, axis=1, keepdims=True) / width
    normed = (hidden * lax.rsqrt(power + NORM_EPS) * gain[...].reshape(1, width)).astype(BF16)
    named = routes[...].astype(F32).astype(BF16)
    for copy in range(out.shape[0]):
        out[copy, :, :width] = normed
        out[copy, :, width:] = jnp.zeros((hidden.shape[0], LANES), BF16)
        out[copy, :, width : width + routes.shape[1]] = named


def stack_kernel(*refs):
    for k, ref in enumerate(refs[:-1]):
        refs[-1][k] = ref[0]


def parts_kernel(kept, got, *outs):
    total = kept[...] + got[...].astype(F32)
    rows = outs[0].shape[0]
    for k, out in enumerate(outs):
        out[...] = total[k * rows : (k + 1) * rows].astype(out.dtype)


def add_kernel(*refs):
    total = refs[0][...]
    for ref in refs[1:-1]:
        total = total + ref[...].astype(F32)
    refs[-1][...] = total.astype(BF16)


def load_kernel(count, passed, *refs):
    sources, passed_out, outs, sems = refs[:count], refs[count], refs[count + 1 : -1], refs[-1]
    split = sems.shape[1]
    copies = []
    for k, (source, out) in enumerate(zip(sources, outs)):
        step = out.shape[0] // split
        for i in range(split):
            span = pl.ds(i * step, step)
            copies.append(
                pltpu.make_async_copy(source.at[0, span], out.at[span], sems.at[k, i])
            )
    fetch(copies)
    passed_out[...] = passed[...]
    for copy in copies:
        copy.wait()


def expert_kernel(top, count, *refs):
    pieces = refs[:count]
    w_router, w_gate, w_up, down_hbm = refs[count : count + 4]
    kept, away, rows_ref, hidden_ref, w_down, sems = refs[count + 4 :]
    expert = lax.axis_index(EXPERT)
    width, units = w_gate.shape
    in_step = 256 if units % 256 == 0 else units
    out_step = 512 if width % 512 == 0 else width
    down_copies = fetch(
        [
            pltpu.make_async_copy(
                down_hbm.at[0, pl.ds(at, in_step)], w_down.at[pl.ds(at, in_step)], sems.at[i]
            )
            for i, at in enumerate(range(0, units, in_step))
        ]
    )
    piece_rows = rows_ref.shape[0] // count
    named = []
    for k, piece in enumerate(pieces):
        whole = piece[...].astype(F32).reshape(piece_rows, -1)
        rows_ref[k * piece_rows : (k + 1) * piece_rows, :] = whole[:, :width].astype(BF16)
        named.append(whole[:, width:])
    named = jnp.concatenate(named, axis=0)
    rows = rows_ref[...]
    logits = dot_nt(rows, w_router[...])
    experts = iota(logits.shape, 1)
    chosen = jnp.zeros(logits.shape, F32)
    for k in range(top):
        route = named[:, k : k + 1].astype(jnp.int32)
        chosen = chosen + jnp.where(route == experts, 1.0, 0.0)
    sig = jax.nn.sigmoid(logits) * chosen
    mine = jnp.sum(jnp.where(experts == expert, sig, 0.0), axis=1, keepdims=True)
    gates = ROUTE_SCALE * mine / jnp.sum(sig, axis=1, keepdims=True)
    for at in range(0, units, in_step):
        gate = dot_nn(rows, w_gate[:, at : at + in_step])
        up = dot_nn(rows, w_up[:, at : at + in_step])
        hidden_ref[:, at : at + in_step] = (gate / (1.0 + jnp.exp(-gate)) * up).astype(BF16)
    half = rows_ref.shape[0] // 2
    for copy in down_copies:
        copy.wait()
    hidden = hidden_ref[...]
    for at in range(0, width, out_step):
        part = dot_nn(hidden, w_down[:, at : at + out_step]) * gates
        kept[:, at : at + out_step] = part[:half]
        away[:, at : at + out_step] = part[half:].astype(BF16)


def halve_kernel(kept, got, keep, away):
    total = kept[...] + got[...].astype(F32)
    half = total.shape[0] // 2
    keep[...] = total[:half]
    away[...] = total[half:].astype(BF16)


def sum_kernel(got, out):
    out[...] = jnp.sum(got[...].astype(F32), axis=0).astype(BF16)


def body(dp_count, expert_count, *arrays):
    (
        cache_lat,
        cache_rope,
        page_scale,
        move_list,
        page_table,
        lengths,
        q_lat,
        q_rope,
        new_lat,
        new_rope,
        w_uv,
        w_out,
        residual,
        norm_gain,
        w_router,
        routes,
        w_gate,
        w_up,
        w_down,
    ) = arrays
    total_devices = dp_count * expert_count
    top_bit = total_devices // 2
    side_bit = 2

    def swap(x, mask, mask_odd=None):
        pairs = []
        for i in range(total_devices):
            other = mask if mask_odd is None or i % 2 == 0 else mask_odd
            pairs.append((i, i ^ other))
        return lax.ppermute(x, ROWS, pairs)

    def deal(x, names):
        return lax.all_to_all(x, names, split_axis=0, concat_axis=0, tiled=True)

    slots, page_len, latent = cache_lat.shape
    moves = move_list.shape[2]
    rollouts, following, heads, rope_dim = q_rope.shape
    view = slots + dp_count * moves
    per_device = heads // expert_count
    tokens = rollouts * following
    width = residual.shape[1]
    partners = dp_count - 1
    rows = tokens * heads
    sizes = (heads, per_device, rollouts, following, view)
    chips = expert_count // 2
    picked = call(
        functools.partial(pick_kernel, partners, moves),
        [shape((moves, page_len, latent), BF16)] * partners
        + [shape((2 * moves, cache_rope.shape[1] // 2 + LANES), BF16)] * partners
        + [shape((slots,), F32)],
        (move_list, page_scale, cache_lat, cache_rope),
        in_specs=[HBM] * 4,
        out_specs=[VMEM] * (2 * partners) + [SMEM],
        scratch=[
            pltpu.SMEM(move_list.shape, jnp.int32),
            pltpu.VMEM(cache_rope.shape, BF16),
            pltpu.VMEM(page_scale.shape, BF16),
            pltpu.VMEM((slots,), F32),
            pltpu.SemaphoreType.DMA((partners, moves)),
            pltpu.SemaphoreType.DMA((4,)),
        ],
        vmem=60,
    )
    got_lat = [swap(picked[k], (k + 1) * expert_count) for k in range(partners)]
    got_rope = [swap(picked[partners + k], (k + 1) * expert_count) for k in range(partners)]

    extra = -(-(2 + partners * moves) // 8) * 8
    local = call(
        functools.partial(local_kernel, sizes, partners),
        [shape((2 * rows + extra, latent + 2 * rope_dim), F32)],
        (
            picked[-1],
            page_table,
            lengths,
            move_list,
            cache_lat,
            cache_rope,
            q_lat,
            q_rope,
            new_lat,
            new_rope,
        ),
        in_specs=[HBM] * 10,
        scratch=[
            pltpu.SMEM((slots,), F32),
            pltpu.VMEM((rows, latent), BF16),
            pltpu.VMEM((2 * rows, 2 * rope_dim), BF16),
            pltpu.SMEM(page_table.shape, jnp.int32),
            pltpu.SMEM(lengths.shape, jnp.int32),
            pltpu.SMEM(move_list.shape, jnp.int32),
            pltpu.VMEM(cache_lat.shape, BF16),
            pltpu.VMEM(cache_rope.shape, BF16),
            pltpu.VMEM(q_lat.shape, BF16),
            pltpu.VMEM(q_rope.shape, BF16),
            pltpu.VMEM(new_lat.shape, BF16),
            pltpu.VMEM(new_rope.shape, BF16),
            pltpu.VMEM((rows // LANES, slots * page_len, LANES), F32),
            pltpu.SMEM((rollouts * view,), jnp.int32),
            pltpu.VMEM((16, latent), F32),
            pltpu.VMEM((16, 2 * rope_dim), F32),
            pltpu.SemaphoreType.DMA((9,)),
            pltpu.SemaphoreType.DMA((slots // GROUP,)),
        ],
        vmem=60,
        cost=(2 * slots * page_len * rows * (2 * latent + 2 * rope_dim), 4 * MIB),
    )
    blocks = call(
        functools.partial(merge_kernel, partners),
        [shape((chips, 2 * tokens * per_device, latent), BF16)],
        (*got_lat, *got_rope, *local),
        scratch=[pltpu.VMEM((rows // LANES, partners * moves * page_len, LANES), F32)],
        cost=(2 * moves * page_len * rows * 2 * latent, MIB),
    )[0]

    away_uv, away_out, blocks = lax.optimization_barrier((w_uv, w_out, blocks))
    other_uv, other_out = swap(away_uv, 1), swap(away_out, 1)
    blocks = deal(blocks, CHIP)

    parts = call(
        functools.partial(project_kernel, tokens),
        [shape((chips, tokens, width), BF16)],
        (blocks, w_uv, other_uv, w_out, other_out),
        cost=(4 * chips * tokens * width * w_out.shape[0], 8 * MIB),
    )[0]
    parts = deal(parts, CHIP)
    far_count = total_devices // 8
    masks = [2 * side_bit * k for k in range(far_count)]
    direct = far_count <= 4
    attn_out, own_rows = call(
        norm_kernel,
        [
            shape((tokens, width), BF16),
            shape((1 if direct else far_count, tokens, width + LANES), BF16),
        ],
        (parts, residual, norm_gain, routes),
    )

    def load(passed, sources, vmem):
        return call(
            functools.partial(load_kernel, len(sources)),
            [shape(passed.shape, BF16)] + [shape(w.shape[1:], BF16) for w in sources],
            (passed, *sources),
            in_specs=[VMEM] + [HBM] * len(sources),
            scratch=[pltpu.SemaphoreType.DMA((len(sources), 8))],
            vmem=vmem,
            cost=(0, 2 * sum(w.size for w in sources)),
        )

    if direct:
        others = [swap(own_rows, mask) for mask in masks[1:]]
        piece = call(
            stack_kernel,
            [shape((far_count, tokens, width + LANES), BF16)],
            (own_rows, *others),
        )[0]
    else:
        piece = deal(own_rows, FAR)
    pieces = [piece, swap(piece, top_bit, side_bit)]
    pieces = pieces + [swap(p, side_bit, top_bit) for p in pieces]
    side_piece, gate_here, up_here = load(pieces[1], (w_gate, w_up), LOAD_MIB)
    pieces = [piece, side_piece] + pieces[2:]
    pieces = pieces + [swap(p, 1) for p in pieces]

    all_rows = total_devices * tokens
    hidden_units = w_gate.shape[2]
    half = all_rows // 2
    kept, away = call(
        functools.partial(expert_kernel, routes.shape[1], len(pieces)),
        [shape((half, width), F32), shape((half, width), BF16)],
        (*pieces, w_router.T, gate_here, up_here, w_down),
        in_specs=[VMEM] * (len(pieces) + 3) + [HBM],
        scratch=[
            pltpu.VMEM((all_rows, width), BF16),
            pltpu.VMEM((all_rows, hidden_units), BF16),
            pltpu.VMEM(w_down.shape[1:], BF16),
            pltpu.SemaphoreType.DMA((16,)),
        ],
        vmem=EXPERT_MIB if all_rows <= 256 else 56,
        cost=(6 * all_rows * width * hidden_units, 6 * width * hidden_units),
    )

    got = swap(away, 1)
    kept, away = call(
        halve_kernel,
        [shape((half // 2, width), F32), shape((half // 2, width), BF16)],
        (kept, got),
    )
    got = swap(away, side_bit, top_bit)
    kept, away = call(
        halve_kernel,
        [shape((half // 4, width), F32), shape((half // 4, width), BF16)],
        (kept, got),
    )
    got = swap(away, top_bit, side_bit)
    moe_shape = [shape((tokens, width), BF16)]
    if direct:
        parts = call(
            parts_kernel, [shape((tokens, width), F32)] + moe_shape * (far_count - 1), (kept, got)
        )
        got = [swap(part, mask) for part, mask in zip(parts[1:], masks[1:])]
        moe_out = call(add_kernel, moe_shape, (parts[0], *got))[0]
    else:
        parts = call(split_kernel, [shape((far_count, tokens, width), BF16)], (kept, got))[0]
        moe_out = call(sum_kernel, moe_shape, (deal(parts, FAR),))[0]
    return (attn_out, moe_out)


def solution(mesh):
    dp_count, expert_count = mesh.shape["dp"], mesh.shape["expert"]
    finer = Mesh(mesh.devices.reshape(2, dp_count // 2, expert_count // 4, 2, 2), ROWS)
    return jax.shard_map(
        functools.partial(body, dp_count, expert_count),
        mesh=finer,
        in_specs=(
            P(ROWS, None, None),
            P(ROWS, None),
            P(ROWS),
            P(ROWS, None, None),
            P(ROWS, None),
            P(ROWS),
            P(ROWS, None, None, None),
            P(ROWS, None, None, None),
            P(ROWS, None, None),
            P(ROWS, None, None),
            P(EXPERT, None, None),
            P(EXPERT, None),
            P(ROWS, None),
            P(),
            P(),
            P(ROWS, None),
            P(EXPERT, None, DP),
            P(EXPERT, None, DP),
            P(EXPERT, DP, None),
        ),
        out_specs=(P(ROWS, None), P(ROWS, None)),
        check_vma=False,
    )
```

```python
import functools

import jax
import jax.numpy as jnp
from jax import lax
from jax.experimental import pallas as pl
from jax.experimental.pallas import tpu as pltpu
from jax.sharding import Mesh, PartitionSpec as P

SCORE_SCALE = 0.07216878364870322
ROUTE_SCALE = 2.5
NORM_EPS = 1e-06
LOW = -1e30
LANES = 128
MIB = 1 << 20
BF16 = jnp.bfloat16
F32 = jnp.float32
VMEM = pl.BlockSpec(memory_space=pltpu.VMEM)
SMEM = pl.BlockSpec(memory_space=pltpu.SMEM)
ANY = pl.BlockSpec(memory_space=pl.ANY)
HBM = pl.BlockSpec(memory_space=pltpu.HBM)
DP = ("top", "low")
EXPERT = ("far", "side", "core")
ROWS = DP + EXPERT
FAR = ("low", "far")
CHIP = ("far", "side")
ROPE_ROWS = 16
LOAD_MIB = 40
SIDE_MIB = 28
EXPERT_MIB = 16


def dot_nt(a, b):
    return lax.dot_general(a, b, (((1,), (1,)), ((), ())), preferred_element_type=F32)


def dot_tn(a, b):
    return lax.dot_general(a, b, (((0,), (0,)), ((), ())), preferred_element_type=F32)


def dot_nn(a, b):
    return jnp.dot(a, b, preferred_element_type=F32)


def call(kernel, outs, operands, in_specs=None, out_specs=None, scratch=(), vmem=16, cost=None):
    flops, moved = cost or (0, 0)
    return pl.pallas_call(
        kernel,
        out_shape=outs,
        in_specs=in_specs or [VMEM] * len(operands),
        out_specs=out_specs or [VMEM] * len(outs),
        scratch_shapes=list(scratch),
        compiler_params=pltpu.CompilerParams(vmem_limit_bytes=vmem * MIB),
        cost_estimate=pl.CostEstimate(flops=flops, bytes_accessed=moved, transcendentals=0),
    )(*operands)


def shape(dims, dtype):
    return jax.ShapeDtypeStruct(dims, dtype)


def iota(dims, axis):
    return lax.broadcasted_iota(jnp.int32, dims, axis)


def fetch(copies):
    for copy in copies:
        copy.start()
    return copies


def row_copies(source, target, sems, first):
    return [
        pltpu.make_async_copy(
            source.at[pl.ds(at, ROPE_ROWS)], target.at[pl.ds(at, ROPE_ROWS)], sems.at[first + i]
        )
        for i, at in enumerate(range(0, source.shape[0], ROPE_ROWS))
    ]


def pick_kernel(partners, moves, move_hbm, scale_hbm, lat, rope_hbm, *rest):
    lat_outs, rope_outs = rest[:partners], rest[partners : 2 * partners]
    scale_out, move, rope, scale_ref, wide_scale, lat_sems, sems = rest[2 * partners :]
    slots, width = rope.shape
    half = width // 2
    me = lax.axis_index(DP)
    get_move, get_scale, *get_rope = fetch(
        [
            pltpu.make_async_copy(move_hbm, move, sems.at[0]),
            pltpu.make_async_copy(scale_hbm, scale_ref, sems.at[1]),
        ]
        + row_copies(rope_hbm, rope, sems, 3)
    )
    get_move.wait()
    copies = []
    for k in range(partners):
        for m in range(moves):
            copies.append(
                pltpu.make_async_copy(
                    lat.at[move[0, me ^ (k + 1), m]], lat_outs[k].at[m], lat_sems.at[k, m]
                )
            )
    fetch(copies)
    get_scale.wait()
    wide_scale[...] = scale_ref[...].astype(F32)
    (put_scale,) = fetch([pltpu.make_async_copy(wide_scale, scale_out, sems.at[2])])
    put_scale.wait()
    for copy in get_rope:
        copy.wait()
    row = iota((2 * moves, 1), 0)
    column = iota((2 * moves, slots), 1)
    for k in range(partners):
        target = jnp.zeros((2 * moves, 1), jnp.int32)
        factor = jnp.zeros((2 * moves, 1), F32)
        for m in range(moves):
            page = move[0, me ^ (k + 1), m]
            target = jnp.where(row // 2 == m, page, target)
            factor = jnp.where(row // 2 == m, scale_out[page], factor)
        hit = column == target
        even = row % 2 == 0
        first = jnp.where(hit & even, 1.0, 0.0).astype(BF16)
        second = jnp.where(hit & (~even), 1.0, 0.0).astype(BF16)
        both = dot_nn(first, rope[:, :half]) + dot_nn(second, rope[:, half:])
        rope_outs[k][:, :half] = both.astype(BF16)
        rope_outs[k][:, half:] = jnp.broadcast_to(factor, (2 * moves, LANES)).astype(BF16)
    for copy in copies:
        copy.wait()


def spread(scores, start, count, stride, part):
    for b in range(scores.shape[0]):
        scores.at[b][pl.ds(start, count, stride=stride), :] = part[:, b * LANES : (b + 1) * LANES]


def read(scores, span):
    parts = [scores[b, span, :] for b in range(scores.shape[0])]
    return parts[0] if len(parts) == 1 else jnp.concatenate(parts, axis=1)


def write(scores, span, part):
    for b in range(scores.shape[0]):
        scores[b, span, :] = part[:, b * LANES : (b + 1) * LANES]


GROUP = 8
HALF = 4
OUT_ROWS = 32


def local_kernel(
    sizes,
    partners,
    scale_hbm,
    table_hbm,
    lengths_hbm,
    move_hbm,
    lat_hbm,
    rope_hbm,
    q_hbm,
    turn_hbm,
    new_lat_hbm,
    new_rope_hbm,
    out_hbm,
    out,
    scale,
    qrel_out,
    q2_out,
    table,
    lengths,
    move,
    lat,
    rope,
    q_lat,
    q_rope,
    new_lat,
    new_rope,
    scores,
    limits,
    new_keys,
    new_turns,
    sems,
    lat_sems,
    out_sems,
):
    heads, per_device, rollouts, following, view = sizes
    slots, page_len, latent = lat.shape
    rows = rollouts * following * heads
    rope_dim = q_rope.shape[3]
    moves = move.shape[2]
    me = lax.axis_index(DP)
    pairs = (
        (table_hbm, table),
        (lengths_hbm, lengths),
        (move_hbm, move),
        (scale_hbm, scale),
        (turn_hbm, q_rope),
        (q_hbm, q_lat),
        (new_lat_hbm, new_lat),
        (new_rope_hbm, new_rope),
    )
    small = fetch(
        [pltpu.make_async_copy(src, dst, sems.at[i]) for i, (src, dst) in enumerate(pairs)]
        + row_copies(rope_hbm, rope, sems, len(pairs))
    )
    chunks = fetch(
        [
            pltpu.make_async_copy(
                lat_hbm.at[pl.ds(at, HALF)], lat.at[pl.ds(at, HALF)], lat_sems.at[at // HALF]
            )
            for at in range(0, slots, HALF)
        ]
    )
    place = iota((rows, rows), 0)
    rollout = (place // following) % rollouts
    token = place % following
    head = place // (following * rollouts)
    source = (rollout * following + token) * heads + head
    order = jnp.where(iota((rows, rows), 1) == source, 1.0, 0.0).astype(BF16)
    at = iota((rope_dim, 2 * rope_dim), 1)
    frm = iota((rope_dim, 2 * rope_dim), 0)
    for copy in small:
        copy.wait()
    for slot in range(rollouts * view):
        limits[slot] = 0
    for r in range(rollouts):
        for a in range(table.shape[1]):
            live = jnp.clip(lengths[r] - a * page_len, 0, page_len)
            limits[r * view + table[r, a]] = live
    q_turn = dot_nn(order, q_rope[...].reshape(rows, rope_dim)).astype(BF16)
    q2_out[:rows, :] = dot_nn(q_turn, jnp.where(at == frm, 1.0, 0.0).astype(BF16)).astype(BF16)
    q2_out[rows:, :] = dot_nn(
        q_turn, jnp.where(at == frm + rope_dim, 1.0, 0.0).astype(BF16)
    ).astype(BF16)
    qrel_out[...] = dot_nn(order, q_lat[...].reshape(rows, latent)).astype(BF16)
    twos = page_len // 2
    wide = 2 * rope_dim
    stacked = jnp.concatenate([rope[:, c * wide : (c + 1) * wide] for c in range(twos)], axis=0)
    turned = dot_nt(stacked, q2_out[...])
    for c in range(twos):
        part = turned[c * slots : (c + 1) * slots]
        spread(scores, 2 * c, slots, page_len, part[:, :rows])
        spread(scores, 2 * c + 1, slots, page_len, part[:, rows:])

    lane_rollout = (iota((1, rows), 1) // following) % rollouts
    lane_token = iota((1, rows), 1) % following
    position = iota((page_len, rows), 0)

    def limit_row(slot):
        row = jnp.full(lane_rollout.shape, limits[slot], jnp.int32)
        for r in range(1, rollouts):
            row = jnp.where(lane_rollout == r, limits[r * view + slot], row)
        return row

    for k in range(partners):
        for m in range(moves):
            at = 2 * rows + 2 + k * moves + m
            limit = limit_row(slots + (me ^ (k + 1)) * moves + m)
            out[at : at + 1, :rows] = limit.astype(F32)
    queries = qrel_out[...]
    out[rows : 2 * rows, :latent] = queries.astype(F32)
    out[: 2 * rows, latent:] = q2_out[...].astype(F32)

    def send(first, count, sem):
        return fetch(
            [pltpu.make_async_copy(out.at[pl.ds(first, count)], out_hbm.at[pl.ds(first, count)], sem)]
        )[0]

    sent = [send(rows, rows, out_sems.at[0])]
    fresh_rows = rollouts * following
    new_keys[...] = jnp.zeros(new_keys.shape, F32)
    new_turns[...] = jnp.zeros(new_turns.shape, F32)
    for r in range(rollouts):
        span = slice(r * following, (r + 1) * following)
        new_keys[span, :] = new_lat[r].astype(F32)
        new_turns[span, :rope_dim] = new_rope[r].astype(F32)
    fresh_keys = new_keys[...].astype(BF16)
    new_part = dot_nt(fresh_keys, queries) + dot_nt(
        new_turns[...].astype(BF16), q2_out[:rows, :]
    )
    new_row = iota(new_part.shape, 0)
    seen = (new_row // following == lane_rollout) & (new_row % following <= lane_token)
    new_part = jnp.where(seen & (new_row < fresh_rows), new_part * SCORE_SCALE, LOW)

    best = jnp.full((page_len, rows), LOW, F32)
    for first in range(0, slots, GROUP):
        for copy in chunks[first // HALF : (first + GROUP) // HALF]:
            copy.wait()
        keys = lat[first : first + GROUP].reshape(GROUP * page_len, latent)
        fresh = dot_nt(keys, queries)
        for g in range(GROUP):
            page = first + g
            span = pl.ds(page * page_len, page_len)
            part = fresh[g * page_len : (g + 1) * page_len] + read(scores, span)
            part = part * (scale[page] * SCORE_SCALE)
            write(scores, span, part)
            best = jnp.maximum(best, jnp.where(position < limit_row(page), part, LOW))
    for m in range(moves):
        page = move[0, me, m]
        part = read(scores, pl.ds(pl.multiple_of(page * page_len, page_len), page_len))
        live = position < limit_row(slots + me * moves + m)
        best = jnp.maximum(best, jnp.where(live, part, LOW))
    peak = jnp.max(best, axis=0, keepdims=True)
    peak = jnp.maximum(peak, jnp.max(new_part, axis=0, keepdims=True))

    def weigh(part, slot, factor, total):
        grown = jnp.where(position < limit_row(slot), jnp.exp(part - peak), 0.0)
        return (grown * factor).astype(BF16), total + grown

    new_exp = jnp.exp(new_part - peak)
    total = jnp.zeros((page_len, rows), F32)
    acc = dot_tn(new_exp.astype(BF16), fresh_keys)
    for first in range(0, slots, GROUP):
        weights = []
        for g in range(GROUP):
            page = first + g
            part = read(scores, pl.ds(page * page_len, page_len))
            weight, total = weigh(part, page, scale[page], total)
            weights.append(weight)
        keys = lat[first : first + GROUP].reshape(GROUP * page_len, latent)
        acc = acc + dot_tn(jnp.concatenate(weights, axis=0), keys)
    weights, keys = [], []
    for m in range(moves):
        page = move[0, me, m]
        part = read(scores, pl.ds(pl.multiple_of(page * page_len, page_len), page_len))
        weight, total = weigh(part, slots + me * moves + m, scale[page], total)
        weights.append(weight)
        keys.append(lat[page])
    acc = acc + dot_tn(jnp.concatenate(weights, axis=0), jnp.concatenate(keys, axis=0))
    whole = jnp.sum(total, axis=0, keepdims=True) + jnp.sum(new_exp, axis=0, keepdims=True)
    out[:rows, :latent] = acc
    out[2 * rows : 2 * rows + 1, :rows] = peak
    out[2 * rows + 1 : 2 * rows + 2, :rows] = whole
    sent.append(send(2 * rows, out.shape[0] - 2 * rows, out_sems.at[1]))
    for i in range(rows // OUT_ROWS):
        sent.append(send(i * OUT_ROWS, OUT_ROWS, out_sems.at[2 + i]))
    for copy in sent:
        copy.wait()


def merge_kernel(partners, *refs):
    got_lat, got_rope = refs[:partners], refs[partners : 2 * partners]
    local, out, scores = refs[2 * partners :]
    moves, page_len, latent = got_lat[0].shape
    rows = out.shape[0] * out.shape[1]
    qrel = local[rows : 2 * rows, :latent].astype(BF16)
    q2 = local[: 2 * rows, latent:].astype(BF16)
    wide = q2.shape[1]
    position = iota((page_len, rows), 0).astype(F32)
    best = jnp.full((page_len, rows), LOW, F32)
    half_lanes = got_rope[0].shape[1] - LANES
    pieces = half_lanes // wide
    span = moves * page_len
    factors = []
    for k in range(partners):
        turns = got_rope[k]
        stacked = jnp.concatenate(
            [turns[:, c * wide : (c + 1) * wide].astype(F32) for c in range(pieces)], axis=0
        ).astype(BF16)
        turned = dot_nt(stacked, q2)
        base = k * span
        for c in range(pieces):
            part = turned[c * 2 * moves : (c + 1) * 2 * moves]
            spread(scores, base + 2 * c, 2 * moves, page_len // 2, part[:, :rows])
            spread(scores, base + 2 * c + 1, 2 * moves, page_len // 2, part[:, rows:])
        fresh = dot_nt(got_lat[k][...].reshape(span, latent), qrel)
        marks = turns[:, half_lanes:].astype(F32)
        for m in range(moves):
            factor = marks[2 * m : 2 * m + 1, :1]
            factors.append(factor)
            where_at = pl.ds(base + m * page_len, page_len)
            part = fresh[m * page_len : (m + 1) * page_len] + read(scores, where_at)
            part = part * (factor * SCORE_SCALE)
            at = 2 * rows + 2 + k * moves + m
            part = jnp.where(position < local[at : at + 1, :rows], part, LOW)
            write(scores, where_at, part)
            best = jnp.maximum(best, part)
    peak_local = local[2 * rows : 2 * rows + 1, :rows]
    peak = jnp.maximum(jnp.max(best, axis=0, keepdims=True), peak_local)
    shrink = jnp.exp(peak_local - peak)
    acc = jnp.zeros((rows, latent), F32)
    grown_sum = jnp.zeros((page_len, rows), F32)
    for k in range(partners):
        weights = []
        for m in range(moves):
            part = read(scores, pl.ds(k * span + m * page_len, page_len))
            grown = jnp.exp(part - peak)
            grown_sum = grown_sum + grown
            weights.append((grown * factors[k * moves + m]).astype(BF16))
        acc = acc + dot_tn(
            jnp.concatenate(weights, axis=0), got_lat[k][...].reshape(span, latent)
        )
    total = local[2 * rows + 1 : 2 * rows + 2, :rows] * shrink + jnp.sum(grown_sum, axis=0, keepdims=True)

    def upright(row):
        return jnp.transpose(jnp.broadcast_to(row, (LANES, rows)))[:, :1]

    result = (local[:rows, :latent] * upright(shrink) + acc) / upright(total)
    out[...] = result.reshape(out.shape).astype(BF16)


def project_kernel(tokens, blocks, w_uv, other_uv, w_out, other_out, out):
    chips = blocks.shape[0]
    per_device = w_uv.shape[0]
    core = lax.axis_index("core")
    stacked = blocks[...].astype(F32).reshape(-1, blocks.shape[2]).astype(BF16)
    rows = stacked.shape[0]
    row_head = (iota((rows, 1), 0) // tokens) % (2 * per_device)
    values = []
    for first, uv in ((core * per_device, w_uv), ((1 - core) * per_device, other_uv)):
        for head in range(per_device):
            part = dot_nn(stacked, uv[head])
            values.append(jnp.where(row_head == first + head, part, 0.0).astype(BF16))
    values = jnp.concatenate(values, axis=1)
    out_row = iota((chips * tokens, rows), 0)
    in_row = iota((chips * tokens, rows), 1)
    same_chip = in_row // (tokens * 2 * per_device) == out_row // tokens
    same = same_chip & (in_row % tokens == out_row % tokens)
    joined = dot_nn(jnp.where(same, 1.0, 0.0).astype(BF16), values).astype(BF16)
    depth, width = w_out.shape
    step = 512 if width % 512 == 0 else width
    for at in range(0, width, step):
        part = dot_nn(joined[:, :depth], w_out[:, at : at + step])
        part = part + dot_nn(joined[:, depth:], other_out[:, at : at + step])
        out[:, :, at : at + step] = part.reshape(chips, tokens, step).astype(BF16)


def split_kernel(kept, got, out):
    total = kept[...] + got[...].astype(F32)
    out[...] = total.reshape(out.shape).astype(BF16)


def norm_kernel(got, residual, gain, routes, attn_out, out):
    total = jnp.sum(got[...].astype(F32), axis=0)
    attn_out[...] = total.astype(BF16)
    hidden = (residual[...].astype(F32) + total).astype(BF16).astype(F32)
    width = hidden.shape[1]
    power = jnp.sum(hidden * hidden, axis=1, keepdims=True) / width
    normed = (hidden * lax.rsqrt(power + NORM_EPS) * gain[...].reshape(1, width)).astype(BF16)
    named = routes[...].astype(F32).astype(BF16)
    for copy in range(out.shape[0]):
        out[copy, :, :width] = normed
        out[copy, :, width:] = jnp.zeros((hidden.shape[0], LANES), BF16)
        out[copy, :, width : width + routes.shape[1]] = named


def stack_kernel(*refs):
    for k, ref in enumerate(refs[:-1]):
        refs[-1][k] = ref[0]


def parts_kernel(kept, got, *outs):
    total = kept[...] + got[...].astype(F32)
    rows = outs[0].shape[0]
    for k, out in enumerate(outs):
        out[...] = total[k * rows : (k + 1) * rows].astype(out.dtype)


def add_kernel(*refs):
    total = refs[0][...]
    for ref in refs[1:-1]:
        total = total + ref[...].astype(F32)
    refs[-1][...] = total.astype(BF16)


def load_kernel(count, held, passed, *refs):
    sources, passed_out = refs[held : held + count], refs[held + count]
    outs, sems = refs[2 * held + count + 1 : -1], refs[-1]
    split = sems.shape[1]
    copies = []
    for k, (source, out) in enumerate(zip(sources, outs)):
        step = out.shape[0] // split
        for i in range(split):
            span = pl.ds(i * step, step)
            copies.append(
                pltpu.make_async_copy(source.at[0, span], out.at[span], sems.at[k, i])
            )
    fetch(copies)
    passed_out[...] = passed[...]
    for copy in copies:
        copy.wait()


def expert_kernel(top, count, *refs):
    pieces = refs[:count]
    w_router, w_gate, w_up, w_down = refs[count : count + 4]
    kept, away, rows_ref, hidden_ref = refs[count + 4 :]
    expert = lax.axis_index(EXPERT)
    width, units = w_gate.shape
    in_step = 256 if units % 256 == 0 else units
    out_step = 512 if width % 512 == 0 else width
    piece_rows = rows_ref.shape[0] // count
    named = []
    for k, piece in enumerate(pieces):
        whole = piece[...].astype(F32).reshape(piece_rows, -1)
        rows_ref[k * piece_rows : (k + 1) * piece_rows, :] = whole[:, :width].astype(BF16)
        named.append(whole[:, width:])
    named = jnp.concatenate(named, axis=0)
    rows = rows_ref[...]
    logits = dot_nt(rows, w_router[...])
    experts = iota(logits.shape, 1)
    chosen = jnp.zeros(logits.shape, F32)
    for k in range(top):
        route = named[:, k : k + 1].astype(jnp.int32)
        chosen = chosen + jnp.where(route == experts, 1.0, 0.0)
    sig = jax.nn.sigmoid(logits) * chosen
    mine = jnp.sum(jnp.where(experts == expert, sig, 0.0), axis=1, keepdims=True)
    gates = ROUTE_SCALE * mine / jnp.sum(sig, axis=1, keepdims=True)
    for at in range(0, units, in_step):
        gate = dot_nn(rows, w_gate[:, at : at + in_step])
        up = dot_nn(rows, w_up[:, at : at + in_step])
        hidden_ref[:, at : at + in_step] = (gate / (1.0 + jnp.exp(-gate)) * up).astype(BF16)
    half = rows_ref.shape[0] // 2
    hidden = hidden_ref[...]
    for at in range(0, width, out_step):
        part = dot_nn(hidden, w_down[:, at : at + out_step]) * gates
        kept[:, at : at + out_step] = part[:half]
        away[:, at : at + out_step] = part[half:].astype(BF16)


def halve_kernel(kept, got, keep, away):
    total = kept[...] + got[...].astype(F32)
    half = total.shape[0] // 2
    keep[...] = total[:half]
    away[...] = total[half:].astype(BF16)


def sum_kernel(got, out):
    out[...] = jnp.sum(got[...].astype(F32), axis=0).astype(BF16)


def body(dp_count, expert_count, *arrays):
    (
        cache_lat,
        cache_rope,
        page_scale,
        move_list,
        page_table,
        lengths,
        q_lat,
        q_rope,
        new_lat,
        new_rope,
        w_uv,
        w_out,
        residual,
        norm_gain,
        w_router,
        routes,
        w_gate,
        w_up,
        w_down,
    ) = arrays
    total_devices = dp_count * expert_count
    top_bit = total_devices // 2
    side_bit = 2

    def swap(x, mask, mask_odd=None):
        pairs = []
        for i in range(total_devices):
            other = mask if mask_odd is None or i % 2 == 0 else mask_odd
            pairs.append((i, i ^ other))
        return lax.ppermute(x, ROWS, pairs)

    def deal(x, names):
        return lax.all_to_all(x, names, split_axis=0, concat_axis=0, tiled=True)

    slots, page_len, latent = cache_lat.shape
    moves = move_list.shape[2]
    rollouts, following, heads, rope_dim = q_rope.shape
    view = slots + dp_count * moves
    per_device = heads // expert_count
    tokens = rollouts * following
    width = residual.shape[1]
    partners = dp_count - 1
    rows = tokens * heads
    sizes = (heads, per_device, rollouts, following, view)
    chips = expert_count // 2
    picked = call(
        functools.partial(pick_kernel, partners, moves),
        [shape((moves, page_len, latent), BF16)] * partners
        + [shape((2 * moves, cache_rope.shape[1] // 2 + LANES), BF16)] * partners
        + [shape((slots,), F32)],
        (move_list, page_scale, cache_lat, cache_rope),
        in_specs=[HBM] * 4,
        out_specs=[VMEM] * (2 * partners) + [SMEM],
        scratch=[
            pltpu.SMEM(move_list.shape, jnp.int32),
            pltpu.VMEM(cache_rope.shape, BF16),
            pltpu.VMEM(page_scale.shape, BF16),
            pltpu.VMEM((slots,), F32),
            pltpu.SemaphoreType.DMA((partners, moves)),
            pltpu.SemaphoreType.DMA((3 + slots // ROPE_ROWS,)),
        ],
        vmem=60,
    )
    got_lat = [swap(picked[k], (k + 1) * expert_count) for k in range(partners)]
    got_rope = [swap(picked[partners + k], (k + 1) * expert_count) for k in range(partners)]

    extra = -(-(2 + partners * moves) // 8) * 8
    local = call(
        functools.partial(local_kernel, sizes, partners),
        [shape((2 * rows + extra, latent + 2 * rope_dim), F32)],
        (
            picked[-1],
            page_table,
            lengths,
            move_list,
            cache_lat,
            cache_rope,
            q_lat,
            q_rope,
            new_lat,
            new_rope,
        ),
        in_specs=[HBM] * 10,
        out_specs=[HBM],
        scratch=[
            pltpu.VMEM((2 * rows + extra, latent + 2 * rope_dim), F32),
            pltpu.SMEM((slots,), F32),
            pltpu.VMEM((rows, latent), BF16),
            pltpu.VMEM((2 * rows, 2 * rope_dim), BF16),
            pltpu.SMEM(page_table.shape, jnp.int32),
            pltpu.SMEM(lengths.shape, jnp.int32),
            pltpu.SMEM(move_list.shape, jnp.int32),
            pltpu.VMEM(cache_lat.shape, BF16),
            pltpu.VMEM(cache_rope.shape, BF16),
            pltpu.VMEM(q_lat.shape, BF16),
            pltpu.VMEM(q_rope.shape, BF16),
            pltpu.VMEM(new_lat.shape, BF16),
            pltpu.VMEM(new_rope.shape, BF16),
            pltpu.VMEM((rows // LANES, slots * page_len, LANES), F32),
            pltpu.SMEM((rollouts * view,), jnp.int32),
            pltpu.VMEM((16, latent), F32),
            pltpu.VMEM((16, 2 * rope_dim), F32),
            pltpu.SemaphoreType.DMA((8 + slots // ROPE_ROWS,)),
            pltpu.SemaphoreType.DMA((slots // HALF,)),
            pltpu.SemaphoreType.DMA((2 + rows // OUT_ROWS,)),
        ],
        vmem=60,
        cost=(2 * slots * page_len * rows * (2 * latent + 2 * rope_dim), 4 * MIB),
    )
    blocks = call(
        functools.partial(merge_kernel, partners),
        [shape((chips, 2 * tokens * per_device, latent), BF16)],
        (*got_lat, *got_rope, *local),
        scratch=[pltpu.VMEM((rows // LANES, partners * moves * page_len, LANES), F32)],
        cost=(2 * moves * page_len * rows * 2 * latent, MIB),
    )[0]

    away_uv, away_out, blocks = lax.optimization_barrier((w_uv, w_out, blocks))
    other_uv, other_out = swap(away_uv, 1), swap(away_out, 1)
    blocks = deal(blocks, CHIP)

    parts = call(
        functools.partial(project_kernel, tokens),
        [shape((chips, tokens, width), BF16)],
        (blocks, w_uv, other_uv, w_out, other_out),
        cost=(4 * chips * tokens * width * w_out.shape[0], 8 * MIB),
    )[0]
    parts = deal(parts, CHIP)
    far_count = total_devices // 8
    masks = [2 * side_bit * k for k in range(far_count)]
    direct = far_count <= 4
    attn_out, own_rows = call(
        norm_kernel,
        [
            shape((tokens, width), BF16),
            shape((1 if direct else far_count, tokens, width + LANES), BF16),
        ],
        (parts, residual, norm_gain, routes),
    )

    def load(passed, sources, vmem, held=()):
        outs = [shape(passed.shape, BF16)] + [shape(x.shape, BF16) for x in held]
        return pl.pallas_call(
            functools.partial(load_kernel, len(sources), len(held)),
            out_shape=outs + [shape(w.shape[1:], BF16) for w in sources],
            in_specs=[VMEM] + [ANY] * len(held) + [HBM] * len(sources),
            out_specs=[VMEM] + [ANY] * len(held) + [VMEM] * len(sources),
            input_output_aliases={1 + i: 1 + i for i in range(len(held))},
            scratch_shapes=[pltpu.SemaphoreType.DMA((len(sources), 8))],
            compiler_params=pltpu.CompilerParams(vmem_limit_bytes=vmem * MIB),
            cost_estimate=pl.CostEstimate(
                flops=0, bytes_accessed=2 * sum(w.size for w in sources), transcendentals=0
            ),
        )(passed, *held, *sources)

    if direct:
        others = [swap(own_rows, mask) for mask in masks[1:]]
        own_rows, down_here = load(own_rows, (w_down,), LOAD_MIB)
        piece = call(
            stack_kernel,
            [shape((far_count, tokens, width + LANES), BF16)],
            (own_rows, *others),
        )[0]
    else:
        own_rows, down_here = load(own_rows, (w_down,), LOAD_MIB)
        piece = deal(own_rows, FAR)
    pieces = [piece, swap(piece, top_bit, side_bit)]
    pieces = pieces + [swap(p, side_bit, top_bit) for p in pieces]
    side_piece, down_here, gate_here, up_here = load(
        pieces[1], (w_gate, w_up), SIDE_MIB, (down_here,)
    )
    pieces = [piece, side_piece] + pieces[2:]
    pieces = pieces + [swap(p, 1) for p in pieces]

    all_rows = total_devices * tokens
    hidden_units = w_gate.shape[2]
    half = all_rows // 2
    kept, away = call(
        functools.partial(expert_kernel, routes.shape[1], len(pieces)),
        [shape((half, width), F32), shape((half, width), BF16)],
        (*pieces, w_router.T, gate_here, up_here, down_here),
        scratch=[
            pltpu.VMEM((all_rows, width), BF16),
            pltpu.VMEM((all_rows, hidden_units), BF16),
        ],
        vmem=EXPERT_MIB if all_rows <= 256 else 56,
        cost=(6 * all_rows * width * hidden_units, 6 * width * hidden_units),
    )

    got = swap(away, 1)
    kept, away = call(
        halve_kernel,
        [shape((half // 2, width), F32), shape((half // 2, width), BF16)],
        (kept, got),
    )
    got = swap(away, side_bit, top_bit)
    kept, away = call(
        halve_kernel,
        [shape((half // 4, width), F32), shape((half // 4, width), BF16)],
        (kept, got),
    )
    got = swap(away, top_bit, side_bit)
    moe_shape = [shape((tokens, width), BF16)]
    if direct:
        parts = call(
            parts_kernel, [shape((tokens, width), F32)] + moe_shape * (far_count - 1), (kept, got)
        )
        got = [swap(part, mask) for part, mask in zip(parts[1:], masks[1:])]
        moe_out = call(add_kernel, moe_shape, (parts[0], *got))[0]
    else:
        parts = call(split_kernel, [shape((far_count, tokens, width), BF16)], (kept, got))[0]
        moe_out = call(sum_kernel, moe_shape, (deal(parts, FAR),))[0]
    return (attn_out, moe_out)


def solution(mesh):
    dp_count, expert_count = mesh.shape["dp"], mesh.shape["expert"]
    finer = Mesh(mesh.devices.reshape(2, dp_count // 2, expert_count // 4, 2, 2), ROWS)
    return jax.shard_map(
        functools.partial(body, dp_count, expert_count),
        mesh=finer,
        in_specs=(
            P(ROWS, None, None),
            P(ROWS, None),
            P(ROWS),
            P(ROWS, None, None),
            P(ROWS, None),
            P(ROWS),
            P(ROWS, None, None, None),
            P(ROWS, None, None, None),
            P(ROWS, None, None),
            P(ROWS, None, None),
            P(EXPERT, None, None),
            P(EXPERT, None),
            P(ROWS, None),
            P(),
            P(),
            P(ROWS, None),
            P(EXPERT, None, DP),
            P(EXPERT, None, DP),
            P(EXPERT, DP, None),
        ),
        out_specs=(P(ROWS, None), P(ROWS, None)),
        check_vma=False,
    )
```

```python
import functools

import jax
import jax.numpy as jnp
from jax import lax
from jax.experimental import pallas as pl
from jax.experimental.pallas import tpu as pltpu
from jax.sharding import Mesh, PartitionSpec as P

SCORE_SCALE = 0.07216878364870322
ROUTE_SCALE = 2.5
NORM_EPS = 1e-06
LOW = -1e30
LANES = 128
MIB = 1 << 20
BF16 = jnp.bfloat16
F32 = jnp.float32
VMEM = pl.BlockSpec(memory_space=pltpu.VMEM)
SMEM = pl.BlockSpec(memory_space=pltpu.SMEM)
ANY = pl.BlockSpec(memory_space=pl.ANY)
HBM = pl.BlockSpec(memory_space=pltpu.HBM)
DP = ("top", "low")
EXPERT = ("far", "side", "core")
ROWS = DP + EXPERT
FAR = ("low", "far")
CHIP = ("far", "side")
ROPE_ROWS = 16
UP_MIB = 40
LOAD_MIB = 34
SIDE_MIB = 28
EXPERT_MIB = 16


def dot_nt(a, b):
    return lax.dot_general(a, b, (((1,), (1,)), ((), ())), preferred_element_type=F32)


def dot_tn(a, b):
    return lax.dot_general(a, b, (((0,), (0,)), ((), ())), preferred_element_type=F32)


def dot_nn(a, b):
    return jnp.dot(a, b, preferred_element_type=F32)


def call(kernel, outs, operands, in_specs=None, out_specs=None, scratch=(), vmem=16, cost=None):
    flops, moved = cost or (0, 0)
    return pl.pallas_call(
        kernel,
        out_shape=outs,
        in_specs=in_specs or [VMEM] * len(operands),
        out_specs=out_specs or [VMEM] * len(outs),
        scratch_shapes=list(scratch),
        compiler_params=pltpu.CompilerParams(vmem_limit_bytes=vmem * MIB),
        cost_estimate=pl.CostEstimate(flops=flops, bytes_accessed=moved, transcendentals=0),
    )(*operands)


def shape(dims, dtype):
    return jax.ShapeDtypeStruct(dims, dtype)


def iota(dims, axis):
    return lax.broadcasted_iota(jnp.int32, dims, axis)


def fetch(copies):
    for copy in copies:
        copy.start()
    return copies


def row_copies(source, target, sems, first):
    return [
        pltpu.make_async_copy(
            source.at[pl.ds(at, ROPE_ROWS)], target.at[pl.ds(at, ROPE_ROWS)], sems.at[first + i]
        )
        for i, at in enumerate(range(0, source.shape[0], ROPE_ROWS))
    ]


def pick_kernel(partners, moves, move_hbm, scale_hbm, lat, rope_hbm, *rest):
    lat_outs, rope_outs = rest[:partners], rest[partners : 2 * partners]
    scale_out, move, rope, scale_ref, wide_scale, lat_sems, sems = rest[2 * partners :]
    slots, width = rope.shape
    half = width // 2
    me = lax.axis_index(DP)
    get_move, get_scale, *get_rope = fetch(
        [
            pltpu.make_async_copy(move_hbm, move, sems.at[0]),
            pltpu.make_async_copy(scale_hbm, scale_ref, sems.at[1]),
        ]
        + row_copies(rope_hbm, rope, sems, 3)
    )
    get_move.wait()
    copies = []
    for k in range(partners):
        for m in range(moves):
            copies.append(
                pltpu.make_async_copy(
                    lat.at[move[0, me ^ (k + 1), m]], lat_outs[k].at[m], lat_sems.at[k, m]
                )
            )
    fetch(copies)
    get_scale.wait()
    wide_scale[...] = scale_ref[...].astype(F32)
    (put_scale,) = fetch([pltpu.make_async_copy(wide_scale, scale_out, sems.at[2])])
    put_scale.wait()
    for copy in get_rope:
        copy.wait()
    row = iota((2 * moves, 1), 0)
    column = iota((2 * moves, slots), 1)
    for k in range(partners):
        target = jnp.zeros((2 * moves, 1), jnp.int32)
        factor = jnp.zeros((2 * moves, 1), F32)
        for m in range(moves):
            page = move[0, me ^ (k + 1), m]
            target = jnp.where(row // 2 == m, page, target)
            factor = jnp.where(row // 2 == m, scale_out[page], factor)
        hit = column == target
        even = row % 2 == 0
        first = jnp.where(hit & even, 1.0, 0.0).astype(BF16)
        second = jnp.where(hit & (~even), 1.0, 0.0).astype(BF16)
        both = dot_nn(first, rope[:, :half]) + dot_nn(second, rope[:, half:])
        rope_outs[k][:, :half] = both.astype(BF16)
        rope_outs[k][:, half:] = jnp.broadcast_to(factor, (2 * moves, LANES)).astype(BF16)
    for copy in copies:
        copy.wait()


def spread(scores, start, count, stride, part):
    for b in range(scores.shape[0]):
        scores.at[b][pl.ds(start, count, stride=stride), :] = part[:, b * LANES : (b + 1) * LANES]


def read(scores, span):
    parts = [scores[b, span, :] for b in range(scores.shape[0])]
    return parts[0] if len(parts) == 1 else jnp.concatenate(parts, axis=1)


def write(scores, span, part):
    for b in range(scores.shape[0]):
        scores[b, span, :] = part[:, b * LANES : (b + 1) * LANES]


GROUP = 8
HALF = 4
OUT_ROWS = 32


def local_kernel(
    sizes,
    partners,
    scale_hbm,
    table_hbm,
    lengths_hbm,
    move_hbm,
    lat_hbm,
    rope_hbm,
    q_hbm,
    turn_hbm,
    new_lat_hbm,
    new_rope_hbm,
    out_hbm,
    out,
    scale,
    qrel_out,
    q2_out,
    table,
    lengths,
    move,
    lat,
    rope,
    q_lat,
    q_rope,
    new_lat,
    new_rope,
    scores,
    limits,
    new_keys,
    new_turns,
    sems,
    lat_sems,
    out_sems,
):
    heads, per_device, rollouts, following, view = sizes
    slots, page_len, latent = lat.shape
    rows = rollouts * following * heads
    rope_dim = q_rope.shape[3]
    moves = move.shape[2]
    me = lax.axis_index(DP)
    pairs = (
        (table_hbm, table),
        (lengths_hbm, lengths),
        (move_hbm, move),
        (scale_hbm, scale),
        (turn_hbm, q_rope),
        (q_hbm, q_lat),
        (new_lat_hbm, new_lat),
        (new_rope_hbm, new_rope),
    )
    small = fetch(
        [pltpu.make_async_copy(src, dst, sems.at[i]) for i, (src, dst) in enumerate(pairs)]
        + row_copies(rope_hbm, rope, sems, len(pairs))
    )
    chunks = fetch(
        [
            pltpu.make_async_copy(
                lat_hbm.at[pl.ds(at, HALF)], lat.at[pl.ds(at, HALF)], lat_sems.at[at // HALF]
            )
            for at in range(0, slots, HALF)
        ]
    )
    place = iota((rows, rows), 0)
    rollout = (place // following) % rollouts
    token = place % following
    head = place // (following * rollouts)
    source = (rollout * following + token) * heads + head
    order = jnp.where(iota((rows, rows), 1) == source, 1.0, 0.0).astype(BF16)
    at = iota((rope_dim, 2 * rope_dim), 1)
    frm = iota((rope_dim, 2 * rope_dim), 0)
    for copy in small:
        copy.wait()
    for slot in range(rollouts * view):
        limits[slot] = 0
    for r in range(rollouts):
        for a in range(table.shape[1]):
            live = jnp.clip(lengths[r] - a * page_len, 0, page_len)
            limits[r * view + table[r, a]] = live
    q_turn = dot_nn(order, q_rope[...].reshape(rows, rope_dim)).astype(BF16)
    q2_out[:rows, :] = dot_nn(q_turn, jnp.where(at == frm, 1.0, 0.0).astype(BF16)).astype(BF16)
    q2_out[rows:, :] = dot_nn(
        q_turn, jnp.where(at == frm + rope_dim, 1.0, 0.0).astype(BF16)
    ).astype(BF16)
    qrel_out[...] = dot_nn(order, q_lat[...].reshape(rows, latent)).astype(BF16)
    twos = page_len // 2
    wide = 2 * rope_dim
    stacked = jnp.concatenate([rope[:, c * wide : (c + 1) * wide] for c in range(twos)], axis=0)
    turned = dot_nt(stacked, q2_out[...])
    for c in range(twos):
        part = turned[c * slots : (c + 1) * slots]
        spread(scores, 2 * c, slots, page_len, part[:, :rows])
        spread(scores, 2 * c + 1, slots, page_len, part[:, rows:])

    lane_rollout = (iota((1, rows), 1) // following) % rollouts
    lane_token = iota((1, rows), 1) % following
    position = iota((page_len, rows), 0)

    def limit_row(slot):
        row = jnp.full(lane_rollout.shape, limits[slot], jnp.int32)
        for r in range(1, rollouts):
            row = jnp.where(lane_rollout == r, limits[r * view + slot], row)
        return row

    for k in range(partners):
        for m in range(moves):
            at = 2 * rows + 2 + k * moves + m
            limit = limit_row(slots + (me ^ (k + 1)) * moves + m)
            out[at : at + 1, :rows] = limit.astype(F32)
    queries = qrel_out[...]
    out[rows : 2 * rows, :latent] = queries.astype(F32)
    out[: 2 * rows, latent:] = q2_out[...].astype(F32)

    def send(first, count, sem):
        return fetch(
            [pltpu.make_async_copy(out.at[pl.ds(first, count)], out_hbm.at[pl.ds(first, count)], sem)]
        )[0]

    sent = [send(rows, rows, out_sems.at[0])]
    fresh_rows = rollouts * following
    new_keys[...] = jnp.zeros(new_keys.shape, F32)
    new_turns[...] = jnp.zeros(new_turns.shape, F32)
    for r in range(rollouts):
        span = slice(r * following, (r + 1) * following)
        new_keys[span, :] = new_lat[r].astype(F32)
        new_turns[span, :rope_dim] = new_rope[r].astype(F32)
    fresh_keys = new_keys[...].astype(BF16)
    new_part = dot_nt(fresh_keys, queries) + dot_nt(
        new_turns[...].astype(BF16), q2_out[:rows, :]
    )
    new_row = iota(new_part.shape, 0)
    seen = (new_row // following == lane_rollout) & (new_row % following <= lane_token)
    new_part = jnp.where(seen & (new_row < fresh_rows), new_part * SCORE_SCALE, LOW)

    best = jnp.full((page_len, rows), LOW, F32)
    for first in range(0, slots, GROUP):
        for copy in chunks[first // HALF : (first + GROUP) // HALF]:
            copy.wait()
        keys = lat[first : first + GROUP].reshape(GROUP * page_len, latent)
        fresh = dot_nt(keys, queries)
        for g in range(GROUP):
            page = first + g
            span = pl.ds(page * page_len, page_len)
            part = fresh[g * page_len : (g + 1) * page_len] + read(scores, span)
            part = part * (scale[page] * SCORE_SCALE)
            write(scores, span, part)
            best = jnp.maximum(best, jnp.where(position < limit_row(page), part, LOW))
    for m in range(moves):
        page = move[0, me, m]
        part = read(scores, pl.ds(pl.multiple_of(page * page_len, page_len), page_len))
        live = position < limit_row(slots + me * moves + m)
        best = jnp.maximum(best, jnp.where(live, part, LOW))
    peak = jnp.max(best, axis=0, keepdims=True)
    peak = jnp.maximum(peak, jnp.max(new_part, axis=0, keepdims=True))

    def weigh(part, slot, factor, total):
        grown = jnp.where(position < limit_row(slot), jnp.exp(part - peak), 0.0)
        return (grown * factor).astype(BF16), total + grown

    new_exp = jnp.exp(new_part - peak)
    total = jnp.zeros((page_len, rows), F32)
    acc = dot_tn(new_exp.astype(BF16), fresh_keys)
    for first in range(0, slots, GROUP):
        weights = []
        for g in range(GROUP):
            page = first + g
            part = read(scores, pl.ds(page * page_len, page_len))
            weight, total = weigh(part, page, scale[page], total)
            weights.append(weight)
        keys = lat[first : first + GROUP].reshape(GROUP * page_len, latent)
        acc = acc + dot_tn(jnp.concatenate(weights, axis=0), keys)
    weights, keys = [], []
    for m in range(moves):
        page = move[0, me, m]
        part = read(scores, pl.ds(pl.multiple_of(page * page_len, page_len), page_len))
        weight, total = weigh(part, slots + me * moves + m, scale[page], total)
        weights.append(weight)
        keys.append(lat[page])
    acc = acc + dot_tn(jnp.concatenate(weights, axis=0), jnp.concatenate(keys, axis=0))
    whole = jnp.sum(total, axis=0, keepdims=True) + jnp.sum(new_exp, axis=0, keepdims=True)
    out[:rows, :latent] = acc
    out[2 * rows : 2 * rows + 1, :rows] = peak
    out[2 * rows + 1 : 2 * rows + 2, :rows] = whole
    sent.append(send(2 * rows, out.shape[0] - 2 * rows, out_sems.at[1]))
    for i in range(rows // OUT_ROWS):
        sent.append(send(i * OUT_ROWS, OUT_ROWS, out_sems.at[2 + i]))
    for copy in sent:
        copy.wait()


def merge_kernel(partners, *refs):
    got_lat, got_rope = refs[:partners], refs[partners : 2 * partners]
    local, out, scores = refs[2 * partners :]
    moves, page_len, latent = got_lat[0].shape
    rows = out.shape[0] * out.shape[1]
    qrel = local[rows : 2 * rows, :latent].astype(BF16)
    q2 = local[: 2 * rows, latent:].astype(BF16)
    wide = q2.shape[1]
    position = iota((page_len, rows), 0).astype(F32)
    best = jnp.full((page_len, rows), LOW, F32)
    half_lanes = got_rope[0].shape[1] - LANES
    pieces = half_lanes // wide
    span = moves * page_len
    factors = []
    for k in range(partners):
        turns = got_rope[k]
        stacked = jnp.concatenate(
            [turns[:, c * wide : (c + 1) * wide].astype(F32) for c in range(pieces)], axis=0
        ).astype(BF16)
        turned = dot_nt(stacked, q2)
        base = k * span
        for c in range(pieces):
            part = turned[c * 2 * moves : (c + 1) * 2 * moves]
            spread(scores, base + 2 * c, 2 * moves, page_len // 2, part[:, :rows])
            spread(scores, base + 2 * c + 1, 2 * moves, page_len // 2, part[:, rows:])
        fresh = dot_nt(got_lat[k][...].reshape(span, latent), qrel)
        marks = turns[:, half_lanes:].astype(F32)
        for m in range(moves):
            factor = marks[2 * m : 2 * m + 1, :1]
            factors.append(factor)
            where_at = pl.ds(base + m * page_len, page_len)
            part = fresh[m * page_len : (m + 1) * page_len] + read(scores, where_at)
            part = part * (factor * SCORE_SCALE)
            at = 2 * rows + 2 + k * moves + m
            part = jnp.where(position < local[at : at + 1, :rows], part, LOW)
            write(scores, where_at, part)
            best = jnp.maximum(best, part)
    peak_local = local[2 * rows : 2 * rows + 1, :rows]
    peak = jnp.maximum(jnp.max(best, axis=0, keepdims=True), peak_local)
    shrink = jnp.exp(peak_local - peak)
    acc = jnp.zeros((rows, latent), F32)
    grown_sum = jnp.zeros((page_len, rows), F32)
    for k in range(partners):
        weights = []
        for m in range(moves):
            part = read(scores, pl.ds(k * span + m * page_len, page_len))
            grown = jnp.exp(part - peak)
            grown_sum = grown_sum + grown
            weights.append((grown * factors[k * moves + m]).astype(BF16))
        acc = acc + dot_tn(
            jnp.concatenate(weights, axis=0), got_lat[k][...].reshape(span, latent)
        )
    total = local[2 * rows + 1 : 2 * rows + 2, :rows] * shrink + jnp.sum(grown_sum, axis=0, keepdims=True)

    def upright(row):
        return jnp.transpose(jnp.broadcast_to(row, (LANES, rows)))[:, :1]

    result = (local[:rows, :latent] * upright(shrink) + acc) / upright(total)
    out[...] = result.reshape(out.shape).astype(BF16)


def project_kernel(tokens, blocks, w_uv, other_uv, w_out, other_out, out):
    chips = blocks.shape[0]
    per_device = w_uv.shape[0]
    core = lax.axis_index("core")
    stacked = blocks[...].astype(F32).reshape(-1, blocks.shape[2]).astype(BF16)
    rows = stacked.shape[0]
    row_head = (iota((rows, 1), 0) // tokens) % (2 * per_device)
    values = []
    for first, uv in ((core * per_device, w_uv), ((1 - core) * per_device, other_uv)):
        for head in range(per_device):
            part = dot_nn(stacked, uv[head])
            values.append(jnp.where(row_head == first + head, part, 0.0).astype(BF16))
    values = jnp.concatenate(values, axis=1)
    out_row = iota((chips * tokens, rows), 0)
    in_row = iota((chips * tokens, rows), 1)
    same_chip = in_row // (tokens * 2 * per_device) == out_row // tokens
    same = same_chip & (in_row % tokens == out_row % tokens)
    joined = dot_nn(jnp.where(same, 1.0, 0.0).astype(BF16), values).astype(BF16)
    depth, width = w_out.shape
    step = 512 if width % 512 == 0 else width
    for at in range(0, width, step):
        part = dot_nn(joined[:, :depth], w_out[:, at : at + step])
        part = part + dot_nn(joined[:, depth:], other_out[:, at : at + step])
        out[:, :, at : at + step] = part.reshape(chips, tokens, step).astype(BF16)


def split_kernel(kept, got, out):
    total = kept[...] + got[...].astype(F32)
    out[...] = total.reshape(out.shape).astype(BF16)


def norm_kernel(got, residual, gain, routes, attn_out, out):
    total = jnp.sum(got[...].astype(F32), axis=0)
    attn_out[...] = total.astype(BF16)
    hidden = (residual[...].astype(F32) + total).astype(BF16).astype(F32)
    width = hidden.shape[1]
    power = jnp.sum(hidden * hidden, axis=1, keepdims=True) / width
    normed = (hidden * lax.rsqrt(power + NORM_EPS) * gain[...].reshape(1, width)).astype(BF16)
    named = routes[...].astype(F32).astype(BF16)
    for copy in range(out.shape[0]):
        out[copy, :, :width] = normed
        out[copy, :, width:] = jnp.zeros((hidden.shape[0], LANES), BF16)
        out[copy, :, width : width + routes.shape[1]] = named


def stack_kernel(*refs):
    for k, ref in enumerate(refs[:-1]):
        refs[-1][k] = ref[0]


def parts_kernel(kept, got, *outs):
    total = kept[...] + got[...].astype(F32)
    rows = outs[0].shape[0]
    for k, out in enumerate(outs):
        out[...] = total[k * rows : (k + 1) * rows].astype(out.dtype)


def add_kernel(*refs):
    total = refs[0][...]
    for ref in refs[1:-1]:
        total = total + ref[...].astype(F32)
    refs[-1][...] = total.astype(BF16)


def load_kernel(count, held, after, passed, *refs):
    sources, passed_out = refs[held : held + count], refs[held + count + after]
    outs, sems = refs[2 * held + count + after + 1 : -1], refs[-1]
    split = sems.shape[1]
    copies = []
    for k, (source, out) in enumerate(zip(sources, outs)):
        step = out.shape[0] // split
        for i in range(split):
            span = pl.ds(i * step, step)
            copies.append(
                pltpu.make_async_copy(source.at[0, span], out.at[span], sems.at[k, i])
            )
    fetch(copies)
    passed_out[...] = passed[...]
    for copy in copies:
        copy.wait()


def expert_kernel(top, count, *refs):
    pieces = refs[:count]
    w_router, w_gate, w_up, w_down = refs[count : count + 4]
    kept, away, rows_ref, hidden_ref = refs[count + 4 :]
    expert = lax.axis_index(EXPERT)
    width, units = w_gate.shape
    in_step = 256 if units % 256 == 0 else units
    out_step = 512 if width % 512 == 0 else width
    piece_rows = rows_ref.shape[0] // count
    named = []
    for k, piece in enumerate(pieces):
        whole = piece[...].astype(F32).reshape(piece_rows, -1)
        rows_ref[k * piece_rows : (k + 1) * piece_rows, :] = whole[:, :width].astype(BF16)
        named.append(whole[:, width:])
    named = jnp.concatenate(named, axis=0)
    rows = rows_ref[...]
    logits = dot_nt(rows, w_router[...])
    experts = iota(logits.shape, 1)
    chosen = jnp.zeros(logits.shape, F32)
    for k in range(top):
        route = named[:, k : k + 1].astype(jnp.int32)
        chosen = chosen + jnp.where(route == experts, 1.0, 0.0)
    sig = jax.nn.sigmoid(logits) * chosen
    mine = jnp.sum(jnp.where(experts == expert, sig, 0.0), axis=1, keepdims=True)
    gates = ROUTE_SCALE * mine / jnp.sum(sig, axis=1, keepdims=True)
    for at in range(0, units, in_step):
        gate = dot_nn(rows, w_gate[:, at : at + in_step])
        up = dot_nn(rows, w_up[:, at : at + in_step])
        hidden_ref[:, at : at + in_step] = (gate / (1.0 + jnp.exp(-gate)) * up).astype(BF16)
    half = rows_ref.shape[0] // 2
    hidden = hidden_ref[...]
    for at in range(0, width, out_step):
        part = dot_nn(hidden, w_down[:, at : at + out_step]) * gates
        kept[:, at : at + out_step] = part[:half]
        away[:, at : at + out_step] = part[half:].astype(BF16)


def halve_kernel(kept, got, keep, away):
    total = kept[...] + got[...].astype(F32)
    half = total.shape[0] // 2
    keep[...] = total[:half]
    away[...] = total[half:].astype(BF16)


def sum_kernel(got, out):
    out[...] = jnp.sum(got[...].astype(F32), axis=0).astype(BF16)


def body(dp_count, expert_count, *arrays):
    (
        cache_lat,
        cache_rope,
        page_scale,
        move_list,
        page_table,
        lengths,
        q_lat,
        q_rope,
        new_lat,
        new_rope,
        w_uv,
        w_out,
        residual,
        norm_gain,
        w_router,
        routes,
        w_gate,
        w_up,
        w_down,
    ) = arrays
    total_devices = dp_count * expert_count
    top_bit = total_devices // 2
    side_bit = 2

    def swap(x, mask, mask_odd=None):
        pairs = []
        for i in range(total_devices):
            other = mask if mask_odd is None or i % 2 == 0 else mask_odd
            pairs.append((i, i ^ other))
        return lax.ppermute(x, ROWS, pairs)

    def deal(x, names):
        return lax.all_to_all(x, names, split_axis=0, concat_axis=0, tiled=True)

    slots, page_len, latent = cache_lat.shape
    moves = move_list.shape[2]
    rollouts, following, heads, rope_dim = q_rope.shape
    view = slots + dp_count * moves
    per_device = heads // expert_count
    tokens = rollouts * following
    width = residual.shape[1]
    partners = dp_count - 1
    rows = tokens * heads
    sizes = (heads, per_device, rollouts, following, view)
    chips = expert_count // 2
    picked = call(
        functools.partial(pick_kernel, partners, moves),
        [shape((moves, page_len, latent), BF16)] * partners
        + [shape((2 * moves, cache_rope.shape[1] // 2 + LANES), BF16)] * partners
        + [shape((slots,), F32)],
        (move_list, page_scale, cache_lat, cache_rope),
        in_specs=[HBM] * 4,
        out_specs=[VMEM] * (2 * partners) + [SMEM],
        scratch=[
            pltpu.SMEM(move_list.shape, jnp.int32),
            pltpu.VMEM(cache_rope.shape, BF16),
            pltpu.VMEM(page_scale.shape, BF16),
            pltpu.VMEM((slots,), F32),
            pltpu.SemaphoreType.DMA((partners, moves)),
            pltpu.SemaphoreType.DMA((3 + slots // ROPE_ROWS,)),
        ],
        vmem=60,
    )
    got_lat = [swap(picked[k], (k + 1) * expert_count) for k in range(partners)]
    got_rope = [swap(picked[partners + k], (k + 1) * expert_count) for k in range(partners)]

    extra = -(-(2 + partners * moves) // 8) * 8
    local = call(
        functools.partial(local_kernel, sizes, partners),
        [shape((2 * rows + extra, latent + 2 * rope_dim), F32)],
        (
            picked[-1],
            page_table,
            lengths,
            move_list,
            cache_lat,
            cache_rope,
            q_lat,
            q_rope,
            new_lat,
            new_rope,
        ),
        in_specs=[HBM] * 10,
        out_specs=[HBM],
        scratch=[
            pltpu.VMEM((2 * rows + extra, latent + 2 * rope_dim), F32),
            pltpu.SMEM((slots,), F32),
            pltpu.VMEM((rows, latent), BF16),
            pltpu.VMEM((2 * rows, 2 * rope_dim), BF16),
            pltpu.SMEM(page_table.shape, jnp.int32),
            pltpu.SMEM(lengths.shape, jnp.int32),
            pltpu.SMEM(move_list.shape, jnp.int32),
            pltpu.VMEM(cache_lat.shape, BF16),
            pltpu.VMEM(cache_rope.shape, BF16),
            pltpu.VMEM(q_lat.shape, BF16),
            pltpu.VMEM(q_rope.shape, BF16),
            pltpu.VMEM(new_lat.shape, BF16),
            pltpu.VMEM(new_rope.shape, BF16),
            pltpu.VMEM((rows // LANES, slots * page_len, LANES), F32),
            pltpu.SMEM((rollouts * view,), jnp.int32),
            pltpu.VMEM((16, latent), F32),
            pltpu.VMEM((16, 2 * rope_dim), F32),
            pltpu.SemaphoreType.DMA((8 + slots // ROPE_ROWS,)),
            pltpu.SemaphoreType.DMA((slots // HALF,)),
            pltpu.SemaphoreType.DMA((2 + rows // OUT_ROWS,)),
        ],
        vmem=60,
        cost=(2 * slots * page_len * rows * (2 * latent + 2 * rope_dim), 4 * MIB),
    )
    blocks = call(
        functools.partial(merge_kernel, partners),
        [shape((chips, 2 * tokens * per_device, latent), BF16)],
        (*got_lat, *got_rope, *local),
        scratch=[pltpu.VMEM((rows // LANES, partners * moves * page_len, LANES), F32)],
        cost=(2 * moves * page_len * rows * 2 * latent, MIB),
    )[0]

    away_uv, away_out, blocks = lax.optimization_barrier((w_uv, w_out, blocks))
    other_uv, other_out = swap(away_uv, 1), swap(away_out, 1)
    def load(passed, sources, vmem, held=(), after=()):
        outs = [shape(passed.shape, BF16)] + [shape(x.shape, BF16) for x in held]
        return pl.pallas_call(
            functools.partial(load_kernel, len(sources), len(held), len(after)),
            out_shape=outs + [shape(w.shape[1:], BF16) for w in sources],
            in_specs=[VMEM] + [ANY] * len(held) + [HBM] * len(sources) + [ANY] * len(after),
            out_specs=[VMEM] + [ANY] * len(held) + [VMEM] * len(sources),
            input_output_aliases={1 + i: 1 + i for i in range(len(held))},
            scratch_shapes=[pltpu.SemaphoreType.DMA((len(sources), 8))],
            compiler_params=pltpu.CompilerParams(vmem_limit_bytes=vmem * MIB),
            cost_estimate=pl.CostEstimate(
                flops=0, bytes_accessed=2 * sum(w.size for w in sources), transcendentals=0
            ),
        )(passed, *held, *sources, *after)

    own_uv, up_here = load(w_uv, (w_up,), UP_MIB, after=(blocks,))
    blocks = deal(blocks, CHIP)

    parts = call(
        functools.partial(project_kernel, tokens),
        [shape((chips, tokens, width), BF16)],
        (blocks, own_uv, other_uv, w_out, other_out),
        cost=(4 * chips * tokens * width * w_out.shape[0], 8 * MIB),
    )[0]
    parts = deal(parts, CHIP)
    far_count = total_devices // 8
    masks = [2 * side_bit * k for k in range(far_count)]
    direct = far_count <= 4
    attn_out, own_rows = call(
        norm_kernel,
        [
            shape((tokens, width), BF16),
            shape((1 if direct else far_count, tokens, width + LANES), BF16),
        ],
        (parts, residual, norm_gain, routes),
    )

    if direct:
        others = [swap(own_rows, mask) for mask in masks[1:]]
        own_rows, up_here, down_here = load(own_rows, (w_down,), LOAD_MIB, (up_here,))
        piece = call(
            stack_kernel,
            [shape((far_count, tokens, width + LANES), BF16)],
            (own_rows, *others),
        )[0]
    else:
        own_rows, up_here, down_here = load(own_rows, (w_down,), LOAD_MIB, (up_here,))
        piece = deal(own_rows, FAR)
    pieces = [piece, swap(piece, top_bit, side_bit)]
    pieces = pieces + [swap(p, side_bit, top_bit) for p in pieces]
    side_piece, up_here, down_here, gate_here = load(
        pieces[1], (w_gate,), SIDE_MIB, (up_here, down_here)
    )
    pieces = [piece, side_piece] + pieces[2:]
    pieces = pieces + [swap(p, 1) for p in pieces]

    all_rows = total_devices * tokens
    hidden_units = w_gate.shape[2]
    half = all_rows // 2
    kept, away = call(
        functools.partial(expert_kernel, routes.shape[1], len(pieces)),
        [shape((half, width), F32), shape((half, width), BF16)],
        (*pieces, w_router.T, gate_here, up_here, down_here),
        scratch=[
            pltpu.VMEM((all_rows, width), BF16),
            pltpu.VMEM((all_rows, hidden_units), BF16),
        ],
        vmem=EXPERT_MIB if all_rows <= 256 else 56,
        cost=(6 * all_rows * width * hidden_units, 6 * width * hidden_units),
    )

    got = swap(away, 1)
    kept, away = call(
        halve_kernel,
        [shape((half // 2, width), F32), shape((half // 2, width), BF16)],
        (kept, got),
    )
    got = swap(away, side_bit, top_bit)
    kept, away = call(
        halve_kernel,
        [shape((half // 4, width), F32), shape((half // 4, width), BF16)],
        (kept, got),
    )
    got = swap(away, top_bit, side_bit)
    moe_shape = [shape((tokens, width), BF16)]
    if direct:
        parts = call(
            parts_kernel, [shape((tokens, width), F32)] + moe_shape * (far_count - 1), (kept, got)
        )
        got = [swap(part, mask) for part, mask in zip(parts[1:], masks[1:])]
        moe_out = call(add_kernel, moe_shape, (parts[0], *got))[0]
    else:
        parts = call(split_kernel, [shape((far_count, tokens, width), BF16)], (kept, got))[0]
        moe_out = call(sum_kernel, moe_shape, (deal(parts, FAR),))[0]
    return (attn_out, moe_out)


def solution(mesh):
    dp_count, expert_count = mesh.shape["dp"], mesh.shape["expert"]
    finer = Mesh(mesh.devices.reshape(2, dp_count // 2, expert_count // 4, 2, 2), ROWS)
    return jax.shard_map(
        functools.partial(body, dp_count, expert_count),
        mesh=finer,
        in_specs=(
            P(ROWS, None, None),
            P(ROWS, None),
            P(ROWS),
            P(ROWS, None, None),
            P(ROWS, None),
            P(ROWS),
            P(ROWS, None, None, None),
            P(ROWS, None, None, None),
            P(ROWS, None, None),
            P(ROWS, None, None),
            P(EXPERT, None, None),
            P(EXPERT, None),
            P(ROWS, None),
            P(),
            P(),
            P(ROWS, None),
            P(EXPERT, None, DP),
            P(EXPERT, None, DP),
            P(EXPERT, DP, None),
        ),
        out_specs=(P(ROWS, None), P(ROWS, None)),
        check_vma=False,
    )
```

```python
import functools

import jax
import jax.numpy as jnp
from jax import lax
from jax.experimental import pallas as pl
from jax.experimental.pallas import tpu as pltpu
from jax.sharding import Mesh, PartitionSpec as P

SCORE_SCALE = 0.07216878364870322
ROUTE_SCALE = 2.5
NORM_EPS = 1e-06
LOW = -1e30
LANES = 128
MIB = 1 << 20
BF16 = jnp.bfloat16
F32 = jnp.float32
VMEM = pl.BlockSpec(memory_space=pltpu.VMEM)
SMEM = pl.BlockSpec(memory_space=pltpu.SMEM)
ANY = pl.BlockSpec(memory_space=pl.ANY)
HBM = pl.BlockSpec(memory_space=pltpu.HBM)
DP = ("top", "low")
EXPERT = ("far", "side", "core")
ROWS = DP + EXPERT
FAR = ("low", "far")
CHIP = ("far", "side")
ROPE_ROWS = 16
LOAD_MIB = 41
UP_MIB = 34
SIDE_MIB = 28
EXPERT_MIB = 16


def dot_nt(a, b):
    return lax.dot_general(a, b, (((1,), (1,)), ((), ())), preferred_element_type=F32)


def dot_tn(a, b):
    return lax.dot_general(a, b, (((0,), (0,)), ((), ())), preferred_element_type=F32)


def dot_nn(a, b):
    return jnp.dot(a, b, preferred_element_type=F32)


def call(kernel, outs, operands, in_specs=None, out_specs=None, scratch=(), vmem=16, cost=None):
    flops, moved = cost or (0, 0)
    return pl.pallas_call(
        kernel,
        out_shape=outs,
        in_specs=in_specs or [VMEM] * len(operands),
        out_specs=out_specs or [VMEM] * len(outs),
        scratch_shapes=list(scratch),
        compiler_params=pltpu.CompilerParams(vmem_limit_bytes=vmem * MIB),
        cost_estimate=pl.CostEstimate(flops=flops, bytes_accessed=moved, transcendentals=0),
    )(*operands)


def shape(dims, dtype):
    return jax.ShapeDtypeStruct(dims, dtype)


def iota(dims, axis):
    return lax.broadcasted_iota(jnp.int32, dims, axis)


def fetch(copies):
    for copy in copies:
        copy.start()
    return copies


def row_copies(source, target, sems, first):
    return [
        pltpu.make_async_copy(
            source.at[pl.ds(at, ROPE_ROWS)], target.at[pl.ds(at, ROPE_ROWS)], sems.at[first + i]
        )
        for i, at in enumerate(range(0, source.shape[0], ROPE_ROWS))
    ]


def pick_kernel(partners, moves, move_hbm, scale_hbm, lat, rope_hbm, *rest):
    lat_outs, rope_outs = rest[:partners], rest[partners : 2 * partners]
    scale_out, move, rope, scale_ref, wide_scale, lat_sems, sems = rest[2 * partners :]
    slots, width = rope.shape
    half = width // 2
    me = lax.axis_index(DP)
    get_move, get_scale, *get_rope = fetch(
        [
            pltpu.make_async_copy(move_hbm, move, sems.at[0]),
            pltpu.make_async_copy(scale_hbm, scale_ref, sems.at[1]),
        ]
        + row_copies(rope_hbm, rope, sems, 3)
    )
    get_move.wait()
    copies = []
    for k in range(partners):
        for m in range(moves):
            copies.append(
                pltpu.make_async_copy(
                    lat.at[move[0, me ^ (k + 1), m]], lat_outs[k].at[m], lat_sems.at[k, m]
                )
            )
    fetch(copies)
    get_scale.wait()
    wide_scale[...] = scale_ref[...].astype(F32)
    (put_scale,) = fetch([pltpu.make_async_copy(wide_scale, scale_out, sems.at[2])])
    put_scale.wait()
    for copy in get_rope:
        copy.wait()
    row = iota((2 * moves, 1), 0)
    column = iota((2 * moves, slots), 1)
    for k in range(partners):
        target = jnp.zeros((2 * moves, 1), jnp.int32)
        factor = jnp.zeros((2 * moves, 1), F32)
        for m in range(moves):
            page = move[0, me ^ (k + 1), m]
            target = jnp.where(row // 2 == m, page, target)
            factor = jnp.where(row // 2 == m, scale_out[page], factor)
        hit = column == target
        even = row % 2 == 0
        first = jnp.where(hit & even, 1.0, 0.0).astype(BF16)
        second = jnp.where(hit & (~even), 1.0, 0.0).astype(BF16)
        both = dot_nn(first, rope[:, :half]) + dot_nn(second, rope[:, half:])
        rope_outs[k][:, :half] = both.astype(BF16)
        rope_outs[k][:, half:] = jnp.broadcast_to(factor, (2 * moves, LANES)).astype(BF16)
    for copy in copies:
        copy.wait()


def spread(scores, start, count, stride, part):
    for b in range(scores.shape[0]):
        scores.at[b][pl.ds(start, count, stride=stride), :] = part[:, b * LANES : (b + 1) * LANES]


def read(scores, span):
    parts = [scores[b, span, :] for b in range(scores.shape[0])]
    return parts[0] if len(parts) == 1 else jnp.concatenate(parts, axis=1)


def write(scores, span, part):
    for b in range(scores.shape[0]):
        scores[b, span, :] = part[:, b * LANES : (b + 1) * LANES]


GROUP = 8
HALF = 4
OUT_ROWS = 32


def local_kernel(
    sizes,
    partners,
    scale_hbm,
    table_hbm,
    lengths_hbm,
    move_hbm,
    lat_hbm,
    rope_hbm,
    q_hbm,
    turn_hbm,
    new_lat_hbm,
    new_rope_hbm,
    out_hbm,
    out,
    scale,
    qrel_out,
    q2_out,
    table,
    lengths,
    move,
    lat,
    rope,
    q_lat,
    q_rope,
    new_lat,
    new_rope,
    scores,
    limits,
    new_keys,
    new_turns,
    sems,
    lat_sems,
    out_sems,
):
    heads, per_device, rollouts, following, view = sizes
    slots, page_len, latent = lat.shape
    rows = rollouts * following * heads
    rope_dim = q_rope.shape[3]
    moves = move.shape[2]
    me = lax.axis_index(DP)
    pairs = (
        (table_hbm, table),
        (lengths_hbm, lengths),
        (move_hbm, move),
        (scale_hbm, scale),
        (turn_hbm, q_rope),
        (q_hbm, q_lat),
        (new_lat_hbm, new_lat),
        (new_rope_hbm, new_rope),
    )
    small = fetch(
        [pltpu.make_async_copy(src, dst, sems.at[i]) for i, (src, dst) in enumerate(pairs)]
        + row_copies(rope_hbm, rope, sems, len(pairs))
    )
    chunks = fetch(
        [
            pltpu.make_async_copy(
                lat_hbm.at[pl.ds(at, HALF)], lat.at[pl.ds(at, HALF)], lat_sems.at[at // HALF]
            )
            for at in range(0, slots, HALF)
        ]
    )
    place = iota((rows, rows), 0)
    rollout = (place // following) % rollouts
    token = place % following
    head = place // (following * rollouts)
    source = (rollout * following + token) * heads + head
    order = jnp.where(iota((rows, rows), 1) == source, 1.0, 0.0).astype(BF16)
    at = iota((rope_dim, 2 * rope_dim), 1)
    frm = iota((rope_dim, 2 * rope_dim), 0)
    for copy in small:
        copy.wait()
    for slot in range(rollouts * view):
        limits[slot] = 0
    for r in range(rollouts):
        for a in range(table.shape[1]):
            live = jnp.clip(lengths[r] - a * page_len, 0, page_len)
            limits[r * view + table[r, a]] = live
    q_turn = dot_nn(order, q_rope[...].reshape(rows, rope_dim)).astype(BF16)
    q2_out[:rows, :] = dot_nn(q_turn, jnp.where(at == frm, 1.0, 0.0).astype(BF16)).astype(BF16)
    q2_out[rows:, :] = dot_nn(
        q_turn, jnp.where(at == frm + rope_dim, 1.0, 0.0).astype(BF16)
    ).astype(BF16)
    qrel_out[...] = dot_nn(order, q_lat[...].reshape(rows, latent)).astype(BF16)
    twos = page_len // 2
    wide = 2 * rope_dim
    stacked = jnp.concatenate([rope[:, c * wide : (c + 1) * wide] for c in range(twos)], axis=0)
    turned = dot_nt(stacked, q2_out[...])
    for c in range(twos):
        part = turned[c * slots : (c + 1) * slots]
        spread(scores, 2 * c, slots, page_len, part[:, :rows])
        spread(scores, 2 * c + 1, slots, page_len, part[:, rows:])

    lane_rollout = (iota((1, rows), 1) // following) % rollouts
    lane_token = iota((1, rows), 1) % following
    position = iota((page_len, rows), 0)

    def limit_row(slot):
        row = jnp.full(lane_rollout.shape, limits[slot], jnp.int32)
        for r in range(1, rollouts):
            row = jnp.where(lane_rollout == r, limits[r * view + slot], row)
        return row

    for k in range(partners):
        for m in range(moves):
            at = 2 * rows + 2 + k * moves + m
            limit = limit_row(slots + (me ^ (k + 1)) * moves + m)
            out[at : at + 1, :rows] = limit.astype(F32)
    queries = qrel_out[...]
    out[rows : 2 * rows, :latent] = queries.astype(F32)
    out[: 2 * rows, latent:] = q2_out[...].astype(F32)

    def send(first, count, sem):
        return fetch(
            [pltpu.make_async_copy(out.at[pl.ds(first, count)], out_hbm.at[pl.ds(first, count)], sem)]
        )[0]

    sent = [send(rows, rows, out_sems.at[0])]
    fresh_rows = rollouts * following
    new_keys[...] = jnp.zeros(new_keys.shape, F32)
    new_turns[...] = jnp.zeros(new_turns.shape, F32)
    for r in range(rollouts):
        span = slice(r * following, (r + 1) * following)
        new_keys[span, :] = new_lat[r].astype(F32)
        new_turns[span, :rope_dim] = new_rope[r].astype(F32)
    fresh_keys = new_keys[...].astype(BF16)
    new_part = dot_nt(fresh_keys, queries) + dot_nt(
        new_turns[...].astype(BF16), q2_out[:rows, :]
    )
    new_row = iota(new_part.shape, 0)
    seen = (new_row // following == lane_rollout) & (new_row % following <= lane_token)
    new_part = jnp.where(seen & (new_row < fresh_rows), new_part * SCORE_SCALE, LOW)

    best = jnp.full((page_len, rows), LOW, F32)
    for first in range(0, slots, GROUP):
        for copy in chunks[first // HALF : (first + GROUP) // HALF]:
            copy.wait()
        keys = lat[first : first + GROUP].reshape(GROUP * page_len, latent)
        fresh = dot_nt(keys, queries)
        for g in range(GROUP):
            page = first + g
            span = pl.ds(page * page_len, page_len)
            part = fresh[g * page_len : (g + 1) * page_len] + read(scores, span)
            part = part * (scale[page] * SCORE_SCALE)
            write(scores, span, part)
            best = jnp.maximum(best, jnp.where(position < limit_row(page), part, LOW))
    for m in range(moves):
        page = move[0, me, m]
        part = read(scores, pl.ds(pl.multiple_of(page * page_len, page_len), page_len))
        live = position < limit_row(slots + me * moves + m)
        best = jnp.maximum(best, jnp.where(live, part, LOW))
    peak = jnp.max(best, axis=0, keepdims=True)
    peak = jnp.maximum(peak, jnp.max(new_part, axis=0, keepdims=True))

    def weigh(part, slot, factor, total):
        grown = jnp.where(position < limit_row(slot), jnp.exp(part - peak), 0.0)
        return (grown * factor).astype(BF16), total + grown

    new_exp = jnp.exp(new_part - peak)
    total = jnp.zeros((page_len, rows), F32)
    acc = dot_tn(new_exp.astype(BF16), fresh_keys)
    for first in range(0, slots, GROUP):
        weights = []
        for g in range(GROUP):
            page = first + g
            part = read(scores, pl.ds(page * page_len, page_len))
            weight, total = weigh(part, page, scale[page], total)
            weights.append(weight)
        keys = lat[first : first + GROUP].reshape(GROUP * page_len, latent)
        acc = acc + dot_tn(jnp.concatenate(weights, axis=0), keys)
    weights, keys = [], []
    for m in range(moves):
        page = move[0, me, m]
        part = read(scores, pl.ds(pl.multiple_of(page * page_len, page_len), page_len))
        weight, total = weigh(part, slots + me * moves + m, scale[page], total)
        weights.append(weight)
        keys.append(lat[page])
    acc = acc + dot_tn(jnp.concatenate(weights, axis=0), jnp.concatenate(keys, axis=0))
    whole = jnp.sum(total, axis=0, keepdims=True) + jnp.sum(new_exp, axis=0, keepdims=True)
    out[:rows, :latent] = acc
    out[2 * rows : 2 * rows + 1, :rows] = peak
    out[2 * rows + 1 : 2 * rows + 2, :rows] = whole
    sent.append(send(2 * rows, out.shape[0] - 2 * rows, out_sems.at[1]))
    for i in range(rows // OUT_ROWS):
        sent.append(send(i * OUT_ROWS, OUT_ROWS, out_sems.at[2 + i]))
    for copy in sent:
        copy.wait()


def merge_kernel(partners, *refs):
    got_lat, got_rope = refs[:partners], refs[partners : 2 * partners]
    local, out, scores = refs[2 * partners :]
    moves, page_len, latent = got_lat[0].shape
    rows = out.shape[0] * out.shape[1]
    qrel = local[rows : 2 * rows, :latent].astype(BF16)
    q2 = local[: 2 * rows, latent:].astype(BF16)
    wide = q2.shape[1]
    position = iota((page_len, rows), 0).astype(F32)
    best = jnp.full((page_len, rows), LOW, F32)
    half_lanes = got_rope[0].shape[1] - LANES
    pieces = half_lanes // wide
    span = moves * page_len
    factors = []
    for k in range(partners):
        turns = got_rope[k]
        stacked = jnp.concatenate(
            [turns[:, c * wide : (c + 1) * wide].astype(F32) for c in range(pieces)], axis=0
        ).astype(BF16)
        turned = dot_nt(stacked, q2)
        base = k * span
        for c in range(pieces):
            part = turned[c * 2 * moves : (c + 1) * 2 * moves]
            spread(scores, base + 2 * c, 2 * moves, page_len // 2, part[:, :rows])
            spread(scores, base + 2 * c + 1, 2 * moves, page_len // 2, part[:, rows:])
        fresh = dot_nt(got_lat[k][...].reshape(span, latent), qrel)
        marks = turns[:, half_lanes:].astype(F32)
        for m in range(moves):
            factor = marks[2 * m : 2 * m + 1, :1]
            factors.append(factor)
            where_at = pl.ds(base + m * page_len, page_len)
            part = fresh[m * page_len : (m + 1) * page_len] + read(scores, where_at)
            part = part * (factor * SCORE_SCALE)
            at = 2 * rows + 2 + k * moves + m
            part = jnp.where(position < local[at : at + 1, :rows], part, LOW)
            write(scores, where_at, part)
            best = jnp.maximum(best, part)
    peak_local = local[2 * rows : 2 * rows + 1, :rows]
    peak = jnp.maximum(jnp.max(best, axis=0, keepdims=True), peak_local)
    shrink = jnp.exp(peak_local - peak)
    acc = jnp.zeros((rows, latent), F32)
    grown_sum = jnp.zeros((page_len, rows), F32)
    for k in range(partners):
        weights = []
        for m in range(moves):
            part = read(scores, pl.ds(k * span + m * page_len, page_len))
            grown = jnp.exp(part - peak)
            grown_sum = grown_sum + grown
            weights.append((grown * factors[k * moves + m]).astype(BF16))
        acc = acc + dot_tn(
            jnp.concatenate(weights, axis=0), got_lat[k][...].reshape(span, latent)
        )
    total = local[2 * rows + 1 : 2 * rows + 2, :rows] * shrink + jnp.sum(grown_sum, axis=0, keepdims=True)

    def upright(row):
        return jnp.transpose(jnp.broadcast_to(row, (LANES, rows)))[:, :1]

    result = (local[:rows, :latent] * upright(shrink) + acc) / upright(total)
    out[...] = result.reshape(out.shape).astype(BF16)


def project_kernel(tokens, blocks, w_uv, other_uv, w_out, other_out, out):
    chips = blocks.shape[0]
    per_device = w_uv.shape[0]
    core = lax.axis_index("core")
    stacked = blocks[...].astype(F32).reshape(-1, blocks.shape[2]).astype(BF16)
    rows = stacked.shape[0]
    row_head = (iota((rows, 1), 0) // tokens) % (2 * per_device)
    values = []
    for first, uv in ((core * per_device, w_uv), ((1 - core) * per_device, other_uv)):
        for head in range(per_device):
            part = dot_nn(stacked, uv[head])
            values.append(jnp.where(row_head == first + head, part, 0.0).astype(BF16))
    values = jnp.concatenate(values, axis=1)
    out_row = iota((chips * tokens, rows), 0)
    in_row = iota((chips * tokens, rows), 1)
    same_chip = in_row // (tokens * 2 * per_device) == out_row // tokens
    same = same_chip & (in_row % tokens == out_row % tokens)
    joined = dot_nn(jnp.where(same, 1.0, 0.0).astype(BF16), values).astype(BF16)
    depth, width = w_out.shape
    step = 512 if width % 512 == 0 else width
    for at in range(0, width, step):
        part = dot_nn(joined[:, :depth], w_out[:, at : at + step])
        part = part + dot_nn(joined[:, depth:], other_out[:, at : at + step])
        out[:, :, at : at + step] = part.reshape(chips, tokens, step).astype(BF16)


def split_kernel(kept, got, out):
    total = kept[...] + got[...].astype(F32)
    out[...] = total.reshape(out.shape).astype(BF16)


def norm_kernel(got, residual, gain, routes, attn_out, out):
    total = jnp.sum(got[...].astype(F32), axis=0)
    attn_out[...] = total.astype(BF16)
    hidden = (residual[...].astype(F32) + total).astype(BF16).astype(F32)
    width = hidden.shape[1]
    power = jnp.sum(hidden * hidden, axis=1, keepdims=True) / width
    normed = (hidden * lax.rsqrt(power + NORM_EPS) * gain[...].reshape(1, width)).astype(BF16)
    named = routes[...].astype(F32).astype(BF16)
    for copy in range(out.shape[0]):
        out[copy, :, :width] = normed
        out[copy, :, width:] = jnp.zeros((hidden.shape[0], LANES), BF16)
        out[copy, :, width : width + routes.shape[1]] = named


def stack_kernel(*refs):
    for k, ref in enumerate(refs[:-1]):
        refs[-1][k] = ref[0]


def parts_kernel(kept, got, *outs):
    total = kept[...] + got[...].astype(F32)
    rows = outs[0].shape[0]
    for k, out in enumerate(outs):
        out[...] = total[k * rows : (k + 1) * rows].astype(out.dtype)


def add_kernel(*refs):
    total = refs[0][...]
    for ref in refs[1:-1]:
        total = total + ref[...].astype(F32)
    refs[-1][...] = total.astype(BF16)


def load_kernel(count, held, passed, *refs):
    sources, passed_out = refs[held : held + count], refs[held + count]
    outs, sems = refs[2 * held + count + 1 : -1], refs[-1]
    split = sems.shape[1]
    copies = []
    for k, (source, out) in enumerate(zip(sources, outs)):
        step = out.shape[0] // split
        for i in range(split):
            span = pl.ds(i * step, step)
            copies.append(
                pltpu.make_async_copy(source.at[0, span], out.at[span], sems.at[k, i])
            )
    fetch(copies)
    passed_out[...] = passed[...]
    for copy in copies:
        copy.wait()


def expert_kernel(top, count, *refs):
    pieces = refs[:count]
    w_router, w_gate, w_up, w_down = refs[count : count + 4]
    kept, away, rows_ref, hidden_ref = refs[count + 4 :]
    expert = lax.axis_index(EXPERT)
    width, units = w_gate.shape
    in_step = 256 if units % 256 == 0 else units
    out_step = 512 if width % 512 == 0 else width
    piece_rows = rows_ref.shape[0] // count
    named = []
    for k, piece in enumerate(pieces):
        whole = piece[...].astype(F32).reshape(piece_rows, -1)
        rows_ref[k * piece_rows : (k + 1) * piece_rows, :] = whole[:, :width].astype(BF16)
        named.append(whole[:, width:])
    named = jnp.concatenate(named, axis=0)
    rows = rows_ref[...]
    logits = dot_nt(rows, w_router[...])
    experts = iota(logits.shape, 1)
    chosen = jnp.zeros(logits.shape, F32)
    for k in range(top):
        route = named[:, k : k + 1].astype(jnp.int32)
        chosen = chosen + jnp.where(route == experts, 1.0, 0.0)
    sig = jax.nn.sigmoid(logits) * chosen
    mine = jnp.sum(jnp.where(experts == expert, sig, 0.0), axis=1, keepdims=True)
    gates = ROUTE_SCALE * mine / jnp.sum(sig, axis=1, keepdims=True)
    for at in range(0, units, in_step):
        gate = dot_nn(rows, w_gate[:, at : at + in_step])
        up = dot_nn(rows, w_up[:, at : at + in_step])
        hidden_ref[:, at : at + in_step] = (gate / (1.0 + jnp.exp(-gate)) * up).astype(BF16)
    half = rows_ref.shape[0] // 2
    hidden = hidden_ref[...]
    for at in range(0, width, out_step):
        part = dot_nn(hidden, w_down[:, at : at + out_step]) * gates
        kept[:, at : at + out_step] = part[:half]
        away[:, at : at + out_step] = part[half:].astype(BF16)


def halve_kernel(kept, got, keep, away):
    total = kept[...] + got[...].astype(F32)
    half = total.shape[0] // 2
    keep[...] = total[:half]
    away[...] = total[half:].astype(BF16)


def sum_kernel(got, out):
    out[...] = jnp.sum(got[...].astype(F32), axis=0).astype(BF16)


def body(dp_count, expert_count, *arrays):
    (
        cache_lat,
        cache_rope,
        page_scale,
        move_list,
        page_table,
        lengths,
        q_lat,
        q_rope,
        new_lat,
        new_rope,
        w_uv,
        w_out,
        residual,
        norm_gain,
        w_router,
        routes,
        w_gate,
        w_up,
        w_down,
    ) = arrays
    total_devices = dp_count * expert_count
    top_bit = total_devices // 2
    side_bit = 2

    def swap(x, mask, mask_odd=None):
        pairs = []
        for i in range(total_devices):
            other = mask if mask_odd is None or i % 2 == 0 else mask_odd
            pairs.append((i, i ^ other))
        return lax.ppermute(x, ROWS, pairs)

    def deal(x, names):
        return lax.all_to_all(x, names, split_axis=0, concat_axis=0, tiled=True)

    slots, page_len, latent = cache_lat.shape
    moves = move_list.shape[2]
    rollouts, following, heads, rope_dim = q_rope.shape
    view = slots + dp_count * moves
    per_device = heads // expert_count
    tokens = rollouts * following
    width = residual.shape[1]
    partners = dp_count - 1
    rows = tokens * heads
    sizes = (heads, per_device, rollouts, following, view)
    chips = expert_count // 2
    picked = call(
        functools.partial(pick_kernel, partners, moves),
        [shape((moves, page_len, latent), BF16)] * partners
        + [shape((2 * moves, cache_rope.shape[1] // 2 + LANES), BF16)] * partners
        + [shape((slots,), F32)],
        (move_list, page_scale, cache_lat, cache_rope),
        in_specs=[HBM] * 4,
        out_specs=[VMEM] * (2 * partners) + [SMEM],
        scratch=[
            pltpu.SMEM(move_list.shape, jnp.int32),
            pltpu.VMEM(cache_rope.shape, BF16),
            pltpu.VMEM(page_scale.shape, BF16),
            pltpu.VMEM((slots,), F32),
            pltpu.SemaphoreType.DMA((partners, moves)),
            pltpu.SemaphoreType.DMA((3 + slots // ROPE_ROWS,)),
        ],
        vmem=60,
    )
    got_lat = [swap(picked[k], (k + 1) * expert_count) for k in range(partners)]
    got_rope = [swap(picked[partners + k], (k + 1) * expert_count) for k in range(partners)]

    extra = -(-(2 + partners * moves) // 8) * 8
    local = call(
        functools.partial(local_kernel, sizes, partners),
        [shape((2 * rows + extra, latent + 2 * rope_dim), F32)],
        (
            picked[-1],
            page_table,
            lengths,
            move_list,
            cache_lat,
            cache_rope,
            q_lat,
            q_rope,
            new_lat,
            new_rope,
        ),
        in_specs=[HBM] * 10,
        out_specs=[HBM],
        scratch=[
            pltpu.VMEM((2 * rows + extra, latent + 2 * rope_dim), F32),
            pltpu.SMEM((slots,), F32),
            pltpu.VMEM((rows, latent), BF16),
            pltpu.VMEM((2 * rows, 2 * rope_dim), BF16),
            pltpu.SMEM(page_table.shape, jnp.int32),
            pltpu.SMEM(lengths.shape, jnp.int32),
            pltpu.SMEM(move_list.shape, jnp.int32),
            pltpu.VMEM(cache_lat.shape, BF16),
            pltpu.VMEM(cache_rope.shape, BF16),
            pltpu.VMEM(q_lat.shape, BF16),
            pltpu.VMEM(q_rope.shape, BF16),
            pltpu.VMEM(new_lat.shape, BF16),
            pltpu.VMEM(new_rope.shape, BF16),
            pltpu.VMEM((rows // LANES, slots * page_len, LANES), F32),
            pltpu.SMEM((rollouts * view,), jnp.int32),
            pltpu.VMEM((16, latent), F32),
            pltpu.VMEM((16, 2 * rope_dim), F32),
            pltpu.SemaphoreType.DMA((8 + slots // ROPE_ROWS,)),
            pltpu.SemaphoreType.DMA((slots // HALF,)),
            pltpu.SemaphoreType.DMA((2 + rows // OUT_ROWS,)),
        ],
        vmem=60,
        cost=(2 * slots * page_len * rows * (2 * latent + 2 * rope_dim), 4 * MIB),
    )
    blocks = call(
        functools.partial(merge_kernel, partners),
        [shape((chips, 2 * tokens * per_device, latent), BF16)],
        (*got_lat, *got_rope, *local),
        scratch=[pltpu.VMEM((rows // LANES, partners * moves * page_len, LANES), F32)],
        cost=(2 * moves * page_len * rows * 2 * latent, MIB),
    )[0]

    away_uv, away_out, blocks = lax.optimization_barrier((w_uv, w_out, blocks))
    other_uv, other_out = swap(away_uv, 1), swap(away_out, 1)
    blocks = deal(blocks, CHIP)

    parts = call(
        functools.partial(project_kernel, tokens),
        [shape((chips, tokens, width), BF16)],
        (blocks, w_uv, other_uv, w_out, other_out),
        cost=(4 * chips * tokens * width * w_out.shape[0], 8 * MIB),
    )[0]
    parts = deal(parts, CHIP)
    far_count = total_devices // 8
    masks = [2 * side_bit * k for k in range(far_count)]
    direct = far_count <= 4
    attn_out, own_rows = call(
        norm_kernel,
        [
            shape((tokens, width), BF16),
            shape((1 if direct else far_count, tokens, width + LANES), BF16),
        ],
        (parts, residual, norm_gain, routes),
    )

    def load(passed, sources, vmem, held=()):
        outs = [shape(passed.shape, BF16)] + [shape(x.shape, BF16) for x in held]
        return pl.pallas_call(
            functools.partial(load_kernel, len(sources), len(held)),
            out_shape=outs + [shape(w.shape[1:], BF16) for w in sources],
            in_specs=[VMEM] + [ANY] * len(held) + [HBM] * len(sources),
            out_specs=[VMEM] + [ANY] * len(held) + [VMEM] * len(sources),
            input_output_aliases={1 + i: 1 + i for i in range(len(held))},
            scratch_shapes=[pltpu.SemaphoreType.DMA((len(sources), 8))],
            compiler_params=pltpu.CompilerParams(vmem_limit_bytes=vmem * MIB),
            cost_estimate=pl.CostEstimate(
                flops=0, bytes_accessed=2 * sum(w.size for w in sources), transcendentals=0
            ),
        )(passed, *held, *sources)

    if direct:
        others = [swap(own_rows, mask) for mask in masks[1:]]
        own_rows, down_here = load(own_rows, (w_down,), LOAD_MIB)
        piece = call(
            stack_kernel,
            [shape((far_count, tokens, width + LANES), BF16)],
            (own_rows, *others),
        )[0]
    else:
        own_rows, down_here = load(own_rows, (w_down,), LOAD_MIB)
        piece = deal(own_rows, FAR)
    side_piece = swap(piece, top_bit, side_bit)
    piece, down_here, up_here = load(piece, (w_up,), UP_MIB, (down_here,))
    pieces = [piece, side_piece, swap(piece, side_bit, top_bit), swap(side_piece, side_bit, top_bit)]
    pieces[1], down_here, up_here, gate_here = load(
        side_piece, (w_gate,), SIDE_MIB, (down_here, up_here)
    )
    pieces = pieces + [swap(p, 1) for p in pieces]

    all_rows = total_devices * tokens
    hidden_units = w_gate.shape[2]
    half = all_rows // 2
    kept, away = call(
        functools.partial(expert_kernel, routes.shape[1], len(pieces)),
        [shape((half, width), F32), shape((half, width), BF16)],
        (*pieces, w_router.T, gate_here, up_here, down_here),
        scratch=[
            pltpu.VMEM((all_rows, width), BF16),
            pltpu.VMEM((all_rows, hidden_units), BF16),
        ],
        vmem=EXPERT_MIB if all_rows <= 256 else 56,
        cost=(6 * all_rows * width * hidden_units, 6 * width * hidden_units),
    )

    got = swap(away, 1)
    kept, away = call(
        halve_kernel,
        [shape((half // 2, width), F32), shape((half // 2, width), BF16)],
        (kept, got),
    )
    got = swap(away, side_bit, top_bit)
    kept, away = call(
        halve_kernel,
        [shape((half // 4, width), F32), shape((half // 4, width), BF16)],
        (kept, got),
    )
    got = swap(away, top_bit, side_bit)
    moe_shape = [shape((tokens, width), BF16)]
    if direct:
        parts = call(
            parts_kernel, [shape((tokens, width), F32)] + moe_shape * (far_count - 1), (kept, got)
        )
        got = [swap(part, mask) for part, mask in zip(parts[1:], masks[1:])]
        moe_out = call(add_kernel, moe_shape, (parts[0], *got))[0]
    else:
        parts = call(split_kernel, [shape((far_count, tokens, width), BF16)], (kept, got))[0]
        moe_out = call(sum_kernel, moe_shape, (deal(parts, FAR),))[0]
    return (attn_out, moe_out)


def solution(mesh):
    dp_count, expert_count = mesh.shape["dp"], mesh.shape["expert"]
    finer = Mesh(mesh.devices.reshape(2, dp_count // 2, expert_count // 4, 2, 2), ROWS)
    return jax.shard_map(
        functools.partial(body, dp_count, expert_count),
        mesh=finer,
        in_specs=(
            P(ROWS, None, None),
            P(ROWS, None),
            P(ROWS),
            P(ROWS, None, None),
            P(ROWS, None),
            P(ROWS),
            P(ROWS, None, None, None),
            P(ROWS, None, None, None),
            P(ROWS, None, None),
            P(ROWS, None, None),
            P(EXPERT, None, None),
            P(EXPERT, None),
            P(ROWS, None),
            P(),
            P(),
            P(ROWS, None),
            P(EXPERT, None, DP),
            P(EXPERT, None, DP),
            P(EXPERT, DP, None),
        ),
        out_specs=(P(ROWS, None), P(ROWS, None)),
        check_vma=False,
    )
```

```python
import functools

import jax
import jax.numpy as jnp
from jax import lax
from jax.experimental import pallas as pl
from jax.experimental.pallas import tpu as pltpu
from jax.sharding import Mesh, PartitionSpec as P

SCORE_SCALE = 0.07216878364870322
ROUTE_SCALE = 2.5
NORM_EPS = 1e-06
LOW = -1e30
LANES = 128
MIB = 1 << 20
BF16 = jnp.bfloat16
F32 = jnp.float32
VMEM = pl.BlockSpec(memory_space=pltpu.VMEM)
SMEM = pl.BlockSpec(memory_space=pltpu.SMEM)
ANY = pl.BlockSpec(memory_space=pl.ANY)
HBM = pl.BlockSpec(memory_space=pltpu.HBM)
DP = ("top", "low")
EXPERT = ("far", "side", "core")
ROWS = DP + EXPERT
FAR = ("low", "far")
CHIP = ("far", "side")
ROPE_ROWS = 16
LOAD_MIB = 41
UP_MIB = 34
SIDE_MIB = 28
EXPERT_MIB = 16


def dot_nt(a, b):
    return lax.dot_general(a, b, (((1,), (1,)), ((), ())), preferred_element_type=F32)


def dot_tn(a, b):
    return lax.dot_general(a, b, (((0,), (0,)), ((), ())), preferred_element_type=F32)


def dot_nn(a, b):
    return jnp.dot(a, b, preferred_element_type=F32)


def call(kernel, outs, operands, in_specs=None, out_specs=None, scratch=(), vmem=16, cost=None):
    flops, moved = cost or (0, 0)
    return pl.pallas_call(
        kernel,
        out_shape=outs,
        in_specs=in_specs or [VMEM] * len(operands),
        out_specs=out_specs or [VMEM] * len(outs),
        scratch_shapes=list(scratch),
        compiler_params=pltpu.CompilerParams(vmem_limit_bytes=vmem * MIB),
        cost_estimate=pl.CostEstimate(flops=flops, bytes_accessed=moved, transcendentals=0),
    )(*operands)


def shape(dims, dtype):
    return jax.ShapeDtypeStruct(dims, dtype)


def iota(dims, axis):
    return lax.broadcasted_iota(jnp.int32, dims, axis)


def fetch(copies):
    for copy in copies:
        copy.start()
    return copies


def row_copies(source, target, sems, first):
    return [
        pltpu.make_async_copy(
            source.at[pl.ds(at, ROPE_ROWS)], target.at[pl.ds(at, ROPE_ROWS)], sems.at[first + i]
        )
        for i, at in enumerate(range(0, source.shape[0], ROPE_ROWS))
    ]


def pick_kernel(partners, moves, move_hbm, scale_hbm, lat, rope_hbm, *rest):
    lat_outs, rope_outs = rest[:partners], rest[partners : 2 * partners]
    scale_out, move, rope, scale_ref, wide_scale, lat_sems, sems = rest[2 * partners :]
    slots, width = rope.shape
    half = width // 2
    me = lax.axis_index(DP)
    get_move, get_scale, *get_rope = fetch(
        [
            pltpu.make_async_copy(move_hbm, move, sems.at[0]),
            pltpu.make_async_copy(scale_hbm, scale_ref, sems.at[1]),
        ]
        + row_copies(rope_hbm, rope, sems, 3)
    )
    get_move.wait()
    copies = []
    for k in range(partners):
        for m in range(moves):
            copies.append(
                pltpu.make_async_copy(
                    lat.at[move[0, me ^ (k + 1), m]], lat_outs[k].at[m], lat_sems.at[k, m]
                )
            )
    fetch(copies)
    get_scale.wait()
    wide_scale[...] = scale_ref[...].astype(F32)
    (put_scale,) = fetch([pltpu.make_async_copy(wide_scale, scale_out, sems.at[2])])
    put_scale.wait()
    for copy in get_rope:
        copy.wait()
    row = iota((2 * moves, 1), 0)
    column = iota((2 * moves, slots), 1)
    for k in range(partners):
        target = jnp.zeros((2 * moves, 1), jnp.int32)
        factor = jnp.zeros((2 * moves, 1), F32)
        for m in range(moves):
            page = move[0, me ^ (k + 1), m]
            target = jnp.where(row // 2 == m, page, target)
            factor = jnp.where(row // 2 == m, scale_out[page], factor)
        hit = column == target
        even = row % 2 == 0
        first = jnp.where(hit & even, 1.0, 0.0).astype(BF16)
        second = jnp.where(hit & (~even), 1.0, 0.0).astype(BF16)
        both = dot_nn(first, rope[:, :half]) + dot_nn(second, rope[:, half:])
        rope_outs[k][:, :half] = both.astype(BF16)
        rope_outs[k][:, half:] = jnp.broadcast_to(factor, (2 * moves, LANES)).astype(BF16)
    for copy in copies:
        copy.wait()


def spread(scores, start, count, stride, part):
    for b in range(scores.shape[0]):
        scores.at[b][pl.ds(start, count, stride=stride), :] = part[:, b * LANES : (b + 1) * LANES]


def read(scores, span):
    parts = [scores[b, span, :] for b in range(scores.shape[0])]
    return parts[0] if len(parts) == 1 else jnp.concatenate(parts, axis=1)


def write(scores, span, part):
    for b in range(scores.shape[0]):
        scores[b, span, :] = part[:, b * LANES : (b + 1) * LANES]


GROUP = 8
HALF = 4
OUT_ROWS = 32


def local_kernel(
    sizes,
    partners,
    scale_hbm,
    table_hbm,
    lengths_hbm,
    move_hbm,
    lat_hbm,
    rope_hbm,
    q_hbm,
    turn_hbm,
    new_lat_hbm,
    new_rope_hbm,
    out_hbm,
    out,
    scale,
    qrel_out,
    q2_out,
    table,
    lengths,
    move,
    lat,
    rope,
    q_lat,
    q_rope,
    new_lat,
    new_rope,
    scores,
    limits,
    new_keys,
    new_turns,
    sems,
    lat_sems,
    out_sems,
):
    heads, per_device, rollouts, following, view = sizes
    slots, page_len, latent = lat.shape
    rows = rollouts * following * heads
    rope_dim = q_rope.shape[3]
    moves = move.shape[2]
    me = lax.axis_index(DP)
    pairs = (
        (table_hbm, table),
        (lengths_hbm, lengths),
        (move_hbm, move),
        (scale_hbm, scale),
        (turn_hbm, q_rope),
        (q_hbm, q_lat),
        (new_lat_hbm, new_lat),
        (new_rope_hbm, new_rope),
    )
    small = fetch(
        [pltpu.make_async_copy(src, dst, sems.at[i]) for i, (src, dst) in enumerate(pairs)]
        + row_copies(rope_hbm, rope, sems, len(pairs))
    )
    chunks = fetch(
        [
            pltpu.make_async_copy(
                lat_hbm.at[pl.ds(at, HALF)], lat.at[pl.ds(at, HALF)], lat_sems.at[at // HALF]
            )
            for at in range(0, slots, HALF)
        ]
    )
    place = iota((rows, rows), 0)
    rollout = (place // following) % rollouts
    token = place % following
    head = place // (following * rollouts)
    source = (rollout * following + token) * heads + head
    order = jnp.where(iota((rows, rows), 1) == source, 1.0, 0.0).astype(BF16)
    at = iota((rope_dim, 2 * rope_dim), 1)
    frm = iota((rope_dim, 2 * rope_dim), 0)
    for copy in small:
        copy.wait()
    for slot in range(rollouts * view):
        limits[slot] = 0
    for r in range(rollouts):
        for a in range(table.shape[1]):
            live = jnp.clip(lengths[r] - a * page_len, 0, page_len)
            limits[r * view + table[r, a]] = live
    q_turn = dot_nn(order, q_rope[...].reshape(rows, rope_dim)).astype(BF16)
    q2_out[:rows, :] = dot_nn(q_turn, jnp.where(at == frm, 1.0, 0.0).astype(BF16)).astype(BF16)
    q2_out[rows:, :] = dot_nn(
        q_turn, jnp.where(at == frm + rope_dim, 1.0, 0.0).astype(BF16)
    ).astype(BF16)
    qrel_out[...] = dot_nn(order, q_lat[...].reshape(rows, latent)).astype(BF16)
    twos = page_len // 2
    wide = 2 * rope_dim
    stacked = jnp.concatenate([rope[:, c * wide : (c + 1) * wide] for c in range(twos)], axis=0)
    turned = dot_nt(stacked, q2_out[...])
    for c in range(twos):
        part = turned[c * slots : (c + 1) * slots]
        spread(scores, 2 * c, slots, page_len, part[:, :rows])
        spread(scores, 2 * c + 1, slots, page_len, part[:, rows:])

    lane_rollout = (iota((1, rows), 1) // following) % rollouts
    lane_token = iota((1, rows), 1) % following
    position = iota((page_len, rows), 0)

    def limit_row(slot):
        row = jnp.full(lane_rollout.shape, limits[slot], jnp.int32)
        for r in range(1, rollouts):
            row = jnp.where(lane_rollout == r, limits[r * view + slot], row)
        return row

    for k in range(partners):
        for m in range(moves):
            at = 2 * rows + 2 + k * moves + m
            limit = limit_row(slots + (me ^ (k + 1)) * moves + m)
            out[at : at + 1, :rows] = limit.astype(F32)
    queries = qrel_out[...]
    out[rows : 2 * rows, :latent] = queries.astype(F32)
    out[: 2 * rows, latent:] = q2_out[...].astype(F32)

    def send(first, count, sem):
        return fetch(
            [pltpu.make_async_copy(out.at[pl.ds(first, count)], out_hbm.at[pl.ds(first, count)], sem)]
        )[0]

    sent = [send(rows, rows, out_sems.at[0])]
    fresh_rows = rollouts * following
    new_keys[...] = jnp.zeros(new_keys.shape, F32)
    new_turns[...] = jnp.zeros(new_turns.shape, F32)
    for r in range(rollouts):
        span = slice(r * following, (r + 1) * following)
        new_keys[span, :] = new_lat[r].astype(F32)
        new_turns[span, :rope_dim] = new_rope[r].astype(F32)
    fresh_keys = new_keys[...].astype(BF16)
    new_part = dot_nt(fresh_keys, queries) + dot_nt(
        new_turns[...].astype(BF16), q2_out[:rows, :]
    )
    new_row = iota(new_part.shape, 0)
    seen = (new_row // following == lane_rollout) & (new_row % following <= lane_token)
    new_part = jnp.where(seen & (new_row < fresh_rows), new_part * SCORE_SCALE, LOW)

    best = jnp.full((page_len, rows), LOW, F32)
    for first in range(0, slots, GROUP):
        for copy in chunks[first // HALF : (first + GROUP) // HALF]:
            copy.wait()
        keys = lat[first : first + GROUP].reshape(GROUP * page_len, latent)
        fresh = dot_nt(keys, queries)
        for g in range(GROUP):
            page = first + g
            span = pl.ds(page * page_len, page_len)
            part = fresh[g * page_len : (g + 1) * page_len] + read(scores, span)
            part = part * (scale[page] * SCORE_SCALE)
            write(scores, span, part)
            best = jnp.maximum(best, jnp.where(position < limit_row(page), part, LOW))
    for m in range(moves):
        page = move[0, me, m]
        part = read(scores, pl.ds(pl.multiple_of(page * page_len, page_len), page_len))
        live = position < limit_row(slots + me * moves + m)
        best = jnp.maximum(best, jnp.where(live, part, LOW))
    peak = jnp.max(best, axis=0, keepdims=True)
    peak = jnp.maximum(peak, jnp.max(new_part, axis=0, keepdims=True))

    def weigh(part, slot, factor, total):
        grown = jnp.where(position < limit_row(slot), jnp.exp(part - peak), 0.0)
        return (grown * factor).astype(BF16), total + grown

    new_exp = jnp.exp(new_part - peak)
    total = jnp.zeros((page_len, rows), F32)
    acc = dot_tn(new_exp.astype(BF16), fresh_keys)
    for first in range(0, slots, GROUP):
        weights = []
        for g in range(GROUP):
            page = first + g
            part = read(scores, pl.ds(page * page_len, page_len))
            weight, total = weigh(part, page, scale[page], total)
            weights.append(weight)
        keys = lat[first : first + GROUP].reshape(GROUP * page_len, latent)
        acc = acc + dot_tn(jnp.concatenate(weights, axis=0), keys)
    weights, keys = [], []
    for m in range(moves):
        page = move[0, me, m]
        part = read(scores, pl.ds(pl.multiple_of(page * page_len, page_len), page_len))
        weight, total = weigh(part, slots + me * moves + m, scale[page], total)
        weights.append(weight)
        keys.append(lat[page])
    acc = acc + dot_tn(jnp.concatenate(weights, axis=0), jnp.concatenate(keys, axis=0))
    whole = jnp.sum(total, axis=0, keepdims=True) + jnp.sum(new_exp, axis=0, keepdims=True)
    out[:rows, :latent] = acc
    out[2 * rows : 2 * rows + 1, :rows] = peak
    out[2 * rows + 1 : 2 * rows + 2, :rows] = whole
    sent.append(send(2 * rows, out.shape[0] - 2 * rows, out_sems.at[1]))
    for i in range(rows // OUT_ROWS):
        sent.append(send(i * OUT_ROWS, OUT_ROWS, out_sems.at[2 + i]))
    for copy in sent:
        copy.wait()


def merge_kernel(partners, *refs):
    got_lat, got_rope = refs[:partners], refs[partners : 2 * partners]
    local, out, scores = refs[2 * partners :]
    moves, page_len, latent = got_lat[0].shape
    rows = out.shape[0] * out.shape[1]
    qrel = local[rows : 2 * rows, :latent].astype(BF16)
    q2 = local[: 2 * rows, latent:].astype(BF16)
    wide = q2.shape[1]
    position = iota((page_len, rows), 0).astype(F32)
    best = jnp.full((page_len, rows), LOW, F32)
    half_lanes = got_rope[0].shape[1] - LANES
    pieces = half_lanes // wide
    span = moves * page_len
    factors = []
    for k in range(partners):
        turns = got_rope[k]
        stacked = jnp.concatenate(
            [turns[:, c * wide : (c + 1) * wide].astype(F32) for c in range(pieces)], axis=0
        ).astype(BF16)
        turned = dot_nt(stacked, q2)
        base = k * span
        for c in range(pieces):
            part = turned[c * 2 * moves : (c + 1) * 2 * moves]
            spread(scores, base + 2 * c, 2 * moves, page_len // 2, part[:, :rows])
            spread(scores, base + 2 * c + 1, 2 * moves, page_len // 2, part[:, rows:])
        fresh = dot_nt(got_lat[k][...].reshape(span, latent), qrel)
        marks = turns[:, half_lanes:].astype(F32)
        for m in range(moves):
            factor = marks[2 * m : 2 * m + 1, :1]
            factors.append(factor)
            where_at = pl.ds(base + m * page_len, page_len)
            part = fresh[m * page_len : (m + 1) * page_len] + read(scores, where_at)
            part = part * (factor * SCORE_SCALE)
            at = 2 * rows + 2 + k * moves + m
            part = jnp.where(position < local[at : at + 1, :rows], part, LOW)
            write(scores, where_at, part)
            best = jnp.maximum(best, part)
    peak_local = local[2 * rows : 2 * rows + 1, :rows]
    peak = jnp.maximum(jnp.max(best, axis=0, keepdims=True), peak_local)
    shrink = jnp.exp(peak_local - peak)
    acc = jnp.zeros((rows, latent), F32)
    grown_sum = jnp.zeros((page_len, rows), F32)
    for k in range(partners):
        weights = []
        for m in range(moves):
            part = read(scores, pl.ds(k * span + m * page_len, page_len))
            grown = jnp.exp(part - peak)
            grown_sum = grown_sum + grown
            weights.append((grown * factors[k * moves + m]).astype(BF16))
        acc = acc + dot_tn(
            jnp.concatenate(weights, axis=0), got_lat[k][...].reshape(span, latent)
        )
    total = local[2 * rows + 1 : 2 * rows + 2, :rows] * shrink + jnp.sum(grown_sum, axis=0, keepdims=True)

    def upright(row):
        return jnp.transpose(jnp.broadcast_to(row, (LANES, rows)))[:, :1]

    result = (local[:rows, :latent] * upright(shrink) + acc) / upright(total)
    out[...] = result.reshape(out.shape).astype(BF16)


def project_kernel(tokens, blocks, w_uv, other_uv, w_out, other_out, out):
    chips = blocks.shape[0]
    per_device = w_uv.shape[0]
    core = lax.axis_index("core")
    stacked = blocks[...].astype(F32).reshape(-1, blocks.shape[2]).astype(BF16)
    rows = stacked.shape[0]
    row_head = (iota((rows, 1), 0) // tokens) % (2 * per_device)
    values = []
    for first, uv in ((core * per_device, w_uv), ((1 - core) * per_device, other_uv)):
        for head in range(per_device):
            part = dot_nn(stacked, uv[head])
            values.append(jnp.where(row_head == first + head, part, 0.0).astype(BF16))
    values = jnp.concatenate(values, axis=1)
    out_row = iota((chips * tokens, rows), 0)
    in_row = iota((chips * tokens, rows), 1)
    same_chip = in_row // (tokens * 2 * per_device) == out_row // tokens
    same = same_chip & (in_row % tokens == out_row % tokens)
    joined = dot_nn(jnp.where(same, 1.0, 0.0).astype(BF16), values).astype(BF16)
    depth, width = w_out.shape
    step = 512 if width % 512 == 0 else width
    for at in range(0, width, step):
        part = dot_nn(joined[:, :depth], w_out[:, at : at + step])
        part = part + dot_nn(joined[:, depth:], other_out[:, at : at + step])
        out[:, :, at : at + step] = part.reshape(chips, tokens, step).astype(BF16)


def split_kernel(kept, got, out):
    total = kept[...] + got[...].astype(F32)
    out[...] = total.reshape(out.shape).astype(BF16)


def norm_kernel(got, residual, gain, routes, attn_out, out):
    total = jnp.sum(got[...].astype(F32), axis=0)
    attn_out[...] = total.astype(BF16)
    hidden = (residual[...].astype(F32) + total).astype(BF16).astype(F32)
    width = hidden.shape[1]
    power = jnp.sum(hidden * hidden, axis=1, keepdims=True) / width
    normed = (hidden * lax.rsqrt(power + NORM_EPS) * gain[...].reshape(1, width)).astype(BF16)
    named = routes[...].astype(F32).astype(BF16)
    for copy in range(out.shape[0]):
        out[copy, :, :width] = normed
        out[copy, :, width:] = jnp.zeros((hidden.shape[0], LANES), BF16)
        out[copy, :, width : width + routes.shape[1]] = named


def stack_kernel(*refs):
    for k, ref in enumerate(refs[:-1]):
        refs[-1][k] = ref[0]


def parts_kernel(kept, got, *outs):
    total = kept[...] + got[...].astype(F32)
    rows = outs[0].shape[0]
    for k, out in enumerate(outs):
        out[...] = total[k * rows : (k + 1) * rows].astype(out.dtype)


def add_kernel(*refs):
    total = refs[0][...]
    for ref in refs[1:-1]:
        total = total + ref[...].astype(F32)
    refs[-1][...] = total.astype(BF16)


def load_kernel(count, held, passes, *refs):
    first_out = passes + held + count
    passed, sources = refs[:passes], refs[passes + held : first_out]
    passed_outs = refs[first_out : first_out + passes]
    outs, sems = refs[first_out + passes + held : -1], refs[-1]
    split = sems.shape[1]
    copies = []
    for k, (source, out) in enumerate(zip(sources, outs)):
        step = out.shape[0] // split
        for i in range(split):
            span = pl.ds(i * step, step)
            copies.append(
                pltpu.make_async_copy(source.at[0, span], out.at[span], sems.at[k, i])
            )
    fetch(copies)
    for source, out in zip(passed, passed_outs):
        out[...] = source[...]
    for copy in copies:
        copy.wait()


def expert_kernel(top, count, *refs):
    pieces = refs[:count]
    w_router, w_gate, w_up, w_down = refs[count : count + 4]
    kept, away, rows_ref, hidden_ref = refs[count + 4 :]
    expert = lax.axis_index(EXPERT)
    width, units = w_gate.shape
    in_step = 256 if units % 256 == 0 else units
    out_step = 512 if width % 512 == 0 else width
    piece_rows = rows_ref.shape[0] // count
    named = []
    for k, piece in enumerate(pieces):
        whole = piece[...].astype(F32).reshape(piece_rows, -1)
        rows_ref[k * piece_rows : (k + 1) * piece_rows, :] = whole[:, :width].astype(BF16)
        named.append(whole[:, width:])
    named = jnp.concatenate(named, axis=0)
    rows = rows_ref[...]
    logits = dot_nt(rows, w_router[...])
    experts = iota(logits.shape, 1)
    chosen = jnp.zeros(logits.shape, F32)
    for k in range(top):
        route = named[:, k : k + 1].astype(jnp.int32)
        chosen = chosen + jnp.where(route == experts, 1.0, 0.0)
    sig = jax.nn.sigmoid(logits) * chosen
    mine = jnp.sum(jnp.where(experts == expert, sig, 0.0), axis=1, keepdims=True)
    gates = ROUTE_SCALE * mine / jnp.sum(sig, axis=1, keepdims=True)
    for at in range(0, units, in_step):
        gate = dot_nn(rows, w_gate[:, at : at + in_step])
        up = dot_nn(rows, w_up[:, at : at + in_step])
        hidden_ref[:, at : at + in_step] = (gate / (1.0 + jnp.exp(-gate)) * up).astype(BF16)
    half = rows_ref.shape[0] // 2
    hidden = hidden_ref[...]
    for at in range(0, width, out_step):
        part = dot_nn(hidden, w_down[:, at : at + out_step]) * gates
        kept[:, at : at + out_step] = part[:half]
        away[:, at : at + out_step] = part[half:].astype(BF16)


def halve_kernel(kept, got, keep, away):
    total = kept[...] + got[...].astype(F32)
    half = total.shape[0] // 2
    keep[...] = total[:half]
    away[...] = total[half:].astype(BF16)


def sum_kernel(got, out):
    out[...] = jnp.sum(got[...].astype(F32), axis=0).astype(BF16)


def body(dp_count, expert_count, *arrays):
    (
        cache_lat,
        cache_rope,
        page_scale,
        move_list,
        page_table,
        lengths,
        q_lat,
        q_rope,
        new_lat,
        new_rope,
        w_uv,
        w_out,
        residual,
        norm_gain,
        w_router,
        routes,
        w_gate,
        w_up,
        w_down,
    ) = arrays
    total_devices = dp_count * expert_count
    top_bit = total_devices // 2
    side_bit = 2

    def swap(x, mask, mask_odd=None):
        pairs = []
        for i in range(total_devices):
            other = mask if mask_odd is None or i % 2 == 0 else mask_odd
            pairs.append((i, i ^ other))
        return lax.ppermute(x, ROWS, pairs)

    def deal(x, names):
        return lax.all_to_all(x, names, split_axis=0, concat_axis=0, tiled=True)

    slots, page_len, latent = cache_lat.shape
    moves = move_list.shape[2]
    rollouts, following, heads, rope_dim = q_rope.shape
    view = slots + dp_count * moves
    per_device = heads // expert_count
    tokens = rollouts * following
    width = residual.shape[1]
    partners = dp_count - 1
    rows = tokens * heads
    sizes = (heads, per_device, rollouts, following, view)
    chips = expert_count // 2
    picked = call(
        functools.partial(pick_kernel, partners, moves),
        [shape((moves, page_len, latent), BF16)] * partners
        + [shape((2 * moves, cache_rope.shape[1] // 2 + LANES), BF16)] * partners
        + [shape((slots,), F32)],
        (move_list, page_scale, cache_lat, cache_rope),
        in_specs=[HBM] * 4,
        out_specs=[VMEM] * (2 * partners) + [SMEM],
        scratch=[
            pltpu.SMEM(move_list.shape, jnp.int32),
            pltpu.VMEM(cache_rope.shape, BF16),
            pltpu.VMEM(page_scale.shape, BF16),
            pltpu.VMEM((slots,), F32),
            pltpu.SemaphoreType.DMA((partners, moves)),
            pltpu.SemaphoreType.DMA((3 + slots // ROPE_ROWS,)),
        ],
        vmem=60,
    )
    got_lat = [swap(picked[k], (k + 1) * expert_count) for k in range(partners)]
    got_rope = [swap(picked[partners + k], (k + 1) * expert_count) for k in range(partners)]

    extra = -(-(2 + partners * moves) // 8) * 8
    local = call(
        functools.partial(local_kernel, sizes, partners),
        [shape((2 * rows + extra, latent + 2 * rope_dim), F32)],
        (
            picked[-1],
            page_table,
            lengths,
            move_list,
            cache_lat,
            cache_rope,
            q_lat,
            q_rope,
            new_lat,
            new_rope,
        ),
        in_specs=[HBM] * 10,
        out_specs=[HBM],
        scratch=[
            pltpu.VMEM((2 * rows + extra, latent + 2 * rope_dim), F32),
            pltpu.SMEM((slots,), F32),
            pltpu.VMEM((rows, latent), BF16),
            pltpu.VMEM((2 * rows, 2 * rope_dim), BF16),
            pltpu.SMEM(page_table.shape, jnp.int32),
            pltpu.SMEM(lengths.shape, jnp.int32),
            pltpu.SMEM(move_list.shape, jnp.int32),
            pltpu.VMEM(cache_lat.shape, BF16),
            pltpu.VMEM(cache_rope.shape, BF16),
            pltpu.VMEM(q_lat.shape, BF16),
            pltpu.VMEM(q_rope.shape, BF16),
            pltpu.VMEM(new_lat.shape, BF16),
            pltpu.VMEM(new_rope.shape, BF16),
            pltpu.VMEM((rows // LANES, slots * page_len, LANES), F32),
            pltpu.SMEM((rollouts * view,), jnp.int32),
            pltpu.VMEM((16, latent), F32),
            pltpu.VMEM((16, 2 * rope_dim), F32),
            pltpu.SemaphoreType.DMA((8 + slots // ROPE_ROWS,)),
            pltpu.SemaphoreType.DMA((slots // HALF,)),
            pltpu.SemaphoreType.DMA((2 + rows // OUT_ROWS,)),
        ],
        vmem=60,
        cost=(2 * slots * page_len * rows * (2 * latent + 2 * rope_dim), 4 * MIB),
    )
    blocks = call(
        functools.partial(merge_kernel, partners),
        [shape((chips, 2 * tokens * per_device, latent), BF16)],
        (*got_lat, *got_rope, *local),
        scratch=[pltpu.VMEM((rows // LANES, partners * moves * page_len, LANES), F32)],
        cost=(2 * moves * page_len * rows * 2 * latent, MIB),
    )[0]

    away_uv, away_out, blocks = lax.optimization_barrier((w_uv, w_out, blocks))
    other_uv, other_out = swap(away_uv, 1), swap(away_out, 1)
    blocks = deal(blocks, CHIP)

    parts = call(
        functools.partial(project_kernel, tokens),
        [shape((chips, tokens, width), BF16)],
        (blocks, w_uv, other_uv, w_out, other_out),
        cost=(4 * chips * tokens * width * w_out.shape[0], 8 * MIB),
    )[0]
    parts = deal(parts, CHIP)
    far_count = total_devices // 8
    masks = [2 * side_bit * k for k in range(far_count)]
    direct = far_count <= 4
    attn_out, own_rows = call(
        norm_kernel,
        [
            shape((tokens, width), BF16),
            shape((1 if direct else far_count, tokens, width + LANES), BF16),
        ],
        (parts, residual, norm_gain, routes),
    )

    def load(passed, sources, vmem, held=()):
        outs = [shape(x.shape, BF16) for x in (*passed, *held)]
        passes = len(passed)
        return pl.pallas_call(
            functools.partial(load_kernel, len(sources), len(held), passes),
            out_shape=outs + [shape(w.shape[1:], BF16) for w in sources],
            in_specs=[VMEM] * passes + [ANY] * len(held) + [HBM] * len(sources),
            out_specs=[VMEM] * passes + [ANY] * len(held) + [VMEM] * len(sources),
            input_output_aliases={passes + i: passes + i for i in range(len(held))},
            scratch_shapes=[pltpu.SemaphoreType.DMA((len(sources), 8))],
            compiler_params=pltpu.CompilerParams(vmem_limit_bytes=vmem * MIB),
            cost_estimate=pl.CostEstimate(
                flops=0, bytes_accessed=2 * sum(w.size for w in sources), transcendentals=0
            ),
        )(*passed, *held, *sources)

    if direct:
        others = [swap(own_rows, mask) for mask in masks[1:]]
        own_rows, down_here = load((own_rows,), (w_down,), LOAD_MIB)
        piece = call(
            stack_kernel,
            [shape((far_count, tokens, width + LANES), BF16)],
            (own_rows, *others),
        )[0]
    else:
        own_rows, down_here = load((own_rows,), (w_down,), LOAD_MIB)
        piece = deal(own_rows, FAR)
    side_piece = swap(piece, top_bit, side_bit)
    piece, down_here, up_here = load((piece,), (w_up,), UP_MIB, (down_here,))
    pieces = [piece, side_piece, swap(piece, side_bit, top_bit), swap(side_piece, side_bit, top_bit)]
    pieces[0], pieces[1], down_here, up_here, gate_here = load(
        (piece, side_piece), (w_gate,), SIDE_MIB, (down_here, up_here)
    )
    pieces = pieces + [swap(p, 1) for p in pieces]

    all_rows = total_devices * tokens
    hidden_units = w_gate.shape[2]
    half = all_rows // 2
    kept, away = call(
        functools.partial(expert_kernel, routes.shape[1], len(pieces)),
        [shape((half, width), F32), shape((half, width), BF16)],
        (*pieces, w_router.T, gate_here, up_here, down_here),
        scratch=[
            pltpu.VMEM((all_rows, width), BF16),
            pltpu.VMEM((all_rows, hidden_units), BF16),
        ],
        vmem=EXPERT_MIB if all_rows <= 256 else 56,
        cost=(6 * all_rows * width * hidden_units, 6 * width * hidden_units),
    )

    got = swap(away, 1)
    kept, away = call(
        halve_kernel,
        [shape((half // 2, width), F32), shape((half // 2, width), BF16)],
        (kept, got),
    )
    got = swap(away, side_bit, top_bit)
    kept, away = call(
        halve_kernel,
        [shape((half // 4, width), F32), shape((half // 4, width), BF16)],
        (kept, got),
    )
    got = swap(away, top_bit, side_bit)
    moe_shape = [shape((tokens, width), BF16)]
    if direct:
        parts = call(
            parts_kernel, [shape((tokens, width), F32)] + moe_shape * (far_count - 1), (kept, got)
        )
        got = [swap(part, mask) for part, mask in zip(parts[1:], masks[1:])]
        moe_out = call(add_kernel, moe_shape, (parts[0], *got))[0]
    else:
        parts = call(split_kernel, [shape((far_count, tokens, width), BF16)], (kept, got))[0]
        moe_out = call(sum_kernel, moe_shape, (deal(parts, FAR),))[0]
    return (attn_out, moe_out)


def solution(mesh):
    dp_count, expert_count = mesh.shape["dp"], mesh.shape["expert"]
    finer = Mesh(mesh.devices.reshape(2, dp_count // 2, expert_count // 4, 2, 2), ROWS)
    return jax.shard_map(
        functools.partial(body, dp_count, expert_count),
        mesh=finer,
        in_specs=(
            P(ROWS, None, None),
            P(ROWS, None),
            P(ROWS),
            P(ROWS, None, None),
            P(ROWS, None),
            P(ROWS),
            P(ROWS, None, None, None),
            P(ROWS, None, None, None),
            P(ROWS, None, None),
            P(ROWS, None, None),
            P(EXPERT, None, None),
            P(EXPERT, None),
            P(ROWS, None),
            P(),
            P(),
            P(ROWS, None),
            P(EXPERT, None, DP),
            P(EXPERT, None, DP),
            P(EXPERT, DP, None),
        ),
        out_specs=(P(ROWS, None), P(ROWS, None)),
        check_vma=False,
    )
```

```python
import functools

import jax
import jax.numpy as jnp
from jax import lax
from jax.experimental import pallas as pl
from jax.experimental.pallas import tpu as pltpu
from jax.sharding import Mesh, PartitionSpec as P

SCORE_SCALE = 0.07216878364870322
ROUTE_SCALE = 2.5
NORM_EPS = 1e-06
LOW = -1e30
LANES = 128
MIB = 1 << 20
BF16 = jnp.bfloat16
F32 = jnp.float32
VMEM = pl.BlockSpec(memory_space=pltpu.VMEM)
SMEM = pl.BlockSpec(memory_space=pltpu.SMEM)
ANY = pl.BlockSpec(memory_space=pl.ANY)
HBM = pl.BlockSpec(memory_space=pltpu.HBM)
DP = ("top", "low")
EXPERT = ("far", "side", "core")
ROWS = DP + EXPERT
FAR = ("low", "far")
CHIP = ("far", "side")
ROPE_ROWS = 16
LOAD_MIB = 41
UP_MIB = 34
SIDE_MIB = 28
EXPERT_MIB = 16


def dot_nt(a, b):
    return lax.dot_general(a, b, (((1,), (1,)), ((), ())), preferred_element_type=F32)


def dot_tn(a, b):
    return lax.dot_general(a, b, (((0,), (0,)), ((), ())), preferred_element_type=F32)


def dot_nn(a, b):
    return jnp.dot(a, b, preferred_element_type=F32)


def call(kernel, outs, operands, in_specs=None, out_specs=None, scratch=(), vmem=16, cost=None):
    flops, moved = cost or (0, 0)
    return pl.pallas_call(
        kernel,
        out_shape=outs,
        in_specs=in_specs or [VMEM] * len(operands),
        out_specs=out_specs or [VMEM] * len(outs),
        scratch_shapes=list(scratch),
        compiler_params=pltpu.CompilerParams(vmem_limit_bytes=vmem * MIB),
        cost_estimate=pl.CostEstimate(flops=flops, bytes_accessed=moved, transcendentals=0),
    )(*operands)


def shape(dims, dtype):
    return jax.ShapeDtypeStruct(dims, dtype)


def iota(dims, axis):
    return lax.broadcasted_iota(jnp.int32, dims, axis)


def fetch(copies):
    for copy in copies:
        copy.start()
    return copies


def row_copies(source, target, sems, first):
    return [
        pltpu.make_async_copy(
            source.at[pl.ds(at, ROPE_ROWS)], target.at[pl.ds(at, ROPE_ROWS)], sems.at[first + i]
        )
        for i, at in enumerate(range(0, source.shape[0], ROPE_ROWS))
    ]


def pick_kernel(partners, moves, move_hbm, scale_hbm, lat, rope_hbm, *rest):
    lat_outs, rope_outs = rest[:partners], rest[partners : 2 * partners]
    scale_out, move, rope, scale_ref, wide_scale, lat_sems, sems = rest[2 * partners :]
    slots, width = rope.shape
    half = width // 2
    me = lax.axis_index(DP)
    get_move, get_scale, *get_rope = fetch(
        [
            pltpu.make_async_copy(move_hbm, move, sems.at[0]),
            pltpu.make_async_copy(scale_hbm, scale_ref, sems.at[1]),
        ]
        + row_copies(rope_hbm, rope, sems, 3)
    )
    get_move.wait()
    copies = []
    for k in range(partners):
        for m in range(moves):
            copies.append(
                pltpu.make_async_copy(
                    lat.at[move[0, me ^ (k + 1), m]], lat_outs[k].at[m], lat_sems.at[k, m]
                )
            )
    fetch(copies)
    get_scale.wait()
    wide_scale[...] = scale_ref[...].astype(F32)
    (put_scale,) = fetch([pltpu.make_async_copy(wide_scale, scale_out, sems.at[2])])
    put_scale.wait()
    for copy in get_rope:
        copy.wait()
    row = iota((2 * moves, 1), 0)
    column = iota((2 * moves, slots), 1)
    for k in range(partners):
        target = jnp.zeros((2 * moves, 1), jnp.int32)
        factor = jnp.zeros((2 * moves, 1), F32)
        for m in range(moves):
            page = move[0, me ^ (k + 1), m]
            target = jnp.where(row // 2 == m, page, target)
            factor = jnp.where(row // 2 == m, scale_out[page], factor)
        hit = column == target
        even = row % 2 == 0
        first = jnp.where(hit & even, 1.0, 0.0).astype(BF16)
        second = jnp.where(hit & (~even), 1.0, 0.0).astype(BF16)
        both = dot_nn(first, rope[:, :half]) + dot_nn(second, rope[:, half:])
        rope_outs[k][:, :half] = both.astype(BF16)
        rope_outs[k][:, half:] = jnp.broadcast_to(factor, (2 * moves, LANES)).astype(BF16)
    for copy in copies:
        copy.wait()


def spread(scores, start, count, stride, part):
    for b in range(scores.shape[0]):
        scores.at[b][pl.ds(start, count, stride=stride), :] = part[:, b * LANES : (b + 1) * LANES]


def read(scores, span):
    parts = [scores[b, span, :] for b in range(scores.shape[0])]
    return parts[0] if len(parts) == 1 else jnp.concatenate(parts, axis=1)


def write(scores, span, part):
    for b in range(scores.shape[0]):
        scores[b, span, :] = part[:, b * LANES : (b + 1) * LANES]


GROUP = 8
HALF = 4
OUT_ROWS = 32


def local_kernel(
    sizes,
    partners,
    scale_hbm,
    table_hbm,
    lengths_hbm,
    move_hbm,
    lat_hbm,
    rope_hbm,
    q_hbm,
    turn_hbm,
    new_lat_hbm,
    new_rope_hbm,
    out_hbm,
    out,
    scale,
    qrel_out,
    q2_out,
    table,
    lengths,
    move,
    lat,
    rope,
    q_lat,
    q_rope,
    new_lat,
    new_rope,
    scores,
    limits,
    new_keys,
    new_turns,
    sems,
    lat_sems,
    out_sems,
):
    heads, per_device, rollouts, following, view = sizes
    slots, page_len, latent = lat.shape
    rows = rollouts * following * heads
    rope_dim = q_rope.shape[3]
    moves = move.shape[2]
    me = lax.axis_index(DP)
    pairs = (
        (table_hbm, table),
        (lengths_hbm, lengths),
        (move_hbm, move),
        (scale_hbm, scale),
        (turn_hbm, q_rope),
        (q_hbm, q_lat),
        (new_lat_hbm, new_lat),
        (new_rope_hbm, new_rope),
    )
    small = fetch(
        [pltpu.make_async_copy(src, dst, sems.at[i]) for i, (src, dst) in enumerate(pairs)]
        + row_copies(rope_hbm, rope, sems, len(pairs))
    )
    chunks = fetch(
        [
            pltpu.make_async_copy(
                lat_hbm.at[pl.ds(at, HALF)], lat.at[pl.ds(at, HALF)], lat_sems.at[at // HALF]
            )
            for at in range(0, slots, HALF)
        ]
    )
    place = iota((rows, rows), 0)
    rollout = (place // following) % rollouts
    token = place % following
    head = place // (following * rollouts)
    source = (rollout * following + token) * heads + head
    order = jnp.where(iota((rows, rows), 1) == source, 1.0, 0.0).astype(BF16)
    at = iota((rope_dim, 2 * rope_dim), 1)
    frm = iota((rope_dim, 2 * rope_dim), 0)
    for copy in small:
        copy.wait()
    for slot in range(rollouts * view):
        limits[slot] = 0
    for r in range(rollouts):
        for a in range(table.shape[1]):
            live = jnp.clip(lengths[r] - a * page_len, 0, page_len)
            limits[r * view + table[r, a]] = live
    q_turn = dot_nn(order, q_rope[...].reshape(rows, rope_dim)).astype(BF16)
    q2_out[:rows, :] = dot_nn(q_turn, jnp.where(at == frm, 1.0, 0.0).astype(BF16)).astype(BF16)
    q2_out[rows:, :] = dot_nn(
        q_turn, jnp.where(at == frm + rope_dim, 1.0, 0.0).astype(BF16)
    ).astype(BF16)
    qrel_out[...] = dot_nn(order, q_lat[...].reshape(rows, latent)).astype(BF16)
    twos = page_len // 2
    wide = 2 * rope_dim
    stacked = jnp.concatenate([rope[:, c * wide : (c + 1) * wide] for c in range(twos)], axis=0)
    turned = dot_nt(stacked, q2_out[...])
    for c in range(twos):
        part = turned[c * slots : (c + 1) * slots]
        spread(scores, 2 * c, slots, page_len, part[:, :rows])
        spread(scores, 2 * c + 1, slots, page_len, part[:, rows:])

    lane_rollout = (iota((1, rows), 1) // following) % rollouts
    lane_token = iota((1, rows), 1) % following
    position = iota((page_len, rows), 0)

    def limit_row(slot):
        row = jnp.full(lane_rollout.shape, limits[slot], jnp.int32)
        for r in range(1, rollouts):
            row = jnp.where(lane_rollout == r, limits[r * view + slot], row)
        return row

    for k in range(partners):
        for m in range(moves):
            at = 2 * rows + 2 + k * moves + m
            limit = limit_row(slots + (me ^ (k + 1)) * moves + m)
            out[at : at + 1, :rows] = limit.astype(F32)
    queries = qrel_out[...]
    out[rows : 2 * rows, :latent] = queries.astype(F32)
    out[: 2 * rows, latent:] = q2_out[...].astype(F32)

    def send(first, count, sem):
        return fetch(
            [pltpu.make_async_copy(out.at[pl.ds(first, count)], out_hbm.at[pl.ds(first, count)], sem)]
        )[0]

    sent = [send(rows, rows, out_sems.at[0])]
    fresh_rows = rollouts * following
    new_keys[...] = jnp.zeros(new_keys.shape, F32)
    new_turns[...] = jnp.zeros(new_turns.shape, F32)
    for r in range(rollouts):
        span = slice(r * following, (r + 1) * following)
        new_keys[span, :] = new_lat[r].astype(F32)
        new_turns[span, :rope_dim] = new_rope[r].astype(F32)
    fresh_keys = new_keys[...].astype(BF16)
    new_part = dot_nt(fresh_keys, queries) + dot_nt(
        new_turns[...].astype(BF16), q2_out[:rows, :]
    )
    new_row = iota(new_part.shape, 0)
    seen = (new_row // following == lane_rollout) & (new_row % following <= lane_token)
    new_part = jnp.where(seen & (new_row < fresh_rows), new_part * SCORE_SCALE, LOW)

    best = jnp.full((page_len, rows), LOW, F32)
    for first in range(0, slots, GROUP):
        for copy in chunks[first // HALF : (first + GROUP) // HALF]:
            copy.wait()
        keys = lat[first : first + GROUP].reshape(GROUP * page_len, latent)
        fresh = dot_nt(keys, queries)
        for g in range(GROUP):
            page = first + g
            span = pl.ds(page * page_len, page_len)
            part = fresh[g * page_len : (g + 1) * page_len] + read(scores, span)
            part = part * (scale[page] * SCORE_SCALE)
            write(scores, span, part)
            best = jnp.maximum(best, jnp.where(position < limit_row(page), part, LOW))
    for m in range(moves):
        page = move[0, me, m]
        part = read(scores, pl.ds(pl.multiple_of(page * page_len, page_len), page_len))
        live = position < limit_row(slots + me * moves + m)
        best = jnp.maximum(best, jnp.where(live, part, LOW))
    peak = jnp.max(best, axis=0, keepdims=True)
    peak = jnp.maximum(peak, jnp.max(new_part, axis=0, keepdims=True))

    def weigh(part, slot, factor, total):
        grown = jnp.where(position < limit_row(slot), jnp.exp(part - peak), 0.0)
        return (grown * factor).astype(BF16), total + grown

    new_exp = jnp.exp(new_part - peak)
    total = jnp.zeros((page_len, rows), F32)
    acc = dot_tn(new_exp.astype(BF16), fresh_keys)
    for first in range(0, slots, GROUP):
        weights = []
        for g in range(GROUP):
            page = first + g
            part = read(scores, pl.ds(page * page_len, page_len))
            weight, total = weigh(part, page, scale[page], total)
            weights.append(weight)
        keys = lat[first : first + GROUP].reshape(GROUP * page_len, latent)
        acc = acc + dot_tn(jnp.concatenate(weights, axis=0), keys)
    weights, keys = [], []
    for m in range(moves):
        page = move[0, me, m]
        part = read(scores, pl.ds(pl.multiple_of(page * page_len, page_len), page_len))
        weight, total = weigh(part, slots + me * moves + m, scale[page], total)
        weights.append(weight)
        keys.append(lat[page])
    acc = acc + dot_tn(jnp.concatenate(weights, axis=0), jnp.concatenate(keys, axis=0))
    whole = jnp.sum(total, axis=0, keepdims=True) + jnp.sum(new_exp, axis=0, keepdims=True)
    out[:rows, :latent] = acc
    out[2 * rows : 2 * rows + 1, :rows] = peak
    out[2 * rows + 1 : 2 * rows + 2, :rows] = whole
    sent.append(send(2 * rows, out.shape[0] - 2 * rows, out_sems.at[1]))
    for i in range(rows // OUT_ROWS):
        sent.append(send(i * OUT_ROWS, OUT_ROWS, out_sems.at[2 + i]))
    for copy in sent:
        copy.wait()


def merge_kernel(partners, *refs):
    got_lat, got_rope = refs[:partners], refs[partners : 2 * partners]
    local, out, scores = refs[2 * partners :]
    moves, page_len, latent = got_lat[0].shape
    rows = out.shape[0] * out.shape[1]
    qrel = local[rows : 2 * rows, :latent].astype(BF16)
    q2 = local[: 2 * rows, latent:].astype(BF16)
    wide = q2.shape[1]
    position = iota((page_len, rows), 0).astype(F32)
    best = jnp.full((page_len, rows), LOW, F32)
    half_lanes = got_rope[0].shape[1] - LANES
    pieces = half_lanes // wide
    span = moves * page_len
    factors = []
    for k in range(partners):
        turns = got_rope[k]
        stacked = jnp.concatenate(
            [turns[:, c * wide : (c + 1) * wide].astype(F32) for c in range(pieces)], axis=0
        ).astype(BF16)
        turned = dot_nt(stacked, q2)
        base = k * span
        for c in range(pieces):
            part = turned[c * 2 * moves : (c + 1) * 2 * moves]
            spread(scores, base + 2 * c, 2 * moves, page_len // 2, part[:, :rows])
            spread(scores, base + 2 * c + 1, 2 * moves, page_len // 2, part[:, rows:])
        fresh = dot_nt(got_lat[k][...].reshape(span, latent), qrel)
        marks = turns[:, half_lanes:].astype(F32)
        for m in range(moves):
            factor = marks[2 * m : 2 * m + 1, :1]
            factors.append(factor)
            where_at = pl.ds(base + m * page_len, page_len)
            part = fresh[m * page_len : (m + 1) * page_len] + read(scores, where_at)
            part = part * (factor * SCORE_SCALE)
            at = 2 * rows + 2 + k * moves + m
            part = jnp.where(position < local[at : at + 1, :rows], part, LOW)
            write(scores, where_at, part)
            best = jnp.maximum(best, part)
    peak_local = local[2 * rows : 2 * rows + 1, :rows]
    peak = jnp.maximum(jnp.max(best, axis=0, keepdims=True), peak_local)
    shrink = jnp.exp(peak_local - peak)
    acc = jnp.zeros((rows, latent), F32)
    grown_sum = jnp.zeros((page_len, rows), F32)
    for k in range(partners):
        weights = []
        for m in range(moves):
            part = read(scores, pl.ds(k * span + m * page_len, page_len))
            grown = jnp.exp(part - peak)
            grown_sum = grown_sum + grown
            weights.append((grown * factors[k * moves + m]).astype(BF16))
        acc = acc + dot_tn(
            jnp.concatenate(weights, axis=0), got_lat[k][...].reshape(span, latent)
        )
    total = local[2 * rows + 1 : 2 * rows + 2, :rows] * shrink + jnp.sum(grown_sum, axis=0, keepdims=True)

    def upright(row):
        return jnp.transpose(jnp.broadcast_to(row, (LANES, rows)))[:, :1]

    result = (local[:rows, :latent] * upright(shrink) + acc) / upright(total)
    out[...] = result.reshape(out.shape).astype(BF16)


def project_kernel(tokens, blocks, w_uv, other_uv, w_out, other_out, out):
    chips = blocks.shape[0]
    per_device = w_uv.shape[0]
    core = lax.axis_index("core")
    stacked = blocks[...].astype(F32).reshape(-1, blocks.shape[2]).astype(BF16)
    rows = stacked.shape[0]
    row_head = (iota((rows, 1), 0) // tokens) % (2 * per_device)
    values = []
    for first, uv in ((core * per_device, w_uv), ((1 - core) * per_device, other_uv)):
        for head in range(per_device):
            part = dot_nn(stacked, uv[head])
            values.append(jnp.where(row_head == first + head, part, 0.0).astype(BF16))
    values = jnp.concatenate(values, axis=1)
    out_row = iota((chips * tokens, rows), 0)
    in_row = iota((chips * tokens, rows), 1)
    same_chip = in_row // (tokens * 2 * per_device) == out_row // tokens
    same = same_chip & (in_row % tokens == out_row % tokens)
    joined = dot_nn(jnp.where(same, 1.0, 0.0).astype(BF16), values).astype(BF16)
    depth, width = w_out.shape
    step = 512 if width % 512 == 0 else width
    for at in range(0, width, step):
        part = dot_nn(joined[:, :depth], w_out[:, at : at + step])
        part = part + dot_nn(joined[:, depth:], other_out[:, at : at + step])
        out[:, :, at : at + step] = part.reshape(chips, tokens, step).astype(BF16)


def split_kernel(kept, got, out):
    total = kept[...] + got[...].astype(F32)
    out[...] = total.reshape(out.shape).astype(BF16)


def norm_kernel(got, residual, gain, routes, attn_out, out):
    total = jnp.sum(got[...].astype(F32), axis=0)
    attn_out[...] = total.astype(BF16)
    hidden = (residual[...].astype(F32) + total).astype(BF16).astype(F32)
    width = hidden.shape[1]
    power = jnp.sum(hidden * hidden, axis=1, keepdims=True) / width
    normed = (hidden * lax.rsqrt(power + NORM_EPS) * gain[...].reshape(1, width)).astype(BF16)
    named = routes[...].astype(F32).astype(BF16)
    for copy in range(out.shape[0]):
        out[copy, :, :width] = normed
        out[copy, :, width:] = jnp.zeros((hidden.shape[0], LANES), BF16)
        out[copy, :, width : width + routes.shape[1]] = named


def stack_kernel(*refs):
    for k, ref in enumerate(refs[:-1]):
        refs[-1][k] = ref[0]


def parts_kernel(kept, got, *outs):
    total = kept[...] + got[...].astype(F32)
    rows = outs[0].shape[0]
    for k, out in enumerate(outs):
        out[...] = total[k * rows : (k + 1) * rows].astype(out.dtype)


def add_kernel(*refs):
    total = refs[0][...]
    for ref in refs[1:-1]:
        total = total + ref[...].astype(F32)
    refs[-1][...] = total.astype(BF16)


def load_kernel(count, held, passes, *refs):
    first_out = passes + held + count
    passed, sources = refs[:passes], refs[passes + held : first_out]
    passed_outs = refs[first_out : first_out + passes]
    outs, sems = refs[first_out + passes + held : -1], refs[-1]
    split = sems.shape[1]
    copies = []
    for k, (source, out) in enumerate(zip(sources, outs)):
        step = out.shape[0] // split
        for i in range(split):
            span = pl.ds(i * step, step)
            copies.append(
                pltpu.make_async_copy(source.at[0, span], out.at[span], sems.at[k, i])
            )
    fetch(copies)
    for source, out in zip(passed, passed_outs):
        out[...] = source[...]
    for copy in copies:
        copy.wait()


def expert_kernel(top, count, *refs):
    pieces = refs[:count]
    w_router, w_gate, w_up, w_down = refs[count : count + 4]
    kept, away, rows_ref, hidden_ref = refs[count + 4 :]
    expert = lax.axis_index(EXPERT)
    width, units = w_gate.shape
    in_step = 256 if units % 256 == 0 else units
    out_step = 512 if width % 512 == 0 else width
    piece_rows = rows_ref.shape[0] // count
    named = []
    for k, piece in enumerate(pieces):
        whole = piece[...].astype(F32).reshape(piece_rows, -1)
        rows_ref[k * piece_rows : (k + 1) * piece_rows, :] = whole[:, :width].astype(BF16)
        named.append(whole[:, width:])
    named = jnp.concatenate(named, axis=0)
    rows = rows_ref[...]
    logits = dot_nt(rows, w_router[...])
    experts = iota(logits.shape, 1)
    chosen = jnp.zeros(logits.shape, F32)
    for k in range(top):
        route = named[:, k : k + 1].astype(jnp.int32)
        chosen = chosen + jnp.where(route == experts, 1.0, 0.0)
    sig = jax.nn.sigmoid(logits) * chosen
    mine = jnp.sum(jnp.where(experts == expert, sig, 0.0), axis=1, keepdims=True)
    gates = ROUTE_SCALE * mine / jnp.sum(sig, axis=1, keepdims=True)
    for at in range(0, units, in_step):
        gate = dot_nn(rows, w_gate[:, at : at + in_step])
        up = dot_nn(rows, w_up[:, at : at + in_step])
        hidden_ref[:, at : at + in_step] = (gate / (1.0 + jnp.exp(-gate)) * up).astype(BF16)
    half = rows_ref.shape[0] // 2
    hidden = hidden_ref[...]
    for at in range(0, width, out_step):
        part = dot_nn(hidden, w_down[:, at : at + out_step]) * gates
        kept[:, at : at + out_step] = part[:half]
        away[:, at : at + out_step] = part[half:].astype(BF16)


def halve_kernel(kept, got, keep, away):
    total = kept[...] + got[...].astype(F32)
    half = total.shape[0] // 2
    keep[...] = total[:half]
    away[...] = total[half:].astype(BF16)


def sum_kernel(got, out):
    out[...] = jnp.sum(got[...].astype(F32), axis=0).astype(BF16)


def body(dp_count, expert_count, *arrays):
    (
        cache_lat,
        cache_rope,
        page_scale,
        move_list,
        page_table,
        lengths,
        q_lat,
        q_rope,
        new_lat,
        new_rope,
        w_uv,
        w_out,
        residual,
        norm_gain,
        w_router,
        routes,
        w_gate,
        w_up,
        w_down,
    ) = arrays
    total_devices = dp_count * expert_count
    top_bit = total_devices // 2
    side_bit = 2

    def swap(x, mask, mask_odd=None):
        pairs = []
        for i in range(total_devices):
            other = mask if mask_odd is None or i % 2 == 0 else mask_odd
            pairs.append((i, i ^ other))
        return lax.ppermute(x, ROWS, pairs)

    def deal(x, names):
        return lax.all_to_all(x, names, split_axis=0, concat_axis=0, tiled=True)

    slots, page_len, latent = cache_lat.shape
    moves = move_list.shape[2]
    rollouts, following, heads, rope_dim = q_rope.shape
    view = slots + dp_count * moves
    per_device = heads // expert_count
    tokens = rollouts * following
    width = residual.shape[1]
    partners = dp_count - 1
    rows = tokens * heads
    sizes = (heads, per_device, rollouts, following, view)
    chips = expert_count // 2
    picked = call(
        functools.partial(pick_kernel, partners, moves),
        [shape((moves, page_len, latent), BF16)] * partners
        + [shape((2 * moves, cache_rope.shape[1] // 2 + LANES), BF16)] * partners
        + [shape((slots,), F32)],
        (move_list, page_scale, cache_lat, cache_rope),
        in_specs=[HBM] * 4,
        out_specs=[VMEM] * (2 * partners) + [SMEM],
        scratch=[
            pltpu.SMEM(move_list.shape, jnp.int32),
            pltpu.VMEM(cache_rope.shape, BF16),
            pltpu.VMEM(page_scale.shape, BF16),
            pltpu.VMEM((slots,), F32),
            pltpu.SemaphoreType.DMA((partners, moves)),
            pltpu.SemaphoreType.DMA((3 + slots // ROPE_ROWS,)),
        ],
        vmem=60,
    )
    got_lat = [swap(picked[k], (k + 1) * expert_count) for k in range(partners)]
    got_rope = [swap(picked[partners + k], (k + 1) * expert_count) for k in range(partners)]

    extra = -(-(2 + partners * moves) // 8) * 8
    local = call(
        functools.partial(local_kernel, sizes, partners),
        [shape((2 * rows + extra, latent + 2 * rope_dim), F32)],
        (
            picked[-1],
            page_table,
            lengths,
            move_list,
            cache_lat,
            cache_rope,
            q_lat,
            q_rope,
            new_lat,
            new_rope,
        ),
        in_specs=[HBM] * 10,
        out_specs=[HBM],
        scratch=[
            pltpu.VMEM((2 * rows + extra, latent + 2 * rope_dim), F32),
            pltpu.SMEM((slots,), F32),
            pltpu.VMEM((rows, latent), BF16),
            pltpu.VMEM((2 * rows, 2 * rope_dim), BF16),
            pltpu.SMEM(page_table.shape, jnp.int32),
            pltpu.SMEM(lengths.shape, jnp.int32),
            pltpu.SMEM(move_list.shape, jnp.int32),
            pltpu.VMEM(cache_lat.shape, BF16),
            pltpu.VMEM(cache_rope.shape, BF16),
            pltpu.VMEM(q_lat.shape, BF16),
            pltpu.VMEM(q_rope.shape, BF16),
            pltpu.VMEM(new_lat.shape, BF16),
            pltpu.VMEM(new_rope.shape, BF16),
            pltpu.VMEM((rows // LANES, (slots + 1) * page_len, LANES), F32),
            pltpu.SMEM((rollouts * view,), jnp.int32),
            pltpu.VMEM((16, latent), F32),
            pltpu.VMEM((16, 2 * rope_dim), F32),
            pltpu.SemaphoreType.DMA((8 + slots // ROPE_ROWS,)),
            pltpu.SemaphoreType.DMA((slots // HALF,)),
            pltpu.SemaphoreType.DMA((2 + rows // OUT_ROWS,)),
        ],
        vmem=60,
        cost=(2 * slots * page_len * rows * (2 * latent + 2 * rope_dim), 4 * MIB),
    )
    blocks = call(
        functools.partial(merge_kernel, partners),
        [shape((chips, 2 * tokens * per_device, latent), BF16)],
        (*got_lat, *got_rope, *local),
        scratch=[pltpu.VMEM((rows // LANES, (partners * moves + 1) * page_len, LANES), F32)],
        cost=(2 * moves * page_len * rows * 2 * latent, MIB),
    )[0]

    away_uv, away_out, blocks = lax.optimization_barrier((w_uv, w_out, blocks))
    other_uv, other_out = swap(away_uv, 1), swap(away_out, 1)
    blocks = deal(blocks, CHIP)

    parts = call(
        functools.partial(project_kernel, tokens),
        [shape((chips, tokens, width), BF16)],
        (blocks, w_uv, other_uv, w_out, other_out),
        cost=(4 * chips * tokens * width * w_out.shape[0], 8 * MIB),
    )[0]
    parts = deal(parts, CHIP)
    far_count = total_devices // 8
    masks = [2 * side_bit * k for k in range(far_count)]
    direct = far_count <= 4
    attn_out, own_rows = call(
        norm_kernel,
        [
            shape((tokens, width), BF16),
            shape((1 if direct else far_count, tokens, width + LANES), BF16),
        ],
        (parts, residual, norm_gain, routes),
    )

    def load(passed, sources, vmem, held=()):
        outs = [shape(x.shape, BF16) for x in (*passed, *held)]
        passes = len(passed)
        return pl.pallas_call(
            functools.partial(load_kernel, len(sources), len(held), passes),
            out_shape=outs + [shape(w.shape[1:], BF16) for w in sources],
            in_specs=[VMEM] * passes + [ANY] * len(held) + [HBM] * len(sources),
            out_specs=[VMEM] * passes + [ANY] * len(held) + [VMEM] * len(sources),
            input_output_aliases={passes + i: passes + i for i in range(len(held))},
            scratch_shapes=[pltpu.SemaphoreType.DMA((len(sources), 8))],
            compiler_params=pltpu.CompilerParams(vmem_limit_bytes=vmem * MIB),
            cost_estimate=pl.CostEstimate(
                flops=0, bytes_accessed=2 * sum(w.size for w in sources), transcendentals=0
            ),
        )(*passed, *held, *sources)

    if direct:
        others = [swap(own_rows, mask) for mask in masks[1:]]
        own_rows, down_here = load((own_rows,), (w_down,), LOAD_MIB)
        piece = call(
            stack_kernel,
            [shape((far_count, tokens, width + LANES), BF16)],
            (own_rows, *others),
        )[0]
    else:
        own_rows, down_here = load((own_rows,), (w_down,), LOAD_MIB)
        piece = deal(own_rows, FAR)
    side_piece = swap(piece, top_bit, side_bit)
    piece, down_here, up_here = load((piece,), (w_up,), UP_MIB, (down_here,))
    pieces = [piece, side_piece, swap(piece, side_bit, top_bit), swap(side_piece, side_bit, top_bit)]
    pieces[0], pieces[1], down_here, up_here, gate_here = load(
        (piece, side_piece), (w_gate,), SIDE_MIB, (down_here, up_here)
    )
    pieces = pieces + [swap(p, 1) for p in pieces]

    all_rows = total_devices * tokens
    hidden_units = w_gate.shape[2]
    half = all_rows // 2
    kept, away = call(
        functools.partial(expert_kernel, routes.shape[1], len(pieces)),
        [shape((half, width), F32), shape((half, width), BF16)],
        (*pieces, w_router.T, gate_here, up_here, down_here),
        scratch=[
            pltpu.VMEM((all_rows, width), BF16),
            pltpu.VMEM((all_rows, hidden_units), BF16),
        ],
        vmem=EXPERT_MIB if all_rows <= 256 else 56,
        cost=(6 * all_rows * width * hidden_units, 6 * width * hidden_units),
    )

    got = swap(away, 1)
    kept, away = call(
        halve_kernel,
        [shape((half // 2, width), F32), shape((half // 2, width), BF16)],
        (kept, got),
    )
    got = swap(away, side_bit, top_bit)
    kept, away = call(
        halve_kernel,
        [shape((half // 4, width), F32), shape((half // 4, width), BF16)],
        (kept, got),
    )
    got = swap(away, top_bit, side_bit)
    moe_shape = [shape((tokens, width), BF16)]
    if direct:
        parts = call(
            parts_kernel, [shape((tokens, width), F32)] + moe_shape * (far_count - 1), (kept, got)
        )
        got = [swap(part, mask) for part, mask in zip(parts[1:], masks[1:])]
        moe_out = call(add_kernel, moe_shape, (parts[0], *got))[0]
    else:
        parts = call(split_kernel, [shape((far_count, tokens, width), BF16)], (kept, got))[0]
        moe_out = call(sum_kernel, moe_shape, (deal(parts, FAR),))[0]
    return (attn_out, moe_out)


def solution(mesh):
    dp_count, expert_count = mesh.shape["dp"], mesh.shape["expert"]
    finer = Mesh(mesh.devices.reshape(2, dp_count // 2, expert_count // 4, 2, 2), ROWS)
    return jax.shard_map(
        functools.partial(body, dp_count, expert_count),
        mesh=finer,
        in_specs=(
            P(ROWS, None, None),
            P(ROWS, None),
            P(ROWS),
            P(ROWS, None, None),
            P(ROWS, None),
            P(ROWS),
            P(ROWS, None, None, None),
            P(ROWS, None, None, None),
            P(ROWS, None, None),
            P(ROWS, None, None),
            P(EXPERT, None, None),
            P(EXPERT, None),
            P(ROWS, None),
            P(),
            P(),
            P(ROWS, None),
            P(EXPERT, None, DP),
            P(EXPERT, None, DP),
            P(EXPERT, DP, None),
        ),
        out_specs=(P(ROWS, None), P(ROWS, None)),
        check_vma=False,
    )
```
